32 devices in a mesh: rep: 2 (over y), req: 4 (over z), mp: 4 (over x, core).
Axes of the slice: x: 2, y: 2, z: 4, core: 2. Of those that a mesh axis runs over, the one named last changes fastest.
Arguments:
- hidden_in: bfloat16 [128, 2, 8192], P(('rep', 'req'), None, 'mp'), parts along dimension 0, may hold values from -6 to 6
- frozen_query_rows: bfloat16 [128, 2, 8192], P(('rep', 'req'), None, 'mp'), parts along dimension 0, may hold values from -6 to 86
- new_kv: bfloat16 [128, 2, 2, 1024], P(('rep', 'req'), None, None, 'mp'), parts along dimension 0, may hold values from -6 to 31
- adapter_of: int32 [128], P(('rep', 'req')), parts along dimension 0, may hold values from 0 to 7, as said below
- adapter_home: int32 [16], P('rep'), parts along dimension 0, may hold values from 0 to 7, as said below
- a_store: bfloat16 [16, 64, 8192], P(('rep', 'req'), None, 'mp'), parts along dimension 0, may hold values from -0.0625 to 0.0625
- b_store: bfloat16 [16, 64, 8192], P(('rep', 'req'), None, 'mp'), parts along dimension 0, may hold values from -0.75 to 0.75
- kv_pool: bfloat16 [2, 1024, 16, 1024], P(None, ('rep', 'req'), None, 'mp'), parts along dimension 1, may hold values from -6 to 31
- page_table: int32 [128, 8], P(('rep', 'req')), parts along dimension 0, may hold values from 0 to 127, as said below
- cached_len: int32 [128], P(('rep', 'req')), parts along dimension 0, may hold values from 32 to 128
- new_group: int32 [128], P(('rep', 'req')), parts along dimension 0, may hold values from 0 to 3, as said below
Outputs:
- attended: bfloat16 [128, 2, 8192], P(('rep', 'req'), None, 'mp'), parts along dimension 0
- cache: bfloat16 [2, 128, 128, 1024], P(None, ('rep', 'req'), None, 'mp'), parts along dimension 1
The draws below stay inside these ranges and needn't reach their ends.
There are 2 independent parts, one for each index of `rep`. The reference program is written for one: setup_inputs(seed, part) draws one part's arguments, and reference() takes and returns one part's arrays. A program takes and returns all parts, laid end to end along the dimension named above; each array names one. Nothing has to cross between parts.
Inputs may be any that keep to these rules, and one draw needn't show every extreme that they name: A permutation: adapter a lives in store slot adapter_home[a], which belongs to group adapter_home[a] div 2. `adapter_of`: the requests of one group (new rows h * 16 to h * 16 + 15) use adapters of min(16, number of groups) different owners, at most 4 requests an owner, a number reached in every group; all requests of one group whose adapters have one owner use the same adapter. `page_table`: the rows of one group name each of its 128 pages once. `new_group`: A request keeps its slot (row mod 16); the same 4 slots keep their group in every group; every group receives exactly one request into each slot; no group sends more than 3 requests to one other group, and some pair of groups reaches it.
All inputs are finite; a program needn't handle non-finite values.
Results may differ from the reference program's by a relative error of at most 0.0069.
Values may be sent and summed in bfloat16 or wider, within the bound.
No kernel may reach another device: no remote copies, remote signals or barrier semaphores. Data moves between devices by JAX's collectives and lax.ppermute only.
A program may use at most 64 MiB of HBM per device.

```python
import jax
import jax.numpy as jnp
from jax import lax

D = 8192
HEAD = 128
RANK = 64
STEPS = 2
PAGE = 16
REQ_DEV = 16
CTX = 128
ADAPT_DEV = 2
QW = 8192
KVW = 1024
REQUESTS = 64
ADAPTERS = 8
PAGES_REQ = 8
POOL_DEV = 128
POOL = 512


def shared_home(key):
    return jax.random.permutation(jax.random.fold_in(key, 17), ADAPTERS).astype(jnp.int32)


def draw_adapter_home(key, part):
    return shared_home(key)


def draw_adapter_of(key, part):
    owner_count = ADAPTERS // ADAPT_DEV
    group_count = REQUESTS // REQ_DEV
    home_slots = shared_home(key)
    inverse = jnp.argsort(home_slots, stable=True).astype(jnp.int32)
    order_keys = jax.random.split(jax.random.fold_in(key, 23), group_count)
    owner_order = jax.vmap(lambda subkey: jax.random.permutation(subkey, owner_count))(order_keys)
    slot_keys = jax.random.split(jax.random.fold_in(key, 29), group_count)
    slot_order = jax.vmap(lambda subkey: jax.random.permutation(subkey, REQ_DEV))(slot_keys)
    owners = jnp.take_along_axis(owner_order, slot_order % owner_count, axis=1)
    local_pick = jax.random.randint(jax.random.fold_in(key, 31), (group_count, owner_count), 0, ADAPT_DEV)
    chosen = jnp.take_along_axis(local_pick, owners, axis=1)
    return inverse[(owners * ADAPT_DEV + chosen).reshape(-1)].astype(jnp.int32)


def draw_new_group(key, part):
    group_count = REQUESTS // REQ_DEV
    stay_count = REQ_DEV // 4
    spread = jax.random.permutation(jax.random.fold_in(key, 37), group_count)
    target = jax.random.permutation(jax.random.fold_in(key, 41), group_count)
    slot_rank = jax.random.permutation(jax.random.fold_in(key, 43), REQ_DEV)
    group_ids = jnp.arange(group_count)[:, None]
    moved = target[(spread[group_ids] + slot_rank[None, :]) % group_count]
    return jnp.where(slot_rank[None, :] < stay_count, group_ids, moved).reshape(-1).astype(jnp.int32)


def draw_page_table(key, part):
    group_count = REQUESTS // REQ_DEV
    page_keys = jax.random.split(jax.random.fold_in(key, 47), group_count)
    perms = jax.vmap(lambda subkey: jax.random.permutation(subkey, POOL_DEV))(page_keys)
    return perms.reshape(REQUESTS, PAGES_REQ).astype(jnp.int32)


def draw_cached_len(key, part):
    lengths = jax.random.randint(jax.random.fold_in(key, 53), (REQUESTS,), CTX // 4, CTX + 1)
    return lengths.at[0].set(CTX).at[1].set(CTX // 4).astype(jnp.int32)


def draw_frozen_query_rows(key, part):
    q_shape = (REQUESTS, STEPS, QW)
    return jnp.clip(jax.random.normal(jax.random.fold_in(key, 1), q_shape), -6.0, 6.0).astype(jnp.bfloat16)


def draw_kv_pool(key, part):
    pool_shape = (2, POOL, PAGE, KVW)
    return jnp.clip(jax.random.normal(jax.random.fold_in(key, 4), pool_shape), -6.0, 6.0).astype(jnp.bfloat16)


def draw_new_kv(key, part):
    kv_shape = (REQUESTS, STEPS, 2, KVW)
    return jnp.clip(jax.random.normal(jax.random.fold_in(key, 8), kv_shape), -6.0, 6.0).astype(jnp.bfloat16)


def level_of(key, extent, cuts, least, high):
    loudness = 1.0
    for position, blocks in cuts:
        steps = jax.random.uniform(jax.random.fold_in(jax.random.fold_in(key, 6), position), (blocks,), jnp.float32, least / len(cuts), high / len(cuts))
        loudness = loudness * jnp.repeat(jnp.exp(steps), extent[position] // blocks).reshape((-1,) + (1,) * (len(extent) - 1 - position))
    return loudness


def normal_values(key, shape, scale, bound, shards=(), held_as=jnp.bfloat16):
    factor_of = level_of(key, shape, shards, -0.22, 0.18) if shards else 1.0
    result = jax.random.normal(key, shape, jnp.float32) * scale * factor_of
    return jnp.minimum(jnp.maximum(result, -bound), bound).astype(held_as)


def setup_inputs(seed: int = 0, part: int = 0) -> dict:
    arg_keys = jax.random.split(jax.random.key(seed), 12)
    part_splits = jax.random.split(jax.random.fold_in(arg_keys[11], part), 12)
    return {
        "hidden_in": normal_values(part_splits[0], (REQUESTS, STEPS, D), 1.0, 6.0, ((0, 4), (2, 4))),
        "frozen_query_rows": draw_frozen_query_rows(jax.random.fold_in(jax.random.fold_in(arg_keys[11], part), 71), part),
        "new_kv": draw_new_kv(jax.random.fold_in(jax.random.fold_in(arg_keys[11], part), 71), part),
        "adapter_of": draw_adapter_of(jax.random.fold_in(jax.random.fold_in(arg_keys[11], part), 71), part),
        "adapter_home": draw_adapter_home(jax.random.fold_in(jax.random.fold_in(arg_keys[11], part), 71), part),
        "a_store": normal_values(part_splits[5], (ADAPTERS, RANK, D), D ** -0.5, 0.0625, ((0, 4), (2, 4))),
        "b_store": normal_values(part_splits[6], (ADAPTERS, RANK, QW), RANK ** -0.5, 0.75, ((0, 4), (2, 4))),
        "kv_pool": draw_kv_pool(jax.random.fold_in(jax.random.fold_in(arg_keys[11], part), 71), part),
        "page_table": draw_page_table(jax.random.fold_in(jax.random.fold_in(arg_keys[11], part), 71), part),
        "cached_len": draw_cached_len(jax.random.fold_in(jax.random.fold_in(arg_keys[11], part), 71), part),
        "new_group": draw_new_group(jax.random.fold_in(jax.random.fold_in(arg_keys[11], part), 71), part),
    }


NEG_FILL = -1.0e30


def attend(query_vectors, cached_keys, cached_values, length, fresh_kv):
    row_count, step_count, q_width = query_vectors.shape
    context = cached_keys.shape[1]
    kv_width = cached_keys.shape[2]
    kv_heads = kv_width // HEAD
    per_kv = q_width // kv_width
    score_scale = HEAD ** -0.5
    q_split = query_vectors.reshape(row_count, step_count, kv_heads, per_kv, HEAD)
    k_split = cached_keys.reshape(row_count, context, kv_heads, HEAD)
    v_split = cached_values.reshape(row_count, context, kv_heads, HEAD)
    new_keys = fresh_kv[:, :, 0].reshape(row_count, step_count, kv_heads, HEAD)
    new_values = fresh_kv[:, :, 1].reshape(row_count, step_count, kv_heads, HEAD)
    old_scores = jnp.einsum("bskgd,bjkd->bskgj", q_split, k_split, preferred_element_type=jnp.float32) * score_scale
    visible = jnp.arange(context)[None, :] < length[:, None]
    old_scores = jnp.where(visible[:, None, None, None, :], old_scores, NEG_FILL)
    new_scores = jnp.einsum("bskgd,btkd->bskgt", q_split, new_keys, preferred_element_type=jnp.float32) * score_scale
    causal = jnp.arange(step_count)[None, :] <= jnp.arange(step_count)[:, None]
    new_scores = jnp.where(causal[None, :, None, None, :], new_scores, NEG_FILL)
    scores = jnp.concatenate([old_scores, new_scores], axis=-1)
    row_max = jnp.max(scores, axis=-1, keepdims=True)
    weights = jnp.exp(scores - row_max)
    probabilities = (weights / jnp.sum(weights, axis=-1, keepdims=True)).astype(jnp.bfloat16)
    attention_out = jnp.einsum("bskgj,bjkd->bskgd", probabilities[..., :context], v_split, preferred_element_type=jnp.float32)
    attention_out = attention_out + jnp.einsum("bskgt,btkd->bskgd", probabilities[..., context:], new_values, preferred_element_type=jnp.float32)
    return attention_out.reshape(row_count, step_count, q_width).astype(jnp.bfloat16)


def reference(hidden_in, frozen_query_rows, new_kv, adapter_of, adapter_home, a_store, b_store, kv_pool, page_table, cached_len, new_group):
    old_rows = jnp.arange(REQUESTS, dtype=jnp.int32)
    new_rows = (new_group * REQ_DEV + old_rows % REQ_DEV).astype(jnp.int32)
    source = jnp.zeros((REQUESTS,), jnp.int32).at[new_rows].set(old_rows)

    def per_request(fresh_position_row):
        old_row = source[fresh_position_row]
        store_slot = adapter_home[adapter_of[fresh_position_row]]
        panel_a = a_store[store_slot]
        up_projection_panel = b_store[store_slot]
        complete_rank_product = jnp.dot(hidden_in[fresh_position_row], panel_a.T, preferred_element_type=jnp.float32).astype(jnp.bfloat16)
        adapter_query_delta = jnp.dot(complete_rank_product, up_projection_panel, preferred_element_type=jnp.float32)
        query_vectors = (frozen_query_rows[fresh_position_row].astype(jnp.float32) + adapter_query_delta).astype(jnp.bfloat16)
        page_ids = ((old_row // REQ_DEV) * POOL_DEV + page_table[old_row]).astype(jnp.int32)
        kv_pages = jnp.take(kv_pool, page_ids, axis=1).reshape(2, CTX, KVW)
        attended_row = attend(query_vectors[None], kv_pages[0][None], kv_pages[1][None], cached_len[old_row][None], new_kv[fresh_position_row][None])[0]
        return attended_row, kv_pages

    attended, cache_rows = lax.map(per_request, old_rows)
    cache = jnp.transpose(cache_rows, (1, 0, 2, 3))
    return (attended, cache)
```

```python
import functools

import jax
import jax.numpy as jnp
from jax import lax
from jax.experimental import pallas as pl
from jax.experimental.pallas import tpu as pltpu
from jax.sharding import PartitionSpec as P

HEAD = 128
LANES = 128
TILE = 16
NEG_FILL = -1e30
VMEM_LIMIT = 40 * 1024 * 1024

IN_VMEM = pl.BlockSpec(memory_space=pltpu.VMEM)
IN_SMEM = pl.BlockSpec(memory_space=pltpu.SMEM)
IN_PLACE = pl.BlockSpec(memory_space=pl.ANY)
PARAMS = pltpu.CompilerParams(vmem_limit_bytes=VMEM_LIMIT)


def to_tiles(rows):
    count, steps, width = rows.shape
    split = rows.reshape(count, steps, width // LANES, LANES)
    return split.transpose(0, 2, 1, 3).reshape(count, width // LANES * steps, LANES)


def from_tiles(tiles, steps):
    count, depth, _ = tiles.shape
    split = tiles.reshape(count, depth // steps, steps, LANES)
    return split.transpose(0, 2, 1, 3).reshape(count, steps, depth // steps * LANES)


def stage_rows_kernel(dims, adapter_of, adapter_home, new_group, cached_len, hidden, frozen, *refs):
    groups, own_cap, move_cap, stores = dims
    messages, plan = refs[:groups], refs[groups]
    counts, picks, meta, sems = refs[groups + 1 :]
    count, depth, _ = hidden.shape
    me = lax.axis_index("req")
    for i in range(groups * (own_cap + move_cap)):
        plan[i] = -1
    for j in range(groups):
        counts[j] = 0
        counts[groups + j] = 0
        picks[j] = 0
    for r in range(count):
        store = adapter_home[adapter_of[r]]
        j = jnp.bitwise_xor(store // stores, me)
        k = counts[j]
        plan[j * own_cap + k] = r
        counts[j] = k + 1
        picks[j] = store % stores
        to = jnp.bitwise_xor(new_group[r], me)

        @pl.when(to != 0)
        def _(to=to, r=r):
            at = counts[groups + to]
            plan[groups * own_cap + to * move_cap + at] = r
            counts[groups + to] = at + 1

    lane = lax.broadcasted_iota(jnp.int32, (TILE, LANES), 1)
    for j in range(groups):
        for k in range(own_cap):
            source = jnp.maximum(plan[j * own_cap + k], 0)
            for part, rows in enumerate((hidden, frozen)):
                pltpu.make_async_copy(
                    rows.at[source],
                    messages[j].at[pl.ds((part * own_cap + k) * depth, depth)],
                    sems.at[j],
                ).start()
        told = jnp.where(lane == 0, picks[j], 0)
        for k in range(move_cap):
            slot = plan[(groups * own_cap) + j * move_cap + k]
            length = cached_len[jnp.maximum(slot, 0)]
            told = jnp.where(lane == 1 + k, slot, told)
            told = jnp.where(lane == 1 + move_cap + k, length, told)
        meta[j] = told.astype(jnp.float32).astype(jnp.bfloat16)
        pltpu.make_async_copy(
            meta.at[j], messages[j].at[pl.ds(2 * own_cap * depth, TILE)], sems.at[j]
        ).start()
    for j in range(groups):
        pltpu.make_async_copy(messages[j], messages[j], sems.at[j]).wait()


def stage_pages_kernel(dims, partners, plan, table, pool, *refs):
    groups, own_cap, move_cap, _ = dims
    outs, sems = refs[: len(partners)], refs[len(partners)]
    page = pool.shape[2]
    for i, j in enumerate(partners):
        for k in range(move_cap):
            source = jnp.maximum(plan[groups * own_cap + j * move_cap + k], 0)
            for p in range(table.shape[0]):
                pltpu.make_async_copy(
                    pool.at[:, table[p, source]],
                    outs[i].at[k, :, pl.ds(p * page, page)],
                    sems.at[i],
                ).start()
    for i in range(len(partners)):
        pltpu.make_async_copy(outs[i], outs[i], sems.at[i]).wait()


def rank_kernel(dims, cached_len, a_ref, *refs):
    groups, own_cap, move_cap, _ = dims
    messages = refs[:groups]
    partial, told = refs[groups : groups + 2]
    x, meta, meta_scalar, sem = refs[groups + 2 :]
    width = a_ref.shape[1]
    blocks = width // LANES
    depth = 2 * blocks
    per = own_cap * depth
    number = groups * own_cap
    for j in range(groups):
        x[j * per : (j + 1) * per, :] = messages[j][0:per, :].astype(jnp.float32)
        tile = messages[j][2 * per : 2 * per + TILE, :].astype(jnp.float32)
        meta[j : j + 1, :] = tile[0:1, :].astype(jnp.int32)
    copy = pltpu.make_async_copy(meta, meta_scalar, sem)
    copy.start()
    columns = [
        jnp.concatenate([x[pl.ds(2 * c + s, number, stride=depth), :] for s in range(2)], axis=0)
        for c in range(blocks)
    ]
    rows = jnp.concatenate(columns, axis=1).astype(jnp.bfloat16)
    partial[...] = lax.dot_general(
        rows, a_ref[...], (((1,), (1,)), ((), ())), preferred_element_type=jnp.float32
    )
    copy.wait()
    count = cached_len.shape[0]
    for r in range(count):
        told[groups + r] = 0
        told[groups + count + r] = 0
        told[groups + 2 * count + r] = cached_len[r]
    for j in range(groups):
        told[j] = meta_scalar[j, 0]
        for k in range(move_cap):
            slot = meta_scalar[j, 1 + k]
            told[groups + 3 * count + j * move_cap + k] = slot
            if j == 0:
                continue

            @pl.when(slot >= 0)
            def _(slot=slot, j=j, k=k):
                told[groups + slot] = j
                told[groups + count + slot] = k
                told[groups + 2 * count + slot] = meta_scalar[j, 1 + move_cap + k]


def pair_sum(parts):
    while len(parts) > 1:
        parts = [parts[i] + parts[i + 1] for i in range(0, len(parts), 2)]
    return parts[0]


def query_kernel(dims, n_parts, told, b_ref, *refs):
    groups, own_cap, _, stores = dims
    partials, messages = refs[:n_parts], refs[n_parts : n_parts + groups]
    outs, x = refs[n_parts + groups : n_parts + 2 * groups], refs[n_parts + 2 * groups]
    width = b_ref.shape[1]
    rank = b_ref.shape[0] // stores
    blocks = width // LANES
    depth = 2 * blocks
    per = own_cap * depth
    number = groups * own_cap
    full = pair_sum([p[...] for p in partials]).astype(jnp.bfloat16)
    row = lax.broadcasted_iota(jnp.int32, full.shape, 0)
    group_of = (row % number) // own_cap
    pick = jnp.zeros(full.shape, jnp.int32)
    for j in range(groups):
        pick = jnp.where(group_of == j, told[j], pick)
    chosen = lax.broadcasted_iota(jnp.int32, full.shape, 1) // rank == pick
    full = jnp.where(chosen, full.astype(jnp.float32), 0.0).astype(jnp.bfloat16)
    delta = jnp.dot(full, b_ref[...], preferred_element_type=jnp.float32)
    for c in range(blocks):
        for s in range(2):
            x[pl.ds(2 * c + s, number, stride=depth), :] = delta[
                s * number : (s + 1) * number, c * LANES : (c + 1) * LANES
            ]
    for j in range(groups):
        base = messages[j][per : 2 * per, :].astype(jnp.float32)
        outs[j][...] = (base + x[j * per : (j + 1) * per, :]).astype(jnp.bfloat16)


def fresh_rows(new_kv, x, heads):
    x[...] = new_kv[...].astype(jnp.float32)
    number = x.shape[0] // (2 * heads)
    return [
        jnp.concatenate(
            [x[pl.ds(2 * h + part, number, stride=2 * heads), :] for h in range(heads)], axis=1
        ).astype(jnp.bfloat16)
        for part in range(2)
    ]


def attend(query, keys, values, fresh, length, slot):
    depth = query.shape[0]
    context, width = keys.shape
    heads = width // HEAD
    per = depth // heads
    scale = HEAD**-0.5
    blank = jnp.zeros((per, HEAD), query.dtype)
    spread = jnp.concatenate(
        [
            jnp.concatenate(
                [query[h * per : (h + 1) * per] if i == h else blank for i in range(heads)], axis=1
            )
            for h in range(heads)
        ],
        axis=0,
    )
    all_keys = jnp.concatenate([keys, fresh[0]], axis=0)
    all_values = jnp.concatenate([values, fresh[1]], axis=0)
    scores = lax.dot_general(
        spread, all_keys, (((1,), (1,)), ((), ())), preferred_element_type=jnp.float32
    )
    column = lax.broadcasted_iota(jnp.int32, scores.shape, 1)
    step = lax.broadcasted_iota(jnp.int32, scores.shape, 0) % 2
    fresh_at = column - context - 2 * slot
    visible = (column < length) | ((fresh_at >= 0) & (fresh_at <= step))
    scores = jnp.where(visible, scores * scale, NEG_FILL)
    weights = jnp.exp(scores - jnp.max(scores, axis=1, keepdims=True))
    chance = (weights / jnp.sum(weights, axis=1, keepdims=True)).astype(jnp.bfloat16)
    out = jnp.dot(chance, all_values, preferred_element_type=jnp.float32)
    out = jnp.concatenate(
        [out[h * per : (h + 1) * per, h * HEAD : (h + 1) * HEAD] for h in range(heads)], axis=0
    )
    return out.astype(jnp.bfloat16)


def early_kernel(dims, partners, plan, told, table, pool, new_kv, *refs):
    groups, own_cap, move_cap, _ = dims
    queries, refs = refs[:groups], refs[groups:]
    pages, refs = refs[: len(partners)], refs[len(partners) :]
    attended, cache, sorted_queries, kv, x, kv_sems, query_sems, out_sems = refs
    count, depth, _ = attended.shape
    page = pool.shape[2]

    def here(source):
        known = source == 0
        for j in partners:
            known = known | (source == j)
        return known

    for r in range(count):
        source = told[groups + r]

        @pl.when(source == 0)
        def _(r=r):
            for p in range(table.shape[0]):
                pltpu.make_async_copy(
                    pool.at[:, table[p, r]], kv.at[:, r, pl.ds(p * page, page)], kv_sems.at[r]
                ).start()

        for i, j in enumerate(partners):

            @pl.when(source == j)
            def _(r=r, i=i):
                pltpu.make_async_copy(
                    pages[i].at[told[groups + count + r]], kv.at[:, r], kv_sems.at[r]
                ).start()

    for j in range(groups):
        for k in range(own_cap):
            slot = plan[j * own_cap + k]

            @pl.when(slot >= 0)
            def _(j=j, k=k, slot=slot):
                pltpu.make_async_copy(
                    queries[j].at[pl.ds(k * depth, depth)],
                    sorted_queries.at[slot],
                    query_sems.at[slot],
                ).start()

    fresh = fresh_rows(new_kv, x, kv.shape[3] // HEAD)
    for r in range(count):
        pltpu.make_async_copy(sorted_queries.at[r], sorted_queries.at[r], query_sems.at[r]).wait()

        @pl.when(here(told[groups + r]))
        def _(r=r):
            pltpu.make_async_copy(kv.at[:, r], kv.at[:, r], kv_sems.at[r]).wait()
            pltpu.make_async_copy(kv.at[:, r], cache.at[:, r], out_sems.at[r]).start()

    for r in range(count):
        attended[r] = attend(
            sorted_queries[r], kv[0, r], kv[1, r], fresh, told[groups + 2 * count + r], r
        )
    for r in range(count):

        @pl.when(here(told[groups + r]))
        def _(r=r):
            pltpu.make_async_copy(kv.at[:, r], cache.at[:, r], out_sems.at[r]).wait()


def late_kernel(dims, partners, told, new_kv, queries, attended_in, cache_in, *refs):
    groups, _, move_cap, _ = dims
    pages, refs = refs[: len(partners)], refs[len(partners) :]
    attended, cache, results, x, page_sems, out_sems = refs
    count = queries.shape[0]
    kv_width = cache.shape[3]
    copies = []
    for i, j in enumerate(partners):
        for k in range(move_cap):
            slot = told[groups + 3 * count + j * move_cap + k]
            at = jnp.maximum(slot, 0)
            n = i * move_cap + k
            copies.append(
                (
                    slot,
                    at,
                    pltpu.make_async_copy(pages[i].at[k], cache.at[:, at], page_sems.at[n]),
                    pltpu.make_async_copy(results.at[n], attended.at[at], out_sems.at[n]),
                )
            )
            pl.when(slot >= 0)(copies[-1][2].start)
    fresh = fresh_rows(new_kv, x, kv_width // HEAD)
    for n, (slot, at, _, _) in enumerate(copies):
        i, k = divmod(n, move_cap)
        results[n] = attend(
            queries[at], pages[i][k, 0], pages[i][k, 1], fresh, told[groups + 2 * count + at], at
        )
    for slot, _, _, copy in copies:
        pl.when(slot >= 0)(copy.start)
    for slot, _, page_copy, copy in copies:

        @pl.when(slot >= 0)
        def _(page_copy=page_copy, copy=copy):
            page_copy.wait()
            copy.wait()


def swap(x, axis, j):
    return lax.ppermute(x, axis, [(i, i ^ j) for i in range(lax.axis_size(axis))])


def per_device(
    hidden_in,
    frozen_query_rows,
    new_kv,
    adapter_of,
    adapter_home,
    a_store,
    b_store,
    kv_pool,
    page_table,
    cached_len,
    new_group,
):
    groups = lax.axis_size("req")
    shards = lax.axis_size("mp")
    count, steps, width = hidden_in.shape
    stores, rank, _ = a_store.shape
    _, _, page, kv_width = kv_pool.shape
    context = page_table.shape[1] * page
    heads = kv_width // HEAD
    own_cap = -(-count // min(16, groups))
    move_cap = -(-(count - count // 4) // groups)
    dims = (groups, own_cap, move_cap, stores)
    depth = width // LANES * steps
    number = groups * own_cap
    half = max(groups // 2, 1)
    late = [groups - 1]
    early = [half] + [j for j in range(1, groups - 1) if j != half]
    hidden, frozen = to_tiles(hidden_in), to_tiles(frozen_query_rows)
    table = page_table.T
    fresh = (
        new_kv.reshape(count, steps, 2, heads, HEAD)
        .transpose(0, 1, 3, 2, 4)
        .reshape(count * steps * heads * 2, HEAD)
    )
    bf16, f32, i32 = jnp.bfloat16, jnp.float32, jnp.int32
    shape = jax.ShapeDtypeStruct

    message = shape((2 * own_cap * depth + TILE, LANES), bf16)
    *messages, plan = pl.pallas_call(
        functools.partial(stage_rows_kernel, dims),
        out_shape=[message] * groups + [shape((groups * (own_cap + move_cap),), i32)],
        in_specs=[IN_SMEM] * 4 + [IN_PLACE] * 2,
        out_specs=[IN_PLACE] * groups + [IN_SMEM],
        scratch_shapes=[
            pltpu.SMEM((2 * groups,), i32),
            pltpu.SMEM((groups,), i32),
            pltpu.VMEM((groups, TILE, LANES), bf16),
            pltpu.SemaphoreType.DMA((groups,)),
        ],
        compiler_params=PARAMS,
        name="stage_rows",
    )(adapter_of, adapter_home, new_group, cached_len, hidden, frozen)
    got = {0: messages[0]}
    for j in early + late:
        got[j] = swap(messages[j], "req", j)
    got = [got[j] for j in range(groups)]

    pages = {}
    for partners in (early[:1], early[1:], late):
        outs = pl.pallas_call(
            functools.partial(stage_pages_kernel, dims, partners),
            out_shape=[shape((move_cap, 2, context, kv_width), bf16)] * len(partners),
            in_specs=[IN_SMEM] * 2 + [IN_PLACE],
            out_specs=[IN_PLACE] * len(partners),
            scratch_shapes=[pltpu.SemaphoreType.DMA((len(partners),))],
            compiler_params=PARAMS,
            name="stage_pages",
        )(plan, table, kv_pool)
        for j, out in zip(partners, outs):
            pages[j] = swap(out, "req", j)

    partial, told = pl.pallas_call(
        functools.partial(rank_kernel, dims),
        out_shape=[
            shape((2 * number, stores * rank), f32),
            shape((groups + 3 * count + groups * move_cap,), i32),
        ],
        in_specs=[IN_SMEM] + [IN_VMEM] * (1 + groups),
        out_specs=[IN_VMEM, IN_SMEM],
        scratch_shapes=[
            pltpu.VMEM((number * depth, LANES), f32),
            pltpu.VMEM((max(groups, 8), LANES), i32),
            pltpu.SMEM((max(groups, 8), LANES), i32),
            pltpu.SemaphoreType.DMA,
        ],
        compiler_params=PARAMS,
        name="rank_products",
    )(cached_len, a_store.reshape(stores * rank, width), *got)
    partials = [partial] + [swap(partial, "mp", j) for j in range(1, shards)]

    queries = pl.pallas_call(
        functools.partial(query_kernel, dims, shards),
        out_shape=[shape((own_cap * depth, LANES), bf16)] * groups,
        in_specs=[IN_SMEM] + [IN_VMEM] * (1 + shards + groups),
        out_specs=[IN_VMEM] * groups,
        scratch_shapes=[pltpu.VMEM((number * depth, LANES), f32)],
        compiler_params=PARAMS,
        name="queries",
    )(told, b_store.reshape(stores * rank, width), *partials, *got)
    queries = [queries[0]] + [swap(queries[j], "req", j) for j in range(1, groups)]

    attended, cache, sorted_queries = pl.pallas_call(
        functools.partial(early_kernel, dims, early),
        out_shape=[
            shape((count, depth, LANES), bf16),
            shape((2, count, context, kv_width), bf16),
            shape((count, depth, LANES), bf16),
        ],
        in_specs=[IN_SMEM] * 3 + [IN_PLACE, IN_VMEM] + [IN_PLACE] * (groups + len(early)),
        out_specs=[IN_VMEM, IN_PLACE, IN_VMEM],
        scratch_shapes=[
            pltpu.VMEM((2, count, context, kv_width), bf16),
            pltpu.VMEM(fresh.shape, f32),
            pltpu.SemaphoreType.DMA((count,)),
            pltpu.SemaphoreType.DMA((count,)),
            pltpu.SemaphoreType.DMA((count,)),
        ],
        compiler_params=PARAMS,
        name="attend_early",
    )(plan, told, table, kv_pool, fresh, *queries, *[pages[j] for j in early])

    attended, cache = pl.pallas_call(
        functools.partial(late_kernel, dims, late),
        out_shape=[shape(attended.shape, bf16), shape(cache.shape, bf16)],
        in_specs=[IN_SMEM, IN_VMEM, IN_VMEM, IN_PLACE, IN_PLACE] + [IN_VMEM] * len(late),
        out_specs=[IN_PLACE, IN_PLACE],
        input_output_aliases={3: 0, 4: 1},
        scratch_shapes=[
            pltpu.VMEM((len(late) * move_cap, depth, LANES), bf16),
            pltpu.VMEM(fresh.shape, f32),
            pltpu.SemaphoreType.DMA((len(late) * move_cap,)),
            pltpu.SemaphoreType.DMA((len(late) * move_cap,)),
        ],
        compiler_params=PARAMS,
        name="attend_late",
    )(told, fresh, sorted_queries, attended, cache, *[pages[j] for j in late])
    return from_tiles(attended, steps), cache


def solution(mesh):
    placed = (
        P(("rep", "req"), None, "mp"),
        P(("rep", "req"), None, "mp"),
        P(("rep", "req"), None, None, "mp"),
        P(("rep", "req")),
        P("rep"),
        P(("rep", "req"), None, "mp"),
        P(("rep", "req"), None, "mp"),
        P(None, ("rep", "req"), None, "mp"),
        P(("rep", "req"), None),
        P(("rep", "req")),
        P(("rep", "req")),
    )
    return jax.shard_map(
        per_device,
        mesh=mesh,
        in_specs=placed,
        out_specs=(P(("rep", "req"), None, "mp"), P(None, ("rep", "req"), None, "mp")),
        check_vma=False,
    )
```

```python
import functools

import jax
import jax.numpy as jnp
from jax import lax
from jax.experimental import pallas as pl
from jax.experimental.pallas import tpu as pltpu
from jax.sharding import PartitionSpec as P

HEAD = 128
LANES = 128
TILE = 16
NEG_FILL = -1e30
VMEM_LIMIT = 40 * 1024 * 1024

IN_VMEM = pl.BlockSpec(memory_space=pltpu.VMEM)
IN_SMEM = pl.BlockSpec(memory_space=pltpu.SMEM)
IN_PLACE = pl.BlockSpec(memory_space=pl.ANY)
BYTES_A_MICROSECOND = 3_000_000
PARAMS = pltpu.CompilerParams(vmem_limit_bytes=VMEM_LIMIT)


def to_tiles(rows):
    count, steps, width = rows.shape
    split = rows.reshape(count, steps, width // LANES, LANES)
    return split.transpose(0, 2, 1, 3).reshape(count, width // LANES * steps, LANES)


def from_tiles(tiles, steps):
    count, depth, _ = tiles.shape
    split = tiles.reshape(count, depth // steps, steps, LANES)
    return split.transpose(0, 2, 1, 3).reshape(count, steps, depth // steps * LANES)


def stage_rows_kernel(dims, adapter_of, adapter_home, new_group, cached_len, hidden, frozen, *refs):
    groups, own_cap, move_cap, stores = dims
    messages, plan = refs[:groups], refs[groups]
    counts, picks, meta, *held, held_sems, sems = refs[groups + 1 :]
    count, depth, _ = hidden.shape
    lists = (adapter_home, adapter_of, new_group, cached_len)
    copies = [
        pltpu.make_async_copy(source, target, held_sems.at[i])
        for i, (source, target) in enumerate(zip(lists, held))
    ]
    for copy in copies:
        copy.start()
    adapter_home, adapter_of, new_group, cached_len = held
    me = lax.axis_index("req")
    for i in range(groups * (own_cap + move_cap)):
        plan[i] = -1
    for j in range(groups):
        counts[j] = 0
        counts[groups + j] = 0
        picks[j] = 0
    for copy in copies:
        copy.wait()
    for r in range(count):
        store = adapter_home[adapter_of[r]]
        j = jnp.bitwise_xor(store // stores, me)
        k = counts[j]
        plan[j * own_cap + k] = r
        counts[j] = k + 1
        picks[j] = store % stores
        to = jnp.bitwise_xor(new_group[r], me)

        @pl.when(to != 0)
        def _(to=to, r=r):
            at = counts[groups + to]
            plan[groups * own_cap + to * move_cap + at] = r
            counts[groups + to] = at + 1

    lane = lax.broadcasted_iota(jnp.int32, (TILE, LANES), 1)
    for j in range(groups):
        for k in range(own_cap):
            source = jnp.maximum(plan[j * own_cap + k], 0)
            for part, rows in enumerate((hidden, frozen)):
                pltpu.make_async_copy(
                    rows.at[source],
                    messages[j].at[pl.ds((part * own_cap + k) * depth, depth)],
                    sems.at[j],
                ).start()
        told = jnp.where(lane == 0, picks[j], 0)
        for k in range(move_cap):
            slot = plan[(groups * own_cap) + j * move_cap + k]
            length = cached_len[jnp.maximum(slot, 0)]
            told = jnp.where(lane == 1 + k, slot, told)
            told = jnp.where(lane == 1 + move_cap + k, length, told)
        meta[j] = told.astype(jnp.float32).astype(jnp.bfloat16)
        pltpu.make_async_copy(
            meta.at[j], messages[j].at[pl.ds(2 * own_cap * depth, TILE)], sems.at[j]
        ).start()
    for j in range(groups):
        pltpu.make_async_copy(messages[j], messages[j], sems.at[j]).wait()


def stage_pages_kernel(dims, partners, plan, table, pool, _, *refs):
    groups, own_cap, move_cap, _ = dims
    outs, sems = refs[: len(partners)], refs[len(partners)]
    page = pool.shape[2]
    for i, j in enumerate(partners):
        for k in range(move_cap):
            source = jnp.maximum(plan[groups * own_cap + j * move_cap + k], 0)
            for p in range(table.shape[0]):
                pltpu.make_async_copy(
                    pool.at[:, table[p, source]],
                    outs[i].at[k, :, pl.ds(p * page, page)],
                    sems.at[i],
                ).start()
    for i in range(len(partners)):
        pltpu.make_async_copy(outs[i], outs[i], sems.at[i]).wait()


def rank_kernel(dims, cached_len, a_ref, _, *refs):
    groups, own_cap, move_cap, _ = dims
    messages = refs[:groups]
    partial, told = refs[groups : groups + 2]
    x, meta, meta_scalar, sem = refs[groups + 2 :]
    width = a_ref.shape[1]
    blocks = width // LANES
    depth = 2 * blocks
    per = own_cap * depth
    number = groups * own_cap
    for j in range(groups):
        x[j * per : (j + 1) * per, :] = messages[j][0:per, :].astype(jnp.float32)
        tile = messages[j][2 * per : 2 * per + TILE, :].astype(jnp.float32)
        meta[j : j + 1, :] = tile[0:1, :].astype(jnp.int32)
    copy = pltpu.make_async_copy(meta, meta_scalar, sem)
    copy.start()
    columns = [
        jnp.concatenate([x[pl.ds(2 * c + s, number, stride=depth), :] for s in range(2)], axis=0)
        for c in range(blocks)
    ]
    rows = jnp.concatenate(columns, axis=1).astype(jnp.bfloat16)
    partial[...] = lax.dot_general(
        rows, a_ref[...], (((1,), (1,)), ((), ())), preferred_element_type=jnp.float32
    )
    copy.wait()
    count = cached_len.shape[0]
    for r in range(count):
        told[groups + r] = 0
        told[groups + count + r] = 0
        told[groups + 2 * count + r] = cached_len[r]
    for j in range(groups):
        told[j] = meta_scalar[j, 0]
        for k in range(move_cap):
            slot = meta_scalar[j, 1 + k]
            told[groups + 3 * count + j * move_cap + k] = slot
            if j == 0:
                continue

            @pl.when(slot >= 0)
            def _(slot=slot, j=j, k=k):
                told[groups + slot] = j
                told[groups + count + slot] = k
                told[groups + 2 * count + slot] = meta_scalar[j, 1 + move_cap + k]


def pair_sum(parts):
    while len(parts) > 1:
        parts = [parts[i] + parts[i + 1] for i in range(0, len(parts), 2)]
    return parts[0]


def query_kernel(dims, n_parts, told, b_ref, *refs):
    groups, own_cap, _, stores = dims
    partials, messages = refs[:n_parts], refs[n_parts : n_parts + groups]
    outs, x = refs[n_parts + groups : n_parts + 2 * groups], refs[n_parts + 2 * groups]
    width = b_ref.shape[1]
    rank = b_ref.shape[0] // stores
    blocks = width // LANES
    depth = 2 * blocks
    per = own_cap * depth
    number = groups * own_cap
    full = pair_sum([p[...] for p in partials]).astype(jnp.bfloat16)
    row = lax.broadcasted_iota(jnp.int32, full.shape, 0)
    group_of = (row % number) // own_cap
    pick = jnp.zeros(full.shape, jnp.int32)
    for j in range(groups):
        pick = jnp.where(group_of == j, told[j], pick)
    chosen = lax.broadcasted_iota(jnp.int32, full.shape, 1) // rank == pick
    full = jnp.where(chosen, full.astype(jnp.float32), 0.0).astype(jnp.bfloat16)
    delta = jnp.dot(full, b_ref[...], preferred_element_type=jnp.float32)
    for c in range(blocks):
        for s in range(2):
            x[pl.ds(2 * c + s, number, stride=depth), :] = delta[
                s * number : (s + 1) * number, c * LANES : (c + 1) * LANES
            ]
    for j in range(groups):
        base = messages[j][per : 2 * per, :].astype(jnp.float32)
        outs[j][...] = (base + x[j * per : (j + 1) * per, :]).astype(jnp.bfloat16)


def fresh_rows(new_kv, x, heads):
    x[...] = new_kv[...].astype(jnp.float32)
    number = x.shape[0] // (2 * heads)
    return [
        jnp.concatenate(
            [x[pl.ds(2 * h + part, number, stride=2 * heads), :] for h in range(heads)], axis=1
        ).astype(jnp.bfloat16)
        for part in range(2)
    ]


def attend(query, keys, values, fresh, length, slot):
    depth = query.shape[0]
    context, width = keys.shape
    heads = width // HEAD
    per = depth // heads
    scale = HEAD**-0.5
    blank = jnp.zeros((per, HEAD), query.dtype)
    spread = jnp.concatenate(
        [
            jnp.concatenate(
                [query[h * per : (h + 1) * per] if i == h else blank for i in range(heads)], axis=1
            )
            for h in range(heads)
        ],
        axis=0,
    )
    all_keys = jnp.concatenate([keys, fresh[0]], axis=0)
    all_values = jnp.concatenate([values, fresh[1]], axis=0)
    scores = lax.dot_general(
        spread, all_keys, (((1,), (1,)), ((), ())), preferred_element_type=jnp.float32
    )
    column = lax.broadcasted_iota(jnp.int32, scores.shape, 1)
    step = lax.broadcasted_iota(jnp.int32, scores.shape, 0) % 2
    fresh_at = column - context - 2 * slot
    visible = (column < length) | ((fresh_at >= 0) & (fresh_at <= step))
    scores = jnp.where(visible, scores * scale, NEG_FILL)
    weights = jnp.exp(scores - jnp.max(scores, axis=1, keepdims=True))
    chance = (weights / jnp.sum(weights, axis=1, keepdims=True)).astype(jnp.bfloat16)
    out = jnp.dot(chance, all_values, preferred_element_type=jnp.float32)
    out = jnp.concatenate(
        [out[h * per : (h + 1) * per, h * HEAD : (h + 1) * HEAD] for h in range(heads)], axis=0
    )
    return out.astype(jnp.bfloat16)


def early_kernel(dims, partners, plan, told, table, pool, new_kv, *refs):
    groups, own_cap, move_cap, _ = dims
    queries, refs = refs[:groups], refs[groups:]
    pages, refs = refs[: len(partners)], refs[len(partners) :]
    attended, cache, sorted_queries, kv, x, kv_sems, query_sems, out_sems = refs
    count, depth, _ = attended.shape
    page = pool.shape[2]

    def here(source):
        known = source == 0
        for j in partners:
            known = known | (source == j)
        return known

    for r in range(count):
        source = told[groups + r]

        @pl.when(source == 0)
        def _(r=r):
            for p in range(table.shape[0]):
                pltpu.make_async_copy(
                    pool.at[:, table[p, r]], kv.at[:, r, pl.ds(p * page, page)], kv_sems.at[r]
                ).start()

        for i, j in enumerate(partners):

            @pl.when(source == j)
            def _(r=r, i=i):
                pltpu.make_async_copy(
                    pages[i].at[told[groups + count + r]], kv.at[:, r], kv_sems.at[r]
                ).start()

    for j in range(groups):
        for k in range(own_cap):
            slot = plan[j * own_cap + k]

            @pl.when(slot >= 0)
            def _(j=j, k=k, slot=slot):
                pltpu.make_async_copy(
                    queries[j].at[pl.ds(k * depth, depth)],
                    sorted_queries.at[slot],
                    query_sems.at[slot],
                ).start()

    fresh = fresh_rows(new_kv, x, kv.shape[3] // HEAD)
    for r in range(count):
        pltpu.make_async_copy(sorted_queries.at[r], sorted_queries.at[r], query_sems.at[r]).wait()

        @pl.when(here(told[groups + r]))
        def _(r=r):
            pltpu.make_async_copy(kv.at[:, r], kv.at[:, r], kv_sems.at[r]).wait()
            pltpu.make_async_copy(kv.at[:, r], cache.at[:, r], out_sems.at[r]).start()

    for r in range(count):
        attended[r] = attend(
            sorted_queries[r], kv[0, r], kv[1, r], fresh, told[groups + 2 * count + r], r
        )
    for r in range(count):

        @pl.when(here(told[groups + r]))
        def _(r=r):
            pltpu.make_async_copy(kv.at[:, r], cache.at[:, r], out_sems.at[r]).wait()


def late_kernel(dims, partners, told, new_kv, queries, attended_in, cache_in, *refs):
    groups, _, move_cap, _ = dims
    pages, refs = refs[: len(partners)], refs[len(partners) :]
    attended, cache, results, x, page_sems, out_sems = refs
    count = queries.shape[0]
    kv_width = cache.shape[3]
    copies = []
    for i, j in enumerate(partners):
        for k in range(move_cap):
            slot = told[groups + 3 * count + j * move_cap + k]
            at = jnp.maximum(slot, 0)
            n = i * move_cap + k
            copies.append(
                (
                    slot,
                    at,
                    pltpu.make_async_copy(pages[i].at[k], cache.at[:, at], page_sems.at[n]),
                    pltpu.make_async_copy(results.at[n], attended.at[at], out_sems.at[n]),
                )
            )
            pl.when(slot >= 0)(copies[-1][2].start)
    fresh = fresh_rows(new_kv, x, kv_width // HEAD)
    for n, (slot, at, _, _) in enumerate(copies):
        i, k = divmod(n, move_cap)
        results[n] = attend(
            queries[at], pages[i][k, 0], pages[i][k, 1], fresh, told[groups + 2 * count + at], at
        )
    for slot, _, _, copy in copies:
        pl.when(slot >= 0)(copy.start)
    for slot, _, page_copy, copy in copies:

        @pl.when(slot >= 0)
        def _(page_copy=page_copy, copy=copy):
            page_copy.wait()
            copy.wait()


def lasts(microseconds):
    return pl.CostEstimate(
        flops=int(microseconds * 1e9), transcendentals=0, bytes_accessed=int(microseconds * BYTES_A_MICROSECOND)
    )


def in_hbm(*arrays):
    return [pltpu.with_memory_space_constraint(x, pltpu.HBM) for x in arrays]


def swap(x, axis, j):
    return lax.ppermute(x, axis, [(i, i ^ j) for i in range(lax.axis_size(axis))])


def per_device(
    hidden_in,
    frozen_query_rows,
    new_kv,
    adapter_of,
    adapter_home,
    a_store,
    b_store,
    kv_pool,
    page_table,
    cached_len,
    new_group,
):
    groups = lax.axis_size("req")
    shards = lax.axis_size("mp")
    count, steps, width = hidden_in.shape
    stores, rank, _ = a_store.shape
    _, _, page, kv_width = kv_pool.shape
    context = page_table.shape[1] * page
    heads = kv_width // HEAD
    own_cap = -(-count // min(16, groups))
    move_cap = -(-(count - count // 4) // groups)
    dims = (groups, own_cap, move_cap, stores)
    depth = width // LANES * steps
    number = groups * own_cap
    half = max(groups // 2, 1)
    late = [groups - 1]
    early = [half] if half not in late else []
    middle = [j for j in range(1, groups) if j not in early + late]
    hidden, frozen = to_tiles(hidden_in), to_tiles(frozen_query_rows)
    table, pool = in_hbm(page_table.T, kv_pool)
    fresh = (
        new_kv.reshape(count, steps, 2, heads, HEAD)
        .transpose(0, 1, 3, 2, 4)
        .reshape(count * steps * heads * 2, HEAD)
    )
    bf16, f32, i32 = jnp.bfloat16, jnp.float32, jnp.int32
    shape = jax.ShapeDtypeStruct

    message = shape((2 * own_cap * depth + TILE, LANES), bf16)
    *messages, plan = pl.pallas_call(
        functools.partial(stage_rows_kernel, dims),
        out_shape=[message] * groups + [shape((groups * (own_cap + move_cap),), i32)],
        in_specs=[IN_PLACE] * 6,
        out_specs=[IN_PLACE] * groups + [IN_SMEM],
        scratch_shapes=[
            pltpu.SMEM((2 * groups,), i32),
            pltpu.SMEM((groups,), i32),
            pltpu.VMEM((groups, TILE, LANES), bf16),
            *[
                pltpu.SMEM(held.shape, i32)
                for held in (adapter_home, adapter_of, new_group, cached_len)
            ],
            pltpu.SemaphoreType.DMA((4,)),
            pltpu.SemaphoreType.DMA((groups,)),
        ],
        compiler_params=PARAMS,
        name="stage_rows",
        cost_estimate=lasts(1),
    )(*in_hbm(adapter_of, adapter_home, new_group, cached_len, hidden, frozen))
    got = {0: messages[0]}
    for j in range(1, groups):
        got[j] = swap(messages[j], "req", j)
    got = [got[j] for j in range(groups)]

    def stage_pages(partners, after):
        return pl.pallas_call(
            functools.partial(stage_pages_kernel, dims, partners),
            out_shape=[shape((move_cap, 2, context, kv_width), bf16)] * len(partners),
            in_specs=[IN_SMEM] * 2 + [IN_PLACE] * 2,
            out_specs=[IN_PLACE] * len(partners),
            scratch_shapes=[pltpu.SemaphoreType.DMA((len(partners),))],
            compiler_params=PARAMS,
            name="stage_pages",
            cost_estimate=lasts(0.1),
        )(plan, table, pool, after)

    first_pages = stage_pages(early, got[1])
    pages = {j: swap(x, "req", j) for j, x in zip(early, first_pages)}

    partial, told = pl.pallas_call(
        functools.partial(rank_kernel, dims),
        out_shape=[
            shape((2 * number, stores * rank), f32),
            shape((groups + 3 * count + groups * move_cap,), i32),
        ],
        in_specs=[IN_SMEM, IN_VMEM, IN_PLACE] + [IN_VMEM] * groups,
        out_specs=[IN_VMEM, IN_SMEM],
        scratch_shapes=[
            pltpu.VMEM((number * depth, LANES), f32),
            pltpu.VMEM((max(groups, 8), LANES), i32),
            pltpu.SMEM((max(groups, 8), LANES), i32),
            pltpu.SemaphoreType.DMA,
        ],
        compiler_params=PARAMS,
        name="rank_products",
        cost_estimate=lasts(10),
    )(cached_len, a_store.reshape(stores * rank, width), first_pages[0], *got)
    partials = [partial] + [swap(partial, "mp", j) for j in range(1, shards)]

    queries = pl.pallas_call(
        functools.partial(query_kernel, dims, shards),
        out_shape=[shape((own_cap * depth, LANES), bf16)] * groups,
        in_specs=[IN_SMEM] + [IN_VMEM] * (1 + shards + groups),
        out_specs=[IN_VMEM] * groups,
        scratch_shapes=[pltpu.VMEM((number * depth, LANES), f32)],
        compiler_params=PARAMS,
        name="queries",
        cost_estimate=lasts(0.1),
    )(told, b_store.reshape(stores * rank, width), *partials, *got)
    queries = [queries[0]] + [swap(queries[j], "req", j) for j in range(1, groups)]
    after = queries[1]
    for partners in (middle, late):
        staged = stage_pages(partners, after)
        pages.update((j, swap(x, "req", j)) for j, x in zip(partners, staged))
        after = staged[0]

    attended, cache, sorted_queries = pl.pallas_call(
        functools.partial(early_kernel, dims, early),
        out_shape=[
            shape((count, depth, LANES), bf16),
            shape((2, count, context, kv_width), bf16),
            shape((count, depth, LANES), bf16),
        ],
        in_specs=[IN_SMEM] * 3 + [IN_PLACE, IN_VMEM] + [IN_PLACE] * (groups + len(early)),
        out_specs=[IN_VMEM, IN_PLACE, IN_VMEM],
        scratch_shapes=[
            pltpu.VMEM((2, count, context, kv_width), bf16),
            pltpu.VMEM(fresh.shape, f32),
            pltpu.SemaphoreType.DMA((count,)),
            pltpu.SemaphoreType.DMA((count,)),
            pltpu.SemaphoreType.DMA((count,)),
        ],
        compiler_params=PARAMS,
        name="attend_early",
        cost_estimate=lasts(60),
    )(plan, told, table, pool, fresh, *queries, *[pages[j] for j in early])

    for partners in (middle, late):
        attended, cache = pl.pallas_call(
            functools.partial(late_kernel, dims, partners),
            out_shape=[shape(attended.shape, bf16), shape(cache.shape, bf16)],
            in_specs=[IN_SMEM, IN_VMEM, IN_VMEM] + [IN_PLACE] * 2 + [IN_VMEM] * len(partners),
            out_specs=[IN_PLACE, IN_PLACE],
            input_output_aliases={3: 0, 4: 1},
            scratch_shapes=[
                pltpu.VMEM((len(partners) * move_cap, depth, LANES), bf16),
                pltpu.VMEM(fresh.shape, f32),
                pltpu.SemaphoreType.DMA((len(partners) * move_cap,)),
                pltpu.SemaphoreType.DMA((len(partners) * move_cap,)),
            ],
            compiler_params=PARAMS,
            name="attend_arrived",
            cost_estimate=lasts(1),
        )(told, fresh, sorted_queries, attended, cache, *[pages[j] for j in partners])
    return from_tiles(attended, steps), cache


def solution(mesh):
    placed = (
        P(("rep", "req"), None, "mp"),
        P(("rep", "req"), None, "mp"),
        P(("rep", "req"), None, None, "mp"),
        P(("rep", "req")),
        P("rep"),
        P(("rep", "req"), None, "mp"),
        P(("rep", "req"), None, "mp"),
        P(None, ("rep", "req"), None, "mp"),
        P(("rep", "req"), None),
        P(("rep", "req")),
        P(("rep", "req")),
    )
    return jax.shard_map(
        per_device,
        mesh=mesh,
        in_specs=placed,
        out_specs=(P(("rep", "req"), None, "mp"), P(None, ("rep", "req"), None, "mp")),
        check_vma=False,
    )
```

```python
import functools

import jax
import jax.numpy as jnp
from jax import lax
from jax.experimental import pallas as pl
from jax.experimental.pallas import tpu as pltpu
from jax.sharding import PartitionSpec as P

HEAD = 128
LANES = 128
TILE = 16
NEG_FILL = -1e30
VMEM_LIMIT = 40 * 1024 * 1024

IN_VMEM = pl.BlockSpec(memory_space=pltpu.VMEM)
IN_SMEM = pl.BlockSpec(memory_space=pltpu.SMEM)
IN_PLACE = pl.BlockSpec(memory_space=pl.ANY)
BYTES_A_MICROSECOND = 3_000_000
PARAMS = pltpu.CompilerParams(vmem_limit_bytes=VMEM_LIMIT)


def to_tiles(rows):
    count, steps, width = rows.shape
    split = rows.reshape(count, steps, width // LANES, LANES)
    return split.transpose(0, 2, 1, 3).reshape(count, width // LANES * steps, LANES)


def from_tiles(tiles, steps):
    count, depth, _ = tiles.shape
    split = tiles.reshape(count, depth // steps, steps, LANES)
    return split.transpose(0, 2, 1, 3).reshape(count, steps, depth // steps * LANES)


def stage_rows_kernel(dims, adapter_of, adapter_home, new_group, cached_len, hidden, frozen, *refs):
    groups, own_cap, move_cap, stores = dims
    messages, plan = refs[:groups], refs[groups]
    counts, picks, meta, *held, held_sems, sems = refs[groups + 1 :]
    count, depth, _ = hidden.shape
    lists = (adapter_home, adapter_of, new_group, cached_len)
    copies = [
        pltpu.make_async_copy(source, target, held_sems.at[i])
        for i, (source, target) in enumerate(zip(lists, held))
    ]
    for copy in copies:
        copy.start()
    adapter_home, adapter_of, new_group, cached_len = held
    me = lax.axis_index("req")
    for i in range(groups * (own_cap + move_cap)):
        plan[i] = -1
    for j in range(groups):
        counts[j] = 0
        counts[groups + j] = 0
        picks[j] = 0
    for copy in copies:
        copy.wait()
    for r in range(count):
        store = adapter_home[adapter_of[r]]
        j = jnp.bitwise_xor(store // stores, me)
        k = counts[j]
        plan[j * own_cap + k] = r
        counts[j] = k + 1
        picks[j] = store % stores
        to = jnp.bitwise_xor(new_group[r], me)

        @pl.when(to != 0)
        def _(to=to, r=r):
            at = counts[groups + to]
            plan[groups * own_cap + to * move_cap + at] = r
            counts[groups + to] = at + 1

    lane = lax.broadcasted_iota(jnp.int32, (TILE, LANES), 1)
    for j in range(groups):
        for k in range(own_cap):
            source = jnp.maximum(plan[j * own_cap + k], 0)
            for part, rows in enumerate((hidden, frozen)):
                pltpu.make_async_copy(
                    rows.at[source],
                    messages[j].at[pl.ds((part * own_cap + k) * depth, depth)],
                    sems.at[j],
                ).start()
        told = jnp.where(lane == 0, picks[j], 0)
        for k in range(move_cap):
            slot = plan[(groups * own_cap) + j * move_cap + k]
            length = cached_len[jnp.maximum(slot, 0)]
            told = jnp.where(lane == 1 + k, slot, told)
            told = jnp.where(lane == 1 + move_cap + k, length, told)
        meta[j] = told.astype(jnp.float32).astype(jnp.bfloat16)
        pltpu.make_async_copy(
            meta.at[j], messages[j].at[pl.ds(2 * own_cap * depth, TILE)], sems.at[j]
        ).start()
    for j in range(groups):
        pltpu.make_async_copy(messages[j], messages[j], sems.at[j]).wait()


def stage_pages_kernel(dims, partners, plan, table, pool, *refs):
    groups, own_cap, move_cap, _ = dims
    *outs, sems = refs[-len(partners) - 1 :]
    page = pool.shape[2]
    for i, j in enumerate(partners):
        for k in range(move_cap):
            source = jnp.maximum(plan[groups * own_cap + j * move_cap + k], 0)
            for p in range(table.shape[0]):
                pltpu.make_async_copy(
                    pool.at[:, table[p, source]],
                    outs[i].at[k, :, pl.ds(p * page, page)],
                    sems.at[i],
                ).start()
    for i in range(len(partners)):
        pltpu.make_async_copy(outs[i], outs[i], sems.at[i]).wait()


def rank_kernel(dims, cached_len, a_ref, _, *refs):
    groups, own_cap, move_cap, _ = dims
    messages = refs[:groups]
    partial, told = refs[groups : groups + 2]
    x, meta, meta_scalar, sem = refs[groups + 2 :]
    width = a_ref.shape[1]
    blocks = width // LANES
    depth = 2 * blocks
    per = own_cap * depth
    number = groups * own_cap
    for j in range(groups):
        x[j * per : (j + 1) * per, :] = messages[j][0:per, :].astype(jnp.float32)
        tile = messages[j][2 * per : 2 * per + TILE, :].astype(jnp.float32)
        meta[j : j + 1, :] = tile[0:1, :].astype(jnp.int32)
    copy = pltpu.make_async_copy(meta, meta_scalar, sem)
    copy.start()
    columns = [
        jnp.concatenate([x[pl.ds(2 * c + s, number, stride=depth), :] for s in range(2)], axis=0)
        for c in range(blocks)
    ]
    rows = jnp.concatenate(columns, axis=1).astype(jnp.bfloat16)
    partial[...] = lax.dot_general(
        rows, a_ref[...], (((1,), (1,)), ((), ())), preferred_element_type=jnp.float32
    )
    copy.wait()
    count = cached_len.shape[0]
    for r in range(count):
        told[groups + r] = 0
        told[groups + count + r] = 0
        told[groups + 2 * count + r] = cached_len[r]
    for j in range(groups):
        told[j] = meta_scalar[j, 0]
        for k in range(move_cap):
            slot = meta_scalar[j, 1 + k]
            told[groups + 3 * count + j * move_cap + k] = slot
            if j == 0:
                continue

            @pl.when(slot >= 0)
            def _(slot=slot, j=j, k=k):
                told[groups + slot] = j
                told[groups + count + slot] = k
                told[groups + 2 * count + slot] = meta_scalar[j, 1 + move_cap + k]


def pair_sum(parts):
    while len(parts) > 1:
        parts = [parts[i] + parts[i + 1] for i in range(0, len(parts), 2)]
    return parts[0]


def query_kernel(dims, n_parts, told, b_ref, _, *refs):
    groups, own_cap, _, stores = dims
    partials, messages = refs[:n_parts], refs[n_parts : n_parts + groups]
    outs, x = refs[n_parts + groups : n_parts + 2 * groups], refs[n_parts + 2 * groups]
    width = b_ref.shape[1]
    rank = b_ref.shape[0] // stores
    blocks = width // LANES
    depth = 2 * blocks
    per = own_cap * depth
    number = groups * own_cap
    full = pair_sum([p[...] for p in partials]).astype(jnp.bfloat16)
    row = lax.broadcasted_iota(jnp.int32, full.shape, 0)
    group_of = (row % number) // own_cap
    pick = jnp.zeros(full.shape, jnp.int32)
    for j in range(groups):
        pick = jnp.where(group_of == j, told[j], pick)
    chosen = lax.broadcasted_iota(jnp.int32, full.shape, 1) // rank == pick
    full = jnp.where(chosen, full.astype(jnp.float32), 0.0).astype(jnp.bfloat16)
    delta = jnp.dot(full, b_ref[...], preferred_element_type=jnp.float32)
    for c in range(blocks):
        for s in range(2):
            x[pl.ds(2 * c + s, number, stride=depth), :] = delta[
                s * number : (s + 1) * number, c * LANES : (c + 1) * LANES
            ]
    for j in range(groups):
        base = messages[j][per : 2 * per, :].astype(jnp.float32)
        outs[j][...] = (base + x[j * per : (j + 1) * per, :]).astype(jnp.bfloat16)


def fresh_rows(new_kv, x, heads):
    x[...] = new_kv[...].astype(jnp.float32)
    number = x.shape[0] // (2 * heads)
    return [
        jnp.concatenate(
            [x[pl.ds(2 * h + part, number, stride=2 * heads), :] for h in range(heads)], axis=1
        ).astype(jnp.bfloat16)
        for part in range(2)
    ]


def attend(query, keys, values, fresh, length, slot):
    depth = query.shape[0]
    context, width = keys.shape
    heads = width // HEAD
    per = depth // heads
    scale = HEAD**-0.5
    blank = jnp.zeros((per, HEAD), query.dtype)
    spread = jnp.concatenate(
        [
            jnp.concatenate(
                [query[h * per : (h + 1) * per] if i == h else blank for i in range(heads)], axis=1
            )
            for h in range(heads)
        ],
        axis=0,
    )
    all_keys = jnp.concatenate([keys, fresh[0]], axis=0)
    all_values = jnp.concatenate([values, fresh[1]], axis=0)
    scores = lax.dot_general(
        spread, all_keys, (((1,), (1,)), ((), ())), preferred_element_type=jnp.float32
    )
    column = lax.broadcasted_iota(jnp.int32, scores.shape, 1)
    step = lax.broadcasted_iota(jnp.int32, scores.shape, 0) % 2
    fresh_at = column - context - 2 * slot
    visible = (column < length) | ((fresh_at >= 0) & (fresh_at <= step))
    scores = jnp.where(visible, scores * scale, NEG_FILL)
    weights = jnp.exp(scores - jnp.max(scores, axis=1, keepdims=True))
    chance = (weights / jnp.sum(weights, axis=1, keepdims=True)).astype(jnp.bfloat16)
    out = jnp.dot(chance, all_values, preferred_element_type=jnp.float32)
    out = jnp.concatenate(
        [out[h * per : (h + 1) * per, h * HEAD : (h + 1) * HEAD] for h in range(heads)], axis=0
    )
    return out.astype(jnp.bfloat16)


def early_kernel(dims, partners, plan, told, table, pool, new_kv, *refs):
    groups, own_cap, move_cap, _ = dims
    queries, refs = refs[:groups], refs[groups:]
    pages, refs = refs[: len(partners)], refs[len(partners) :]
    attended, cache, sorted_queries, kv, x, kv_sems, query_sems, out_sems = refs
    count, depth, _ = attended.shape
    page = pool.shape[2]

    def here(source):
        known = source == 0
        for j in partners:
            known = known | (source == j)
        return known

    for r in range(count):
        source = told[groups + r]

        @pl.when(source == 0)
        def _(r=r):
            for p in range(table.shape[0]):
                pltpu.make_async_copy(
                    pool.at[:, table[p, r]], kv.at[:, r, pl.ds(p * page, page)], kv_sems.at[r]
                ).start()

        for i, j in enumerate(partners):

            @pl.when(source == j)
            def _(r=r, i=i):
                pltpu.make_async_copy(
                    pages[i].at[told[groups + count + r]], kv.at[:, r], kv_sems.at[r]
                ).start()

    for j in range(groups):
        for k in range(own_cap):
            slot = plan[j * own_cap + k]

            @pl.when(slot >= 0)
            def _(j=j, k=k, slot=slot):
                pltpu.make_async_copy(
                    queries[j].at[pl.ds(k * depth, depth)],
                    sorted_queries.at[slot],
                    query_sems.at[slot],
                ).start()

    fresh = fresh_rows(new_kv, x, kv.shape[3] // HEAD)
    for r in range(count):
        pltpu.make_async_copy(sorted_queries.at[r], sorted_queries.at[r], query_sems.at[r]).wait()

        @pl.when(here(told[groups + r]))
        def _(r=r):
            pltpu.make_async_copy(kv.at[:, r], kv.at[:, r], kv_sems.at[r]).wait()
            pltpu.make_async_copy(kv.at[:, r], cache.at[:, r], out_sems.at[r]).start()

    for r in range(count):
        attended[r] = attend(
            sorted_queries[r], kv[0, r], kv[1, r], fresh, told[groups + 2 * count + r], r
        )
    for r in range(count):

        @pl.when(here(told[groups + r]))
        def _(r=r):
            pltpu.make_async_copy(kv.at[:, r], cache.at[:, r], out_sems.at[r]).wait()


def late_kernel(dims, partners, told, new_kv, queries, attended_in, cache_in, *refs):
    groups, _, move_cap, _ = dims
    pages, refs = refs[: len(partners)], refs[len(partners) :]
    attended, cache, results, x, page_sems, out_sems = refs
    count = queries.shape[0]
    kv_width = cache.shape[3]
    copies = []
    for i, j in enumerate(partners):
        for k in range(move_cap):
            slot = told[groups + 3 * count + j * move_cap + k]
            at = jnp.maximum(slot, 0)
            n = i * move_cap + k
            copies.append(
                (
                    slot,
                    at,
                    pltpu.make_async_copy(pages[i].at[k], cache.at[:, at], page_sems.at[n]),
                    pltpu.make_async_copy(results.at[n], attended.at[at], out_sems.at[n]),
                )
            )
            pl.when(slot >= 0)(copies[-1][2].start)
    fresh = fresh_rows(new_kv, x, kv_width // HEAD)
    for n, (slot, at, _, _) in enumerate(copies):
        i, k = divmod(n, move_cap)
        results[n] = attend(
            queries[at], pages[i][k, 0], pages[i][k, 1], fresh, told[groups + 2 * count + at], at
        )
    for slot, _, _, copy in copies:
        pl.when(slot >= 0)(copy.start)
    for slot, _, page_copy, copy in copies:

        @pl.when(slot >= 0)
        def _(page_copy=page_copy, copy=copy):
            page_copy.wait()
            copy.wait()


def lasts(microseconds):
    return pl.CostEstimate(
        flops=int(microseconds * 1e9), transcendentals=0, bytes_accessed=int(microseconds * BYTES_A_MICROSECOND)
    )


def in_hbm(*arrays):
    return [pltpu.with_memory_space_constraint(x, pltpu.HBM) for x in arrays]


def swap(x, axis, j):
    return lax.ppermute(x, axis, [(i, i ^ j) for i in range(lax.axis_size(axis))])


def per_device(
    hidden_in,
    frozen_query_rows,
    new_kv,
    adapter_of,
    adapter_home,
    a_store,
    b_store,
    kv_pool,
    page_table,
    cached_len,
    new_group,
):
    groups = lax.axis_size("req")
    shards = lax.axis_size("mp")
    count, steps, width = hidden_in.shape
    stores, rank, _ = a_store.shape
    _, _, page, kv_width = kv_pool.shape
    context = page_table.shape[1] * page
    heads = kv_width // HEAD
    own_cap = -(-count // min(16, groups))
    move_cap = -(-(count - count // 4) // groups)
    dims = (groups, own_cap, move_cap, stores)
    depth = width // LANES * steps
    number = groups * own_cap
    half = max(groups // 2, 1)
    late = [groups - 1]
    early = [half] if half not in late else []
    middle = [j for j in range(1, groups) if j not in early + late]
    hidden, frozen = to_tiles(hidden_in), to_tiles(frozen_query_rows)
    table, pool = in_hbm(page_table.T, kv_pool)
    fresh = (
        new_kv.reshape(count, steps, 2, heads, HEAD)
        .transpose(0, 1, 3, 2, 4)
        .reshape(count * steps * heads * 2, HEAD)
    )
    bf16, f32, i32 = jnp.bfloat16, jnp.float32, jnp.int32
    shape = jax.ShapeDtypeStruct

    message = shape((2 * own_cap * depth + TILE, LANES), bf16)
    *messages, plan = pl.pallas_call(
        functools.partial(stage_rows_kernel, dims),
        out_shape=[message] * groups + [shape((groups * (own_cap + move_cap),), i32)],
        in_specs=[IN_PLACE] * 6,
        out_specs=[IN_PLACE] * groups + [IN_SMEM],
        scratch_shapes=[
            pltpu.SMEM((2 * groups,), i32),
            pltpu.SMEM((groups,), i32),
            pltpu.VMEM((groups, TILE, LANES), bf16),
            *[
                pltpu.SMEM(held.shape, i32)
                for held in (adapter_home, adapter_of, new_group, cached_len)
            ],
            pltpu.SemaphoreType.DMA((4,)),
            pltpu.SemaphoreType.DMA((groups,)),
        ],
        compiler_params=PARAMS,
        name="stage_rows",
        cost_estimate=lasts(1),
    )(*in_hbm(adapter_of, adapter_home, new_group, cached_len, hidden, frozen))
    got = {0: messages[0]}
    for j in range(1, groups):
        got[j] = swap(messages[j], "req", j)
    got = [got[j] for j in range(groups)]

    def stage_pages(partners, *after):
        return pl.pallas_call(
            functools.partial(stage_pages_kernel, dims, partners),
            out_shape=[shape((move_cap, 2, context, kv_width), bf16)] * len(partners),
            in_specs=[IN_SMEM] * 2 + [IN_PLACE] * (1 + len(after)),
            out_specs=[IN_PLACE] * len(partners),
            scratch_shapes=[pltpu.SemaphoreType.DMA((len(partners),))],
            compiler_params=PARAMS,
            name="stage_pages",
            cost_estimate=lasts(0.1),
        )(plan, table, pool, *after)

    first_pages = stage_pages(early, got[half])
    pages = {j: swap(x, "req", j) for j, x in zip(early, first_pages)}

    partial, told = pl.pallas_call(
        functools.partial(rank_kernel, dims),
        out_shape=[
            shape((2 * number, stores * rank), f32),
            shape((groups + 3 * count + groups * move_cap,), i32),
        ],
        in_specs=[IN_SMEM, IN_VMEM, IN_PLACE] + [IN_VMEM] * groups,
        out_specs=[IN_VMEM, IN_SMEM],
        scratch_shapes=[
            pltpu.VMEM((number * depth, LANES), f32),
            pltpu.VMEM((max(groups, 8), LANES), i32),
            pltpu.SMEM((max(groups, 8), LANES), i32),
            pltpu.SemaphoreType.DMA,
        ],
        compiler_params=PARAMS,
        name="rank_products",
        cost_estimate=lasts(10),
    )(cached_len, a_store.reshape(stores * rank, width), first_pages[0], *got)
    partials = [partial] + [swap(partial, "mp", j) for j in range(1, shards)]

    other_pages = stage_pages(late + middle)
    queries = pl.pallas_call(
        functools.partial(query_kernel, dims, shards),
        out_shape=[shape((own_cap * depth, LANES), bf16)] * groups,
        in_specs=[IN_SMEM, IN_VMEM, IN_PLACE] + [IN_VMEM] * (shards + groups),
        out_specs=[IN_VMEM] * groups,
        scratch_shapes=[pltpu.VMEM((number * depth, LANES), f32)],
        compiler_params=PARAMS,
        name="queries",
        cost_estimate=lasts(0.1),
    )(told, b_store.reshape(stores * rank, width), other_pages[0], *partials, *got)
    queries = [queries[0]] + [swap(queries[j], "req", j) for j in range(1, groups)]
    pages.update((j, swap(x, "req", j)) for j, x in zip(late + middle, other_pages))

    attended, cache, sorted_queries = pl.pallas_call(
        functools.partial(early_kernel, dims, early),
        out_shape=[
            shape((count, depth, LANES), bf16),
            shape((2, count, context, kv_width), bf16),
            shape((count, depth, LANES), bf16),
        ],
        in_specs=[IN_SMEM] * 3 + [IN_PLACE, IN_VMEM] + [IN_PLACE] * (groups + len(early)),
        out_specs=[IN_VMEM, IN_PLACE, IN_VMEM],
        scratch_shapes=[
            pltpu.VMEM((2, count, context, kv_width), bf16),
            pltpu.VMEM(fresh.shape, f32),
            pltpu.SemaphoreType.DMA((count,)),
            pltpu.SemaphoreType.DMA((count,)),
            pltpu.SemaphoreType.DMA((count,)),
        ],
        compiler_params=PARAMS,
        name="attend_early",
        cost_estimate=lasts(60),
    )(plan, told, table, pool, fresh, *queries, *[pages[j] for j in early])

    for partners in (middle, late):
        attended, cache = pl.pallas_call(
            functools.partial(late_kernel, dims, partners),
            out_shape=[shape(attended.shape, bf16), shape(cache.shape, bf16)],
            in_specs=[IN_SMEM, IN_VMEM, IN_VMEM] + [IN_PLACE] * 2 + [IN_VMEM] * len(partners),
            out_specs=[IN_PLACE, IN_PLACE],
            input_output_aliases={3: 0, 4: 1},
            scratch_shapes=[
                pltpu.VMEM((len(partners) * move_cap, depth, LANES), bf16),
                pltpu.VMEM(fresh.shape, f32),
                pltpu.SemaphoreType.DMA((len(partners) * move_cap,)),
                pltpu.SemaphoreType.DMA((len(partners) * move_cap,)),
            ],
            compiler_params=PARAMS,
            name="attend_arrived",
            cost_estimate=lasts(1),
        )(told, fresh, sorted_queries, attended, cache, *[pages[j] for j in partners])
    return from_tiles(attended, steps), cache


def solution(mesh):
    placed = (
        P(("rep", "req"), None, "mp"),
        P(("rep", "req"), None, "mp"),
        P(("rep", "req"), None, None, "mp"),
        P(("rep", "req")),
        P("rep"),
        P(("rep", "req"), None, "mp"),
        P(("rep", "req"), None, "mp"),
        P(None, ("rep", "req"), None, "mp"),
        P(("rep", "req"), None),
        P(("rep", "req")),
        P(("rep", "req")),
    )
    return jax.shard_map(
        per_device,
        mesh=mesh,
        in_specs=placed,
        out_specs=(P(("rep", "req"), None, "mp"), P(None, ("rep", "req"), None, "mp")),
        check_vma=False,
    )
```

```python
import functools

import jax
import jax.numpy as jnp
from jax import lax
from jax.experimental import pallas as pl
from jax.experimental.pallas import tpu as pltpu
from jax.sharding import PartitionSpec as P

HEAD = 128
LANES = 128
TILE = 16
NEG_FILL = -1e30
VMEM_LIMIT = 40 * 1024 * 1024

IN_VMEM = pl.BlockSpec(memory_space=pltpu.VMEM)
IN_SMEM = pl.BlockSpec(memory_space=pltpu.SMEM)
IN_PLACE = pl.BlockSpec(memory_space=pl.ANY)
BYTES_A_MICROSECOND = 3_000_000
PARAMS = pltpu.CompilerParams(vmem_limit_bytes=VMEM_LIMIT)


def to_tiles(rows):
    count, steps, width = rows.shape
    split = rows.reshape(count, steps, width // LANES, LANES)
    return split.transpose(0, 2, 1, 3).reshape(count, width // LANES * steps, LANES)


def from_tiles(tiles, steps):
    count, depth, _ = tiles.shape
    split = tiles.reshape(count, depth // steps, steps, LANES)
    return split.transpose(0, 2, 1, 3).reshape(count, steps, depth // steps * LANES)


def stage_rows_kernel(dims, adapter_of, adapter_home, new_group, cached_len, hidden, frozen, *refs):
    groups, own_cap, move_cap, stores = dims
    messages, plan = refs[:groups], refs[groups]
    counts, picks, meta, *held, held_sems, sems = refs[groups + 1 :]
    count, depth, _ = hidden.shape
    lists = (adapter_home, adapter_of, new_group, cached_len)
    copies = [
        pltpu.make_async_copy(source, target, held_sems.at[i])
        for i, (source, target) in enumerate(zip(lists, held))
    ]
    for copy in copies:
        copy.start()
    adapter_home, adapter_of, new_group, cached_len = held
    me = lax.axis_index("req")
    for i in range(groups * (own_cap + move_cap)):
        plan[i] = -1
    for j in range(groups):
        counts[j] = 0
        counts[groups + j] = 0
        picks[j] = 0
    for copy in copies:
        copy.wait()
    for r in range(count):
        store = adapter_home[adapter_of[r]]
        j = jnp.bitwise_xor(store // stores, me)
        k = counts[j]
        plan[j * own_cap + k] = r
        counts[j] = k + 1
        picks[j] = store % stores
        to = jnp.bitwise_xor(new_group[r], me)

        @pl.when(to != 0)
        def _(to=to, r=r):
            at = counts[groups + to]
            plan[groups * own_cap + to * move_cap + at] = r
            counts[groups + to] = at + 1

    lane = lax.broadcasted_iota(jnp.int32, (TILE, LANES), 1)
    for j in range(groups):
        for k in range(own_cap):
            source = jnp.maximum(plan[j * own_cap + k], 0)
            for part, rows in enumerate((hidden, frozen)):
                pltpu.make_async_copy(
                    rows.at[source],
                    messages[j].at[pl.ds((part * own_cap + k) * depth, depth)],
                    sems.at[j],
                ).start()
        told = jnp.where(lane == 0, picks[j], 0)
        for k in range(move_cap):
            slot = plan[(groups * own_cap) + j * move_cap + k]
            length = cached_len[jnp.maximum(slot, 0)]
            told = jnp.where(lane == 1 + k, slot, told)
            told = jnp.where(lane == 1 + move_cap + k, length, told)
        meta[j] = told.astype(jnp.float32).astype(jnp.bfloat16)
        pltpu.make_async_copy(
            meta.at[j], messages[j].at[pl.ds(2 * own_cap * depth, TILE)], sems.at[j]
        ).start()
    for j in range(groups):
        pltpu.make_async_copy(messages[j], messages[j], sems.at[j]).wait()


def stage_pages_kernel(dims, partners, plan, table, pool, *refs):
    groups, own_cap, move_cap, _ = dims
    *outs, sems = refs[-len(partners) - 1 :]
    page = pool.shape[2]
    for i, j in enumerate(partners):
        for k in range(move_cap):
            source = jnp.maximum(plan[groups * own_cap + j * move_cap + k], 0)
            for p in range(table.shape[0]):
                pltpu.make_async_copy(
                    pool.at[:, table[p, source]],
                    outs[i].at[k, :, pl.ds(p * page, page)],
                    sems.at[i],
                ).start()
    for i in range(len(partners)):
        pltpu.make_async_copy(outs[i], outs[i], sems.at[i]).wait()


def rank_kernel(dims, cached_len, a_ref, _, *refs):
    groups, own_cap, move_cap, _ = dims
    messages = refs[:groups]
    partial, told = refs[groups : groups + 2]
    x, meta, meta_scalar, sem = refs[groups + 2 :]
    width = a_ref.shape[1]
    blocks = width // LANES
    depth = 2 * blocks
    per = own_cap * depth
    number = groups * own_cap
    for j in range(groups):
        x[j * per : (j + 1) * per, :] = messages[j][0:per, :].astype(jnp.float32)
        tile = messages[j][2 * per : 2 * per + TILE, :].astype(jnp.float32)
        meta[j : j + 1, :] = tile[0:1, :].astype(jnp.int32)
    copy = pltpu.make_async_copy(meta, meta_scalar, sem)
    copy.start()
    columns = [
        jnp.concatenate([x[pl.ds(2 * c + s, number, stride=depth), :] for s in range(2)], axis=0)
        for c in range(blocks)
    ]
    rows = jnp.concatenate(columns, axis=1).astype(jnp.bfloat16)
    partial[...] = lax.dot_general(
        rows, a_ref[...], (((1,), (1,)), ((), ())), preferred_element_type=jnp.float32
    )
    copy.wait()
    count = cached_len.shape[0]
    for r in range(count):
        told[groups + r] = 0
        told[groups + count + r] = 0
        told[groups + 2 * count + r] = cached_len[r]
    for j in range(groups):
        told[j] = meta_scalar[j, 0]
        for k in range(move_cap):
            slot = meta_scalar[j, 1 + k]
            told[groups + 3 * count + j * move_cap + k] = slot
            if j == 0:
                continue

            @pl.when(slot >= 0)
            def _(slot=slot, j=j, k=k):
                told[groups + slot] = j
                told[groups + count + slot] = k
                told[groups + 2 * count + slot] = meta_scalar[j, 1 + move_cap + k]


def pair_sum(parts):
    while len(parts) > 1:
        parts = [parts[i] + parts[i + 1] for i in range(0, len(parts), 2)]
    return parts[0]


def query_kernel(dims, n_parts, told, b_ref, _, *refs):
    groups, own_cap, _, stores = dims
    partials, messages = refs[:n_parts], refs[n_parts : n_parts + groups]
    outs, x = refs[n_parts + groups : n_parts + 2 * groups], refs[n_parts + 2 * groups]
    width = b_ref.shape[1]
    rank = b_ref.shape[0] // stores
    blocks = width // LANES
    depth = 2 * blocks
    per = own_cap * depth
    number = groups * own_cap
    full = pair_sum([p[...] for p in partials]).astype(jnp.bfloat16)
    row = lax.broadcasted_iota(jnp.int32, full.shape, 0)
    group_of = (row % number) // own_cap
    pick = jnp.zeros(full.shape, jnp.int32)
    for j in range(groups):
        pick = jnp.where(group_of == j, told[j], pick)
    chosen = lax.broadcasted_iota(jnp.int32, full.shape, 1) // rank == pick
    full = jnp.where(chosen, full.astype(jnp.float32), 0.0).astype(jnp.bfloat16)
    delta = jnp.dot(full, b_ref[...], preferred_element_type=jnp.float32)
    for c in range(blocks):
        for s in range(2):
            x[pl.ds(2 * c + s, number, stride=depth), :] = delta[
                s * number : (s + 1) * number, c * LANES : (c + 1) * LANES
            ]
    for j in range(groups):
        base = messages[j][per : 2 * per, :].astype(jnp.float32)
        outs[j][...] = (base + x[j * per : (j + 1) * per, :]).astype(jnp.bfloat16)


def fresh_rows(new_kv, x, heads):
    x[...] = new_kv[...].astype(jnp.float32)
    number = x.shape[0] // (2 * heads)
    return [
        jnp.concatenate(
            [x[pl.ds(2 * h + part, number, stride=2 * heads), :] for h in range(heads)], axis=1
        ).astype(jnp.bfloat16)
        for part in range(2)
    ]


def by_head(query, heads):
    per = query.shape[0] // heads
    blank = jnp.zeros((per, HEAD), query.dtype)
    return jnp.concatenate(
        [
            jnp.concatenate(
                [query[h * per : (h + 1) * per] if i == h else blank for i in range(heads)], axis=1
            )
            for h in range(heads)
        ],
        axis=0,
    )


def attend(queries, keys, values, fresh, lengths, slots):
    depth = queries[0].shape[0]
    context, width = keys[0].shape
    heads = width // HEAD
    per = depth // heads
    scale = HEAD**-0.5
    scores = []
    for query, key, length, slot in zip(queries, keys, lengths, slots):
        product = lax.dot_general(
            by_head(query, heads),
            jnp.concatenate([key, fresh[0]], axis=0),
            (((1,), (1,)), ((), ())),
            preferred_element_type=jnp.float32,
        )
        column = lax.broadcasted_iota(jnp.int32, product.shape, 1)
        step = lax.broadcasted_iota(jnp.int32, product.shape, 0) % 2
        fresh_at = column - context - 2 * slot
        visible = (column < length) | ((fresh_at >= 0) & (fresh_at <= step))
        scores.append(jnp.where(visible, product * scale, NEG_FILL))
    scores = jnp.concatenate(scores, axis=0)
    weights = jnp.exp(scores - jnp.max(scores, axis=1, keepdims=True))
    chances = (weights / jnp.sum(weights, axis=1, keepdims=True)).astype(jnp.bfloat16)
    results = []
    for n, value in enumerate(values):
        out = jnp.dot(
            chances[n * depth : (n + 1) * depth],
            jnp.concatenate([value, fresh[1]], axis=0),
            preferred_element_type=jnp.float32,
        )
        out = jnp.concatenate(
            [out[h * per : (h + 1) * per, h * HEAD : (h + 1) * HEAD] for h in range(heads)], axis=0
        )
        results.append(out.astype(jnp.bfloat16))
    return results


def place_kernel(dims, told, table, pool, _, cache, kv, kv_sems, out_sems):
    groups = dims[0]
    count = kv.shape[1]
    page = pool.shape[2]
    for r in range(count):

        @pl.when(told[groups + r] == 0)
        def _(r=r):
            for p in range(table.shape[0]):
                pltpu.make_async_copy(
                    pool.at[:, table[p, r]], kv.at[:, r, pl.ds(p * page, page)], kv_sems.at[r]
                ).start()

    for r in range(count):

        @pl.when(told[groups + r] == 0)
        def _(r=r):
            pltpu.make_async_copy(kv.at[:, r], kv.at[:, r], kv_sems.at[r]).wait()
            pltpu.make_async_copy(kv.at[:, r], cache.at[:, r], out_sems.at[r]).start()

    for r in range(count):

        @pl.when(told[groups + r] == 0)
        def _(r=r):
            pltpu.make_async_copy(kv.at[:, r], cache.at[:, r], out_sems.at[r]).wait()


def arrivals(dims, partners, told, count, pages):
    groups, _, move_cap, _ = dims
    blocks, slots = [], []
    for i, j in enumerate(partners):
        for k in range(move_cap):
            blocks.append(pages[i].at[k])
            slots.append(told[groups + 3 * count + j * move_cap + k])
    return blocks, slots, [jnp.maximum(slot, 0) for slot in slots]


def early_kernel(dims, partners, plan, told, kv, new_kv, cache_in, *refs):
    groups, own_cap, _, _ = dims
    queries, refs = refs[:groups], refs[groups:]
    pages, refs = refs[: len(partners)], refs[len(partners) :]
    attended, sorted_queries, cache, x, page_sems = refs
    count, depth, _ = attended.shape
    blocks, slots, places = arrivals(dims, partners, told, count, pages)
    copies = [
        pltpu.make_async_copy(block, cache.at[:, at], page_sems.at[n])
        for n, (block, at) in enumerate(zip(blocks, places))
    ]
    for slot, copy in zip(slots, copies):
        pl.when(slot >= 0)(copy.start)
    for j in range(groups):
        for k in range(own_cap):
            slot = plan[j * own_cap + k]

            @pl.when(slot >= 0)
            def _(j=j, k=k, slot=slot):
                sorted_queries[slot] = queries[j][k * depth : (k + 1) * depth, :]

    every = list(range(count))
    results = attend(
        [sorted_queries[at] for at in every + places],
        [kv[0, r] for r in every] + [block[0] for block in blocks],
        [kv[1, r] for r in every] + [block[1] for block in blocks],
        fresh_rows(new_kv, x, kv.shape[3] // HEAD),
        [told[groups + 2 * count + at] for at in every + places],
        every + places,
    )
    for r in every:
        attended[r] = results[r]
    for n, (slot, at) in enumerate(zip(slots, places)):

        @pl.when(slot >= 0)
        def _(n=n, at=at):
            attended[at] = results[count + n]

    for slot, copy in zip(slots, copies):
        pl.when(slot >= 0)(copy.wait)


def late_kernel(dims, partners, told, new_kv, queries, attended_in, cache_in, *refs):
    groups = dims[0]
    pages, refs = refs[: len(partners)], refs[len(partners) :]
    attended, cache, results, x, page_sems, out_sems = refs
    count = queries.shape[0]
    blocks, slots, places = arrivals(dims, partners, told, count, pages)
    copies = [
        (
            pltpu.make_async_copy(block, cache.at[:, at], page_sems.at[n]),
            pltpu.make_async_copy(results.at[n], attended.at[at], out_sems.at[n]),
        )
        for n, (block, at) in enumerate(zip(blocks, places))
    ]
    for slot, (copy, _) in zip(slots, copies):
        pl.when(slot >= 0)(copy.start)
    outs = attend(
        [queries[at] for at in places],
        [block[0] for block in blocks],
        [block[1] for block in blocks],
        fresh_rows(new_kv, x, cache.shape[3] // HEAD),
        [told[groups + 2 * count + at] for at in places],
        places,
    )
    for n, out in enumerate(outs):
        results[n] = out
    for slot, (_, copy) in zip(slots, copies):
        pl.when(slot >= 0)(copy.start)
    for slot, pair in zip(slots, copies):

        @pl.when(slot >= 0)
        def _(pair=pair):
            for copy in pair:
                copy.wait()


def lasts(microseconds):
    return pl.CostEstimate(
        flops=int(microseconds * 1e9), transcendentals=0, bytes_accessed=int(microseconds * BYTES_A_MICROSECOND)
    )


def in_hbm(*arrays):
    return [pltpu.with_memory_space_constraint(x, pltpu.HBM) for x in arrays]


def swap(x, axis, j):
    return lax.ppermute(x, axis, [(i, i ^ j) for i in range(lax.axis_size(axis))])


def per_device(
    hidden_in,
    frozen_query_rows,
    new_kv,
    adapter_of,
    adapter_home,
    a_store,
    b_store,
    kv_pool,
    page_table,
    cached_len,
    new_group,
):
    groups = lax.axis_size("req")
    shards = lax.axis_size("mp")
    count, steps, width = hidden_in.shape
    stores, rank, _ = a_store.shape
    _, _, page, kv_width = kv_pool.shape
    context = page_table.shape[1] * page
    heads = kv_width // HEAD
    own_cap = -(-count // min(16, groups))
    move_cap = -(-(count - count // 4) // groups)
    dims = (groups, own_cap, move_cap, stores)
    depth = width // LANES * steps
    number = groups * own_cap
    half = max(groups // 2, 1)
    early = [half]
    late = [j for j in range(1, groups) if j != half]
    hidden, frozen = to_tiles(hidden_in), to_tiles(frozen_query_rows)
    table, pool = in_hbm(page_table.T, kv_pool)
    fresh = (
        new_kv.reshape(count, steps, 2, heads, HEAD)
        .transpose(0, 1, 3, 2, 4)
        .reshape(count * steps * heads * 2, HEAD)
    )
    bf16, f32, i32 = jnp.bfloat16, jnp.float32, jnp.int32
    shape = jax.ShapeDtypeStruct

    message = shape((2 * own_cap * depth + TILE, LANES), bf16)
    *messages, plan = pl.pallas_call(
        functools.partial(stage_rows_kernel, dims),
        out_shape=[message] * groups + [shape((groups * (own_cap + move_cap),), i32)],
        in_specs=[IN_PLACE] * 6,
        out_specs=[IN_PLACE] * groups + [IN_SMEM],
        scratch_shapes=[
            pltpu.SMEM((2 * groups,), i32),
            pltpu.SMEM((groups,), i32),
            pltpu.VMEM((groups, TILE, LANES), bf16),
            *[
                pltpu.SMEM(held.shape, i32)
                for held in (adapter_home, adapter_of, new_group, cached_len)
            ],
            pltpu.SemaphoreType.DMA((4,)),
            pltpu.SemaphoreType.DMA((groups,)),
        ],
        compiler_params=PARAMS,
        name="stage_rows",
        cost_estimate=lasts(1),
    )(*in_hbm(adapter_of, adapter_home, new_group, cached_len, hidden, frozen))
    got = {0: messages[0]}
    for j in range(1, groups):
        got[j] = swap(messages[j], "req", j)
    got = [got[j] for j in range(groups)]

    def stage_pages(partners, *after):
        return pl.pallas_call(
            functools.partial(stage_pages_kernel, dims, partners),
            out_shape=[shape((move_cap, 2, context, kv_width), bf16)] * len(partners),
            in_specs=[IN_SMEM] * 2 + [IN_PLACE] * (1 + len(after)),
            out_specs=[IN_PLACE] * len(partners),
            scratch_shapes=[pltpu.SemaphoreType.DMA((len(partners),))],
            compiler_params=PARAMS,
            name="stage_pages",
            cost_estimate=lasts(0.1),
        )(plan, table, pool, *after)

    staged = stage_pages(early, got[half])
    pages = {j: swap(x, "req", j) for j, x in zip(early, staged)}

    partial, told = pl.pallas_call(
        functools.partial(rank_kernel, dims),
        out_shape=[
            shape((2 * number, stores * rank), f32),
            shape((groups + 3 * count + groups * move_cap,), i32),
        ],
        in_specs=[IN_SMEM, IN_VMEM, IN_PLACE] + [IN_VMEM] * groups,
        out_specs=[IN_VMEM, IN_SMEM],
        scratch_shapes=[
            pltpu.VMEM((number * depth, LANES), f32),
            pltpu.VMEM((max(groups, 8), LANES), i32),
            pltpu.SMEM((max(groups, 8), LANES), i32),
            pltpu.SemaphoreType.DMA,
        ],
        compiler_params=PARAMS,
        name="rank_products",
        cost_estimate=lasts(10),
    )(cached_len, a_store.reshape(stores * rank, width), staged[-1], *got)
    partials = [partial] + [swap(partial, "mp", j) for j in range(1, shards)]

    last_pages = stage_pages(late)
    queries = pl.pallas_call(
        functools.partial(query_kernel, dims, shards),
        out_shape=[shape((own_cap * depth, LANES), bf16)] * groups,
        in_specs=[IN_SMEM, IN_VMEM, IN_PLACE] + [IN_VMEM] * (shards + groups),
        out_specs=[IN_VMEM] * groups,
        scratch_shapes=[pltpu.VMEM((number * depth, LANES), f32)],
        compiler_params=PARAMS,
        name="queries",
        cost_estimate=lasts(0.1),
    )(told, b_store.reshape(stores * rank, width), last_pages[0], *partials, *got)
    queries = [queries[0]] + [swap(queries[j], "req", j) for j in range(1, groups)]
    pages.update((j, swap(x, "req", j)) for j, x in zip(late, last_pages))

    cache, kv = pl.pallas_call(
        functools.partial(place_kernel, dims),
        out_shape=[shape((2, count, context, kv_width), bf16)] * 2,
        in_specs=[IN_SMEM] * 2 + [IN_PLACE] * 2,
        out_specs=[IN_PLACE] * 2,
        scratch_shapes=[pltpu.SemaphoreType.DMA((count,))] * 2,
        compiler_params=PARAMS,
        name="place_pages",
        cost_estimate=lasts(0.1),
    )(told, table, pool, queries[0])
    attended, sorted_queries, cache = pl.pallas_call(
        functools.partial(early_kernel, dims, early),
        out_shape=[shape((count, depth, LANES), bf16)] * 2 + [shape(cache.shape, bf16)],
        in_specs=[IN_SMEM] * 2 + [IN_VMEM] * 2 + [IN_PLACE] + [IN_VMEM] * (groups + len(early)),
        out_specs=[IN_VMEM] * 2 + [IN_PLACE],
        input_output_aliases={4: 2},
        scratch_shapes=[
            pltpu.VMEM(fresh.shape, f32),
            pltpu.SemaphoreType.DMA((len(early) * move_cap,)),
        ],
        compiler_params=PARAMS,
        name="attend_early",
        cost_estimate=lasts(60),
    )(plan, told, kv, fresh, cache, *queries, *[pages[j] for j in early])
    for partners in (late,):
        attended, cache = pl.pallas_call(
            functools.partial(late_kernel, dims, partners),
            out_shape=[shape(attended.shape, bf16), shape(cache.shape, bf16)],
            in_specs=[IN_SMEM, IN_VMEM, IN_VMEM] + [IN_PLACE] * 2 + [IN_VMEM] * len(partners),
            out_specs=[IN_PLACE, IN_PLACE],
            input_output_aliases={3: 0, 4: 1},
            scratch_shapes=[
                pltpu.VMEM((len(partners) * move_cap, depth, LANES), bf16),
                pltpu.VMEM(fresh.shape, f32),
                pltpu.SemaphoreType.DMA((len(partners) * move_cap,)),
                pltpu.SemaphoreType.DMA((len(partners) * move_cap,)),
            ],
            compiler_params=PARAMS,
            name="attend_arrived",
            cost_estimate=lasts(1),
        )(told, fresh, sorted_queries, attended, cache, *[pages[j] for j in partners])
    return from_tiles(attended, steps), cache


def solution(mesh):
    placed = (
        P(("rep", "req"), None, "mp"),
        P(("rep", "req"), None, "mp"),
        P(("rep", "req"), None, None, "mp"),
        P(("rep", "req")),
        P("rep"),
        P(("rep", "req"), None, "mp"),
        P(("rep", "req"), None, "mp"),
        P(None, ("rep", "req"), None, "mp"),
        P(("rep", "req"), None),
        P(("rep", "req")),
        P(("rep", "req")),
    )
    return jax.shard_map(
        per_device,
        mesh=mesh,
        in_specs=placed,
        out_specs=(P(("rep", "req"), None, "mp"), P(None, ("rep", "req"), None, "mp")),
        check_vma=False,
    )
```

```python
import functools

import jax
import jax.numpy as jnp
from jax import lax
from jax.experimental import pallas as pl
from jax.experimental.pallas import tpu as pltpu
from jax.sharding import PartitionSpec as P

HEAD = 128
LANES = 128
TILE = 16
NEG_FILL = -1e30
VMEM_LIMIT = 40 * 1024 * 1024

IN_VMEM = pl.BlockSpec(memory_space=pltpu.VMEM)
IN_SMEM = pl.BlockSpec(memory_space=pltpu.SMEM)
IN_PLACE = pl.BlockSpec(memory_space=pl.ANY)
BYTES_A_MICROSECOND = 3_000_000
PARAMS = pltpu.CompilerParams(vmem_limit_bytes=VMEM_LIMIT)


def to_tiles(rows):
    count, steps, width = rows.shape
    split = rows.reshape(count, steps, width // LANES, LANES)
    return split.transpose(0, 2, 1, 3).reshape(count, width // LANES * steps, LANES)


def from_tiles(tiles, steps):
    count, depth, _ = tiles.shape
    split = tiles.reshape(count, depth // steps, steps, LANES)
    return split.transpose(0, 2, 1, 3).reshape(count, steps, depth // steps * LANES)


def stage_rows_kernel(dims, adapter_of, adapter_home, new_group, cached_len, hidden, frozen, *refs):
    groups, own_cap, move_cap, stores = dims
    messages, plan = refs[:groups], refs[groups]
    counts, picks, *held, held_sems = refs[groups + 1 :]
    count, depth, _ = hidden.shape
    lists = (adapter_home, adapter_of, new_group, cached_len, hidden, frozen)
    copies = [
        pltpu.make_async_copy(source, target, held_sems.at[i])
        for i, (source, target) in enumerate(zip(lists, held))
    ]
    for copy in copies:
        copy.start()
    adapter_home, adapter_of, new_group, cached_len, hidden, frozen = held
    me = lax.axis_index("req")
    for i in range(groups * (own_cap + move_cap)):
        plan[i] = -1
    for j in range(groups):
        counts[j] = 0
        counts[groups + j] = 0
        picks[j] = 0
    for copy in copies[:4]:
        copy.wait()
    for r in range(count):
        store = adapter_home[adapter_of[r]]
        j = jnp.bitwise_xor(store // stores, me)
        k = counts[j]
        plan[j * own_cap + k] = r
        counts[j] = k + 1
        picks[j] = store % stores
        to = jnp.bitwise_xor(new_group[r], me)

        @pl.when(to != 0)
        def _(to=to, r=r):
            at = counts[groups + to]
            plan[groups * own_cap + to * move_cap + at] = r
            counts[groups + to] = at + 1

    lane = lax.broadcasted_iota(jnp.int32, (TILE, LANES), 1)
    for j in range(groups):
        told = jnp.where(lane == 0, picks[j], 0)
        for k in range(move_cap):
            slot = plan[groups * own_cap + j * move_cap + k]
            length = cached_len[jnp.maximum(slot, 0)]
            told = jnp.where(lane == 1 + k, slot, told)
            told = jnp.where(lane == 1 + move_cap + k, length, told)
        messages[j][2 * own_cap * depth :, :] = told.astype(jnp.float32).astype(jnp.bfloat16)
    for part, rows in enumerate((hidden, frozen)):
        copies[4 + part].wait()
        for j in range(groups):
            for k in range(own_cap):
                source = jnp.maximum(plan[j * own_cap + k], 0)
                at = (part * own_cap + k) * depth
                messages[j][at : at + depth, :] = rows[source]


def page_routes(groups):
    half = groups // 2

    def across(j):
        return tuple(g ^ j for g in range(groups))

    between = [across(j) for j in range(1, groups - 1) if j != half]
    return between + [across(half)], [across(groups - 1)] if groups > 2 else []


def partner(route, me, arriving):
    if arriving:
        route = [route.index(g) if g in route else -1 for g in range(len(route))]
    codes = [g ^ other if other >= 0 else 0 for g, other in enumerate(route)]
    if len(set(codes)) == 1:
        return codes[0]
    chosen = 0
    for g, code in enumerate(codes):
        chosen = jnp.where(me == g, code, chosen)
    return chosen


def stage_pages_kernel(dims, routes, plan, table, pool, *refs):
    groups, own_cap, move_cap, _ = dims
    *outs, sems = refs[-len(routes) - 1 :]
    page = pool.shape[2]
    me = lax.axis_index("req")
    for i, route in enumerate(routes):
        j = partner(route, me, False)
        for k in range(move_cap):
            source = jnp.maximum(plan[groups * own_cap + j * move_cap + k], 0)
            for p in range(table.shape[0]):
                pltpu.make_async_copy(
                    pool.at[:, table[p, source]],
                    outs[i].at[k, :, pl.ds(p * page, page)],
                    sems.at[i],
                ).start()
    for i in range(len(routes)):
        pltpu.make_async_copy(outs[i], outs[i], sems.at[i]).wait()


def rank_kernel(dims, order, cached_len, a_ref, _, *refs):
    groups, own_cap, move_cap, _ = dims
    messages = [refs[order.index(j)] for j in range(groups)]
    partial, told = refs[groups : groups + 2]
    x, meta, meta_scalar, sem = refs[groups + 2 :]
    width = a_ref.shape[1]
    blocks = width // LANES
    depth = 2 * blocks
    per = own_cap * depth
    number = groups * own_cap
    for j in range(groups):
        x[j * per : (j + 1) * per, :] = messages[j][0:per, :].astype(jnp.float32)
        tile = messages[j][2 * per : 2 * per + TILE, :].astype(jnp.float32)
        meta[j : j + 1, :] = tile[0:1, :].astype(jnp.int32)
    copy = pltpu.make_async_copy(meta, meta_scalar, sem)
    copy.start()
    columns = [
        jnp.concatenate([x[pl.ds(2 * c + s, number, stride=depth), :] for s in range(2)], axis=0)
        for c in range(blocks)
    ]
    rows = jnp.concatenate(columns, axis=1).astype(jnp.bfloat16)
    partial[...] = lax.dot_general(
        rows, a_ref[...], (((1,), (1,)), ((), ())), preferred_element_type=jnp.float32
    )
    copy.wait()
    count = cached_len.shape[0]
    for r in range(count):
        told[groups + r] = 0
        told[groups + count + r] = 0
        told[groups + 2 * count + r] = cached_len[r]
    for j in range(groups):
        told[j] = meta_scalar[j, 0]
        for k in range(move_cap):
            slot = meta_scalar[j, 1 + k]
            told[groups + 3 * count + j * move_cap + k] = slot
            if j == 0:
                continue

            @pl.when(slot >= 0)
            def _(slot=slot, j=j, k=k):
                told[groups + slot] = j
                told[groups + count + slot] = k
                told[groups + 2 * count + slot] = meta_scalar[j, 1 + move_cap + k]


def pair_sum(parts):
    while len(parts) > 1:
        parts = [parts[i] + parts[i + 1] for i in range(0, len(parts), 2)]
    return parts[0]


def query_kernel(dims, n_parts, told, b_ref, _, *refs):
    groups, own_cap, _, stores = dims
    partials, messages = refs[:n_parts], refs[n_parts : n_parts + groups]
    outs, x = refs[n_parts + groups : n_parts + 2 * groups], refs[n_parts + 2 * groups]
    width = b_ref.shape[1]
    rank = b_ref.shape[0] // stores
    blocks = width // LANES
    depth = 2 * blocks
    per = own_cap * depth
    number = groups * own_cap
    full = pair_sum([p[...] for p in partials]).astype(jnp.bfloat16)
    row = lax.broadcasted_iota(jnp.int32, full.shape, 0)
    group_of = (row % number) // own_cap
    pick = jnp.zeros(full.shape, jnp.int32)
    for j in range(groups):
        pick = jnp.where(group_of == j, told[j], pick)
    chosen = lax.broadcasted_iota(jnp.int32, full.shape, 1) // rank == pick
    full = jnp.where(chosen, full.astype(jnp.float32), 0.0).astype(jnp.bfloat16)
    delta = jnp.dot(full, b_ref[...], preferred_element_type=jnp.float32)
    for c in range(blocks):
        for s in range(2):
            x[pl.ds(2 * c + s, number, stride=depth), :] = delta[
                s * number : (s + 1) * number, c * LANES : (c + 1) * LANES
            ]
    for j in range(groups):
        base = messages[j][per : 2 * per, :].astype(jnp.float32)
        outs[j][...] = (base + x[j * per : (j + 1) * per, :]).astype(jnp.bfloat16)


def fresh_rows(new_kv, x, heads):
    x[...] = new_kv[...].astype(jnp.float32)
    number = x.shape[0] // (2 * heads)
    return [
        jnp.concatenate(
            [x[pl.ds(2 * h + part, number, stride=2 * heads), :] for h in range(heads)], axis=1
        ).astype(jnp.bfloat16)
        for part in range(2)
    ]


def by_head(query, heads):
    per = query.shape[0] // heads
    blank = jnp.zeros((per, HEAD), query.dtype)
    return jnp.concatenate(
        [
            jnp.concatenate(
                [query[h * per : (h + 1) * per] if i == h else blank for i in range(heads)], axis=1
            )
            for h in range(heads)
        ],
        axis=0,
    )


def attend(queries, keys, values, fresh, lengths, slots):
    depth = queries[0].shape[0]
    context, width = keys[0].shape
    heads = width // HEAD
    per = depth // heads
    scale = HEAD**-0.5
    scores = []
    for query, key, length, slot in zip(queries, keys, lengths, slots):
        product = lax.dot_general(
            by_head(query, heads),
            jnp.concatenate([key, fresh[0]], axis=0),
            (((1,), (1,)), ((), ())),
            preferred_element_type=jnp.float32,
        )
        column = lax.broadcasted_iota(jnp.int32, product.shape, 1)
        step = lax.broadcasted_iota(jnp.int32, product.shape, 0) % 2
        fresh_at = column - context - 2 * slot
        visible = (column < length) | ((fresh_at >= 0) & (fresh_at <= step))
        scores.append(jnp.where(visible, product * scale, NEG_FILL))
    scores = jnp.concatenate(scores, axis=0)
    weights = jnp.exp(scores - jnp.max(scores, axis=1, keepdims=True))
    chances = (weights / jnp.sum(weights, axis=1, keepdims=True)).astype(jnp.bfloat16)
    results = []
    for n, value in enumerate(values):
        out = jnp.dot(
            chances[n * depth : (n + 1) * depth],
            jnp.concatenate([value, fresh[1]], axis=0),
            preferred_element_type=jnp.float32,
        )
        out = jnp.concatenate(
            [out[h * per : (h + 1) * per, h * HEAD : (h + 1) * HEAD] for h in range(heads)], axis=0
        )
        results.append(out.astype(jnp.bfloat16))
    return results


def place_kernel(dims, told, table, pool, *refs):
    cache, kv, kv_sems, out_sems = refs[-4:]
    groups = dims[0]
    count = kv.shape[1]
    page = pool.shape[2]
    for r in range(count):

        @pl.when(told[groups + r] == 0)
        def _(r=r):
            for p in range(table.shape[0]):
                pltpu.make_async_copy(
                    pool.at[:, table[p, r]], kv.at[:, r, pl.ds(p * page, page)], kv_sems.at[r]
                ).start()

    for r in range(count):

        @pl.when(told[groups + r] == 0)
        def _(r=r):
            pltpu.make_async_copy(kv.at[:, r], kv.at[:, r], kv_sems.at[r]).wait()
            pltpu.make_async_copy(kv.at[:, r], cache.at[:, r], out_sems.at[r]).start()

    for r in range(count):

        @pl.when(told[groups + r] == 0)
        def _(r=r):
            pltpu.make_async_copy(kv.at[:, r], cache.at[:, r], out_sems.at[r]).wait()


def arrivals(dims, routes, told, count, pages):
    groups, _, move_cap, _ = dims
    me = lax.axis_index("req")
    blocks, slots = [], []
    for i, route in enumerate(routes):
        j = partner(route, me, True)
        for k in range(move_cap):
            blocks.append(pages[i].at[k])
            slots.append(told[groups + 3 * count + j * move_cap + k])
    return blocks, slots, [jnp.maximum(slot, 0) for slot in slots]


def early_kernel(dims, routes, plan, told, kv, new_kv, cache_in, *refs):
    groups, own_cap, _, _ = dims
    queries, refs = refs[:groups], refs[groups:]
    pages, refs = refs[: len(routes)], refs[len(routes) :]
    attended, sorted_queries, cache, x, page_sems = refs
    count, depth, _ = attended.shape
    blocks, slots, places = arrivals(dims, routes, told, count, pages)
    copies = [
        pltpu.make_async_copy(block, cache.at[:, at], page_sems.at[n])
        for n, (block, at) in enumerate(zip(blocks, places))
    ]
    for slot, copy in zip(slots, copies):
        pl.when(slot >= 0)(copy.start)
    for j in range(groups):
        for k in range(own_cap):
            slot = plan[j * own_cap + k]

            @pl.when(slot >= 0)
            def _(j=j, k=k, slot=slot):
                sorted_queries[slot] = queries[j][k * depth : (k + 1) * depth, :]

    every = list(range(count))
    results = attend(
        [sorted_queries[at] for at in every + places],
        [kv[0, r] for r in every] + [block[0] for block in blocks],
        [kv[1, r] for r in every] + [block[1] for block in blocks],
        fresh_rows(new_kv, x, kv.shape[3] // HEAD),
        [told[groups + 2 * count + at] for at in every + places],
        every + places,
    )
    for r in every:
        attended[r] = results[r]
    for n, (slot, at) in enumerate(zip(slots, places)):

        @pl.when(slot >= 0)
        def _(n=n, at=at):
            attended[at] = results[count + n]

    for slot, copy in zip(slots, copies):
        pl.when(slot >= 0)(copy.wait)


def late_kernel(dims, routes, told, new_kv, queries, attended_in, cache_in, *refs):
    groups = dims[0]
    pages, refs = refs[: len(routes)], refs[len(routes) :]
    attended, cache, results, x, page_sems, out_sems = refs
    count = queries.shape[0]
    blocks, slots, places = arrivals(dims, routes, told, count, pages)
    copies = [
        (
            pltpu.make_async_copy(block, cache.at[:, at], page_sems.at[n]),
            pltpu.make_async_copy(results.at[n], attended.at[at], out_sems.at[n]),
        )
        for n, (block, at) in enumerate(zip(blocks, places))
    ]
    for slot, (copy, _) in zip(slots, copies):
        pl.when(slot >= 0)(copy.start)
    outs = attend(
        [queries[at] for at in places],
        [block[0] for block in blocks],
        [block[1] for block in blocks],
        fresh_rows(new_kv, x, cache.shape[3] // HEAD),
        [told[groups + 2 * count + at] for at in places],
        places,
    )
    for n, out in enumerate(outs):
        results[n] = out
    for slot, (_, copy) in zip(slots, copies):
        pl.when(slot >= 0)(copy.start)
    for slot, pair in zip(slots, copies):

        @pl.when(slot >= 0)
        def _(pair=pair):
            for copy in pair:
                copy.wait()


def lasts(microseconds):
    return pl.CostEstimate(
        flops=int(microseconds * 1e9), transcendentals=0, bytes_accessed=int(microseconds * BYTES_A_MICROSECOND)
    )


def in_hbm(*arrays):
    return [pltpu.with_memory_space_constraint(x, pltpu.HBM) for x in arrays]


def swap(x, axis, j):
    return lax.ppermute(x, axis, [(i, i ^ j) for i in range(lax.axis_size(axis))])


def per_device(
    hidden_in,
    frozen_query_rows,
    new_kv,
    adapter_of,
    adapter_home,
    a_store,
    b_store,
    kv_pool,
    page_table,
    cached_len,
    new_group,
):
    groups = lax.axis_size("req")
    shards = lax.axis_size("mp")
    count, steps, width = hidden_in.shape
    stores, rank, _ = a_store.shape
    _, _, page, kv_width = kv_pool.shape
    context = page_table.shape[1] * page
    heads = kv_width // HEAD
    own_cap = -(-count // min(16, groups))
    move_cap = -(-(count - count // 4) // groups)
    dims = (groups, own_cap, move_cap, stores)
    depth = width // LANES * steps
    number = groups * own_cap
    half = max(groups // 2, 1)
    first, last = page_routes(groups)
    hidden, frozen = to_tiles(hidden_in), to_tiles(frozen_query_rows)
    table, pool = in_hbm(page_table.T, kv_pool)
    fresh = (
        new_kv.reshape(count, steps, 2, heads, HEAD)
        .transpose(0, 1, 3, 2, 4)
        .reshape(count * steps * heads * 2, HEAD)
    )
    bf16, f32, i32 = jnp.bfloat16, jnp.float32, jnp.int32
    shape = jax.ShapeDtypeStruct

    message = shape((2 * own_cap * depth + TILE, LANES), bf16)
    *messages, plan = pl.pallas_call(
        functools.partial(stage_rows_kernel, dims),
        out_shape=[message] * groups + [shape((groups * (own_cap + move_cap),), i32)],
        in_specs=[IN_PLACE] * 6,
        out_specs=[IN_VMEM] * groups + [IN_SMEM],
        scratch_shapes=[
            pltpu.SMEM((2 * groups,), i32),
            pltpu.SMEM((groups,), i32),
            *[
                pltpu.SMEM(held.shape, i32)
                for held in (adapter_home, adapter_of, new_group, cached_len)
            ],
            pltpu.VMEM(hidden.shape, bf16),
            pltpu.VMEM(frozen.shape, bf16),
            pltpu.SemaphoreType.DMA((6,)),
        ],
        compiler_params=PARAMS,
        name="stage_rows",
        cost_estimate=lasts(1),
    )(*in_hbm(adapter_of, adapter_home, new_group, cached_len, hidden, frozen))
    got = {0: messages[0]}
    order = [half] + [j for j in range(1, groups) if j != half] + [0]
    for j in order[:-1]:
        got[j] = swap(messages[j], "req", j)
    got = [got[j] for j in range(groups)]

    def stage_pages(routes, *after):
        return pl.pallas_call(
            functools.partial(stage_pages_kernel, dims, routes),
            out_shape=[shape((move_cap, 2, context, kv_width), bf16)] * len(routes),
            in_specs=[IN_SMEM] * 2 + [IN_PLACE] * (1 + len(after)),
            out_specs=[IN_PLACE] * len(routes),
            scratch_shapes=[pltpu.SemaphoreType.DMA((len(routes),))],
            compiler_params=PARAMS,
            name="stage_pages",
            cost_estimate=lasts(0.1),
        )(plan, table, pool, *after)

    def send_pages(routes, staged):
        for route, x in zip(routes, staged):
            pairs = [(g, other) for g, other in enumerate(route) if other >= 0]
            pages[route] = lax.ppermute(x, "req", pairs)

    pages = {}
    first_pages = stage_pages(first) if first else [hidden]
    send_pages(first, first_pages)

    partial, told = pl.pallas_call(
        functools.partial(rank_kernel, dims, order),
        out_shape=[
            shape((2 * number, stores * rank), f32),
            shape((groups + 3 * count + groups * move_cap,), i32),
        ],
        in_specs=[IN_SMEM, IN_VMEM, IN_PLACE] + [IN_VMEM] * groups,
        out_specs=[IN_VMEM, IN_SMEM],
        scratch_shapes=[
            pltpu.VMEM((number * depth, LANES), f32),
            pltpu.VMEM((max(groups, 8), LANES), i32),
            pltpu.SMEM((max(groups, 8), LANES), i32),
            pltpu.SemaphoreType.DMA,
        ],
        compiler_params=PARAMS,
        name="rank_products",
        cost_estimate=lasts(10),
    )(cached_len, a_store.reshape(stores * rank, width), first_pages[-1], *[got[j] for j in order])
    partials = [partial] + [swap(partial, "mp", j) for j in range(1, shards)]

    last_pages = stage_pages(last, partial)
    queries = pl.pallas_call(
        functools.partial(query_kernel, dims, shards),
        out_shape=[shape((own_cap * depth, LANES), bf16)] * groups,
        in_specs=[IN_SMEM, IN_VMEM, IN_PLACE] + [IN_VMEM] * (shards + groups),
        out_specs=[IN_VMEM] * groups,
        scratch_shapes=[pltpu.VMEM((number * depth, LANES), f32)],
        compiler_params=PARAMS,
        name="queries",
        cost_estimate=lasts(0.1),
    )(told, b_store.reshape(stores * rank, width), last_pages[-1], *partials, *got)
    queries = [queries[0]] + [swap(queries[j], "req", j) for j in range(1, groups)]
    send_pages(last, last_pages)

    cache, kv = pl.pallas_call(
        functools.partial(place_kernel, dims),
        out_shape=[shape((2, count, context, kv_width), bf16)] * 2,
        in_specs=[IN_SMEM] * 2 + [IN_PLACE] * (1 + len(first[:-1])),
        out_specs=[IN_PLACE] * 2,
        scratch_shapes=[pltpu.SemaphoreType.DMA((count,))] * 2,
        compiler_params=PARAMS,
        name="place_pages",
        cost_estimate=lasts(0.1),
    )(told, table, pool, *[pages[route] for route in first[:-1]])
    attended, sorted_queries, cache = pl.pallas_call(
        functools.partial(early_kernel, dims, first),
        out_shape=[shape((count, depth, LANES), bf16)] * 2 + [shape(cache.shape, bf16)],
        in_specs=[IN_SMEM] * 2 + [IN_VMEM] * 2 + [IN_PLACE] + [IN_VMEM] * (groups + len(first)),
        out_specs=[IN_VMEM] * 2 + [IN_PLACE],
        input_output_aliases={4: 2},
        scratch_shapes=[
            pltpu.VMEM(fresh.shape, f32),
            pltpu.SemaphoreType.DMA((len(first) * move_cap,)),
        ],
        compiler_params=PARAMS,
        name="attend_early",
        cost_estimate=lasts(60),
    )(plan, told, kv, fresh, cache, *queries, *[pages[route] for route in first])
    for routes in (last,):
        attended, cache = pl.pallas_call(
            functools.partial(late_kernel, dims, routes),
            out_shape=[shape(attended.shape, bf16), shape(cache.shape, bf16)],
            in_specs=[IN_SMEM, IN_VMEM, IN_VMEM] + [IN_PLACE] * 2 + [IN_VMEM] * len(routes),
            out_specs=[IN_PLACE, IN_PLACE],
            input_output_aliases={3: 0, 4: 1},
            scratch_shapes=[
                pltpu.VMEM((len(routes) * move_cap, depth, LANES), bf16),
                pltpu.VMEM(fresh.shape, f32),
                pltpu.SemaphoreType.DMA((len(routes) * move_cap,)),
                pltpu.SemaphoreType.DMA((len(routes) * move_cap,)),
            ],
            compiler_params=PARAMS,
            name="attend_arrived",
            cost_estimate=lasts(1),
        )(told, fresh, sorted_queries, attended, cache, *[pages[route] for route in routes])
    return from_tiles(attended, steps), cache


def solution(mesh):
    placed = (
        P(("rep", "req"), None, "mp"),
        P(("rep", "req"), None, "mp"),
        P(("rep", "req"), None, None, "mp"),
        P(("rep", "req")),
        P("rep"),
        P(("rep", "req"), None, "mp"),
        P(("rep", "req"), None, "mp"),
        P(None, ("rep", "req"), None, "mp"),
        P(("rep", "req"), None),
        P(("rep", "req")),
        P(("rep", "req")),
    )
    return jax.shard_map(
        per_device,
        mesh=mesh,
        in_specs=placed,
        out_specs=(P(("rep", "req"), None, "mp"), P(None, ("rep", "req"), None, "mp")),
        check_vma=False,
    )
```

```python
import functools

import jax
import jax.numpy as jnp
from jax import lax
from jax.experimental import pallas as pl
from jax.experimental.pallas import tpu as pltpu
from jax.sharding import PartitionSpec as P

HEAD = 128
LANES = 128
TILE = 16
NEG_FILL = -1e30
VMEM_LIMIT = 40 * 1024 * 1024

IN_VMEM = pl.BlockSpec(memory_space=pltpu.VMEM)
IN_SMEM = pl.BlockSpec(memory_space=pltpu.SMEM)
IN_PLACE = pl.BlockSpec(memory_space=pl.ANY)
BYTES_A_MICROSECOND = 3_000_000
PARAMS = pltpu.CompilerParams(vmem_limit_bytes=VMEM_LIMIT)


def to_tiles(rows):
    count, steps, width = rows.shape
    split = rows.reshape(count, steps, width // LANES, LANES)
    return split.transpose(0, 2, 1, 3).reshape(count, width // LANES * steps, LANES)


def from_tiles(tiles, steps):
    count, depth, _ = tiles.shape
    split = tiles.reshape(count, depth // steps, steps, LANES)
    return split.transpose(0, 2, 1, 3).reshape(count, steps, depth // steps * LANES)


def stage_rows_kernel(dims, adapter_of, adapter_home, new_group, cached_len, hidden, frozen, *refs):
    groups, own_cap, move_cap, stores = dims
    messages, plan = refs[:groups], refs[groups]
    counts, picks, *held, held_sems = refs[groups + 1 :]
    count, depth, _ = hidden.shape
    lists = (adapter_home, adapter_of, new_group, cached_len, hidden, frozen)
    copies = [
        pltpu.make_async_copy(source, target, held_sems.at[i])
        for i, (source, target) in enumerate(zip(lists, held))
    ]
    for copy in copies:
        copy.start()
    adapter_home, adapter_of, new_group, cached_len, hidden, frozen = held
    me = lax.axis_index("req")
    for i in range(groups * (own_cap + move_cap)):
        plan[i] = -1
    for j in range(groups):
        counts[j] = 0
        counts[groups + j] = 0
        picks[j] = 0
    for copy in copies[:4]:
        copy.wait()
    for r in range(count):
        store = adapter_home[adapter_of[r]]
        j = jnp.bitwise_xor(store // stores, me)
        k = counts[j]
        plan[j * own_cap + k] = r
        counts[j] = k + 1
        picks[j] = store % stores
        to = jnp.bitwise_xor(new_group[r], me)

        @pl.when(to != 0)
        def _(to=to, r=r):
            at = counts[groups + to]
            plan[groups * own_cap + to * move_cap + at] = r
            counts[groups + to] = at + 1

    lane = lax.broadcasted_iota(jnp.int32, (TILE, LANES), 1)
    for j in range(groups):
        told = jnp.where(lane == 0, picks[j], 0)
        for k in range(move_cap):
            slot = plan[groups * own_cap + j * move_cap + k]
            length = cached_len[jnp.maximum(slot, 0)]
            told = jnp.where(lane == 1 + k, slot, told)
            told = jnp.where(lane == 1 + move_cap + k, length, told)
        messages[j][2 * own_cap * depth :, :] = told.astype(jnp.float32).astype(jnp.bfloat16)
    for part, rows in enumerate((hidden, frozen)):
        copies[4 + part].wait()
        for j in range(groups):
            for k in range(own_cap):
                source = jnp.maximum(plan[j * own_cap + k], 0)
                at = (part * own_cap + k) * depth
                messages[j][at : at + depth, :] = rows[source]


def page_routes(groups):
    half = groups // 2

    def across(j):
        return tuple(g ^ j for g in range(groups))

    between = [across(j) for j in range(1, groups - 1) if j != half]
    return between + [across(half)], [across(groups - 1)] if groups > 2 else []


def partner(route, me, arriving):
    if arriving:
        route = [route.index(g) if g in route else -1 for g in range(len(route))]
    codes = [g ^ other if other >= 0 else 0 for g, other in enumerate(route)]
    if len(set(codes)) == 1:
        return codes[0]
    chosen = 0
    for g, code in enumerate(codes):
        chosen = jnp.where(me == g, code, chosen)
    return chosen


def stage_pages_kernel(dims, routes, plan, table, pool, *refs):
    groups, own_cap, move_cap, _ = dims
    *outs, sems = refs[-len(routes) - 1 :]
    page = pool.shape[2]
    me = lax.axis_index("req")
    for i, route in enumerate(routes):
        j = partner(route, me, False)
        for k in range(move_cap):
            source = jnp.maximum(plan[groups * own_cap + j * move_cap + k], 0)
            for p in range(table.shape[0]):
                pltpu.make_async_copy(
                    pool.at[:, table[p, source]],
                    outs[i].at[k, :, pl.ds(p * page, page)],
                    sems.at[i],
                ).start()
    for i in range(len(routes)):
        pltpu.make_async_copy(outs[i], outs[i], sems.at[i]).wait()


def rank_kernel(dims, order, cached_len, a_ref, _, *refs):
    groups, own_cap, move_cap, _ = dims
    messages = [refs[order.index(j)] for j in range(groups)]
    partial, told = refs[groups : groups + 2]
    x, meta, meta_scalar, sem = refs[groups + 2 :]
    width = a_ref.shape[1]
    blocks = width // LANES
    depth = 2 * blocks
    per = own_cap * depth
    number = groups * own_cap
    for j in range(groups):
        x[j * per : (j + 1) * per, :] = messages[j][0:per, :].astype(jnp.float32)
        tile = messages[j][2 * per : 2 * per + TILE, :].astype(jnp.float32)
        meta[j : j + 1, :] = tile[0:1, :].astype(jnp.int32)
    copy = pltpu.make_async_copy(meta, meta_scalar, sem)
    copy.start()
    columns = [
        jnp.concatenate([x[pl.ds(2 * c + s, number, stride=depth), :] for s in range(2)], axis=0)
        for c in range(blocks)
    ]
    rows = jnp.concatenate(columns, axis=1).astype(jnp.bfloat16)
    partial[...] = lax.dot_general(
        rows, a_ref[...], (((1,), (1,)), ((), ())), preferred_element_type=jnp.float32
    )
    copy.wait()
    count = cached_len.shape[0]
    for r in range(count):
        told[groups + r] = 0
        told[groups + count + r] = 0
        told[groups + 2 * count + r] = cached_len[r]
    for j in range(groups):
        told[j] = meta_scalar[j, 0]
        for k in range(move_cap):
            slot = meta_scalar[j, 1 + k]
            told[groups + 3 * count + j * move_cap + k] = slot
            if j == 0:
                continue

            @pl.when(slot >= 0)
            def _(slot=slot, j=j, k=k):
                told[groups + slot] = j
                told[groups + count + slot] = k
                told[groups + 2 * count + slot] = meta_scalar[j, 1 + move_cap + k]


def pair_sum(parts):
    while len(parts) > 1:
        parts = [parts[i] + parts[i + 1] for i in range(0, len(parts), 2)]
    return parts[0]


def query_kernel(dims, n_parts, told, b_ref, _, *refs):
    groups, own_cap, _, stores = dims
    partials, messages = refs[:n_parts], refs[n_parts : n_parts + groups]
    outs, x = refs[n_parts + groups : n_parts + 2 * groups], refs[n_parts + 2 * groups]
    width = b_ref.shape[1]
    rank = b_ref.shape[0] // stores
    blocks = width // LANES
    depth = 2 * blocks
    per = own_cap * depth
    number = groups * own_cap
    full = pair_sum([p[...] for p in partials]).astype(jnp.bfloat16)
    row = lax.broadcasted_iota(jnp.int32, full.shape, 0)
    group_of = (row % number) // own_cap
    pick = jnp.zeros(full.shape, jnp.int32)
    for j in range(groups):
        pick = jnp.where(group_of == j, told[j], pick)
    chosen = lax.broadcasted_iota(jnp.int32, full.shape, 1) // rank == pick
    full = jnp.where(chosen, full.astype(jnp.float32), 0.0).astype(jnp.bfloat16)
    delta = jnp.dot(full, b_ref[...], preferred_element_type=jnp.float32)
    for c in range(blocks):
        for s in range(2):
            x[pl.ds(2 * c + s, number, stride=depth), :] = delta[
                s * number : (s + 1) * number, c * LANES : (c + 1) * LANES
            ]
    for j in range(groups):
        base = messages[j][per : 2 * per, :].astype(jnp.float32)
        outs[j][...] = (base + x[j * per : (j + 1) * per, :]).astype(jnp.bfloat16)


def fresh_rows(new_kv, x, heads):
    x[...] = new_kv[...].astype(jnp.float32)
    number = x.shape[0] // (2 * heads)
    return [
        jnp.concatenate(
            [x[pl.ds(2 * h + part, number, stride=2 * heads), :] for h in range(heads)], axis=1
        ).astype(jnp.bfloat16)
        for part in range(2)
    ]


def by_head(query, heads):
    per = query.shape[0] // heads
    blank = jnp.zeros((per, HEAD), query.dtype)
    return jnp.concatenate(
        [
            jnp.concatenate(
                [query[h * per : (h + 1) * per] if i == h else blank for i in range(heads)], axis=1
            )
            for h in range(heads)
        ],
        axis=0,
    )


def visible(depth, context, count, length, slot):
    column = lax.broadcasted_iota(jnp.int32, (depth, context + 2 * count), 1)
    step = lax.broadcasted_iota(jnp.int32, (depth, context + 2 * count), 0) % 2
    fresh_at = column - context - 2 * slot
    return (column < length) | ((fresh_at >= 0) & (fresh_at <= step))


def attend(queries, keys, values, fresh, masks):
    depth = queries[0].shape[0]
    heads = keys[0].shape[1] // HEAD
    per = depth // heads
    scale = HEAD**-0.5
    scores = []
    for query, key, mask in zip(queries, keys, masks):
        product = lax.dot_general(
            by_head(query, heads),
            jnp.concatenate([key, fresh[0]], axis=0),
            (((1,), (1,)), ((), ())),
            preferred_element_type=jnp.float32,
        )
        scores.append(jnp.where(mask, product * scale, NEG_FILL))
    scores = jnp.concatenate(scores, axis=0)
    weights = jnp.exp(scores - jnp.max(scores, axis=1, keepdims=True))
    chances = (weights / jnp.sum(weights, axis=1, keepdims=True)).astype(jnp.bfloat16)
    results = []
    for n, value in enumerate(values):
        out = jnp.dot(
            chances[n * depth : (n + 1) * depth],
            jnp.concatenate([value, fresh[1]], axis=0),
            preferred_element_type=jnp.float32,
        )
        out = jnp.concatenate(
            [out[h * per : (h + 1) * per, h * HEAD : (h + 1) * HEAD] for h in range(heads)], axis=0
        )
        results.append(out.astype(jnp.bfloat16))
    return results


def place_kernel(dims, told, table, pool, *refs):
    cache, kv, kv_sems, out_sems = refs[-4:]
    groups = dims[0]
    count = kv.shape[1]
    page = pool.shape[2]
    for r in range(count):

        @pl.when(told[groups + r] == 0)
        def _(r=r):
            for p in range(table.shape[0]):
                pltpu.make_async_copy(
                    pool.at[:, table[p, r]], kv.at[:, r, pl.ds(p * page, page)], kv_sems.at[r]
                ).start()

    for r in range(count):

        @pl.when(told[groups + r] == 0)
        def _(r=r):
            pltpu.make_async_copy(kv.at[:, r], kv.at[:, r], kv_sems.at[r]).wait()
            pltpu.make_async_copy(kv.at[:, r], cache.at[:, r], out_sems.at[r]).start()

    for r in range(count):

        @pl.when(told[groups + r] == 0)
        def _(r=r):
            pltpu.make_async_copy(kv.at[:, r], cache.at[:, r], out_sems.at[r]).wait()


def arrivals(dims, routes, told, count):
    groups, _, move_cap, _ = dims
    me = lax.axis_index("req")
    slots = []
    for route in routes:
        j = partner(route, me, True)
        slots += [told[groups + 3 * count + j * move_cap + k] for k in range(move_cap)]
    return slots, [jnp.maximum(slot, 0) for slot in slots]


def early_kernel(dims, routes, later, plan, told, kv, new_kv, cache_in, *refs):
    groups, own_cap, move_cap, _ = dims
    queries, refs = refs[:groups], refs[groups:]
    pages, refs = refs[: len(routes)], refs[len(routes) :]
    attended, cache, late_queries, late_masks, new_keys, new_values = refs[:6]
    sorted_queries, x, page_sems = refs[6:]
    count, depth, _ = attended.shape
    _, _, context, width = kv.shape
    blocks = [ref.at[k] for ref in pages for k in range(move_cap)]
    slots, places = arrivals(dims, routes, told, count)
    copies = [
        pltpu.make_async_copy(block, cache.at[:, at], page_sems.at[n])
        for n, (block, at) in enumerate(zip(blocks, places))
    ]
    for slot, copy in zip(slots, copies):
        pl.when(slot >= 0)(copy.start)
    for j in range(groups):
        for k in range(own_cap):
            slot = plan[j * own_cap + k]

            @pl.when(slot >= 0)
            def _(j=j, k=k, slot=slot):
                sorted_queries[slot] = queries[j][k * depth : (k + 1) * depth, :]

    def mask(at):
        return visible(depth, context, count, told[groups + 2 * count + at], at)

    every = list(range(count))
    fresh = fresh_rows(new_kv, x, width // HEAD)
    results = attend(
        [sorted_queries[at] for at in every + places],
        [kv[0, r] for r in every] + [block[0] for block in blocks],
        [kv[1, r] for r in every] + [block[1] for block in blocks],
        fresh,
        [mask(at) for at in every + places],
    )
    for r in every:
        attended[r] = results[r]
    for n, (slot, at) in enumerate(zip(slots, places)):

        @pl.when(slot >= 0)
        def _(n=n, at=at):
            attended[at] = results[count + n]

    new_keys[...], new_values[...] = fresh
    for n, at in enumerate(arrivals(dims, later, told, count)[1]):
        late_queries[n] = sorted_queries[at]
        late_masks[n] = jnp.where(mask(at), 1.0, 0.0)
    for slot, copy in zip(slots, copies):
        pl.when(slot >= 0)(copy.wait)


def late_kernel(
    dims, routes, told, queries, masks, new_keys, new_values, attended_in, cache_in, *refs
):
    pages, refs = refs[: len(routes)], refs[len(routes) :]
    attended, cache, slots_held, results, told_sem, page_sems, out_sems = refs
    number, count = queries.shape[0], attended.shape[0]
    blocks = [ref.at[k] for ref in pages for k in range(dims[2])]
    told_copy = pltpu.make_async_copy(told, slots_held, told_sem)
    told_copy.start()
    outs = attend(
        [queries[n] for n in range(number)],
        [block[0] for block in blocks],
        [block[1] for block in blocks],
        (new_keys[...], new_values[...]),
        [masks[n] > 0.5 for n in range(number)],
    )
    told_copy.wait()
    slots, places = arrivals(dims, routes, slots_held, count)
    copies = [
        (
            pltpu.make_async_copy(block, cache.at[:, at], page_sems.at[n]),
            pltpu.make_async_copy(results.at[n], attended.at[at], out_sems.at[n]),
        )
        for n, (block, at) in enumerate(zip(blocks, places))
    ]
    for slot, (copy, _) in zip(slots, copies):
        pl.when(slot >= 0)(copy.start)
    for n, out in enumerate(outs):
        results[n] = out
    for slot, (_, copy) in zip(slots, copies):
        pl.when(slot >= 0)(copy.start)
    for slot, pair in zip(slots, copies):

        @pl.when(slot >= 0)
        def _(pair=pair):
            for copy in pair:
                copy.wait()


def lasts(microseconds):
    return pl.CostEstimate(
        flops=int(microseconds * 1e9), transcendentals=0, bytes_accessed=int(microseconds * BYTES_A_MICROSECOND)
    )


def in_hbm(*arrays):
    return [pltpu.with_memory_space_constraint(x, pltpu.HBM) for x in arrays]


def swap(x, axis, j):
    return lax.ppermute(x, axis, [(i, i ^ j) for i in range(lax.axis_size(axis))])


def per_device(
    hidden_in,
    frozen_query_rows,
    new_kv,
    adapter_of,
    adapter_home,
    a_store,
    b_store,
    kv_pool,
    page_table,
    cached_len,
    new_group,
):
    groups = lax.axis_size("req")
    shards = lax.axis_size("mp")
    count, steps, width = hidden_in.shape
    stores, rank, _ = a_store.shape
    _, _, page, kv_width = kv_pool.shape
    context = page_table.shape[1] * page
    heads = kv_width // HEAD
    own_cap = -(-count // min(16, groups))
    move_cap = -(-(count - count // 4) // groups)
    dims = (groups, own_cap, move_cap, stores)
    depth = width // LANES * steps
    number = groups * own_cap
    half = max(groups // 2, 1)
    first, last = page_routes(groups)
    hidden, frozen = to_tiles(hidden_in), to_tiles(frozen_query_rows)
    table, pool = in_hbm(page_table.T, kv_pool)
    fresh = (
        new_kv.reshape(count, steps, 2, heads, HEAD)
        .transpose(0, 1, 3, 2, 4)
        .reshape(count * steps * heads * 2, HEAD)
    )
    bf16, f32, i32 = jnp.bfloat16, jnp.float32, jnp.int32
    shape = jax.ShapeDtypeStruct

    message = shape((2 * own_cap * depth + TILE, LANES), bf16)
    *messages, plan = pl.pallas_call(
        functools.partial(stage_rows_kernel, dims),
        out_shape=[message] * groups + [shape((groups * (own_cap + move_cap),), i32)],
        in_specs=[IN_PLACE] * 6,
        out_specs=[IN_VMEM] * groups + [IN_SMEM],
        scratch_shapes=[
            pltpu.SMEM((2 * groups,), i32),
            pltpu.SMEM((groups,), i32),
            *[
                pltpu.SMEM(held.shape, i32)
                for held in (adapter_home, adapter_of, new_group, cached_len)
            ],
            pltpu.VMEM(hidden.shape, bf16),
            pltpu.VMEM(frozen.shape, bf16),
            pltpu.SemaphoreType.DMA((6,)),
        ],
        compiler_params=PARAMS,
        name="stage_rows",
        cost_estimate=lasts(1),
    )(*in_hbm(adapter_of, adapter_home, new_group, cached_len, hidden, frozen))
    got = {0: messages[0]}
    order = [half] + [j for j in range(1, groups) if j != half] + [0]
    for j in order[:-1]:
        got[j] = swap(messages[j], "req", j)
    got = [got[j] for j in range(groups)]

    def stage_pages(routes, *after):
        return pl.pallas_call(
            functools.partial(stage_pages_kernel, dims, routes),
            out_shape=[shape((move_cap, 2, context, kv_width), bf16)] * len(routes),
            in_specs=[IN_SMEM] * 2 + [IN_PLACE] * (1 + len(after)),
            out_specs=[IN_PLACE] * len(routes),
            scratch_shapes=[pltpu.SemaphoreType.DMA((len(routes),))],
            compiler_params=PARAMS,
            name="stage_pages",
            cost_estimate=lasts(0.1),
        )(plan, table, pool, *after)

    def send_pages(routes, staged):
        for route, x in zip(routes, staged):
            pairs = [(g, other) for g, other in enumerate(route) if other >= 0]
            pages[route] = lax.ppermute(x, "req", pairs)

    pages = {}
    first_pages = stage_pages(first) if first else [hidden]
    send_pages(first, first_pages)

    partial, told = pl.pallas_call(
        functools.partial(rank_kernel, dims, order),
        out_shape=[
            shape((2 * number, stores * rank), f32),
            shape((groups + 3 * count + groups * move_cap,), i32),
        ],
        in_specs=[IN_SMEM, IN_VMEM, IN_PLACE] + [IN_VMEM] * groups,
        out_specs=[IN_VMEM, IN_SMEM],
        scratch_shapes=[
            pltpu.VMEM((number * depth, LANES), f32),
            pltpu.VMEM((max(groups, 8), LANES), i32),
            pltpu.SMEM((max(groups, 8), LANES), i32),
            pltpu.SemaphoreType.DMA,
        ],
        compiler_params=PARAMS,
        name="rank_products",
        cost_estimate=lasts(10),
    )(cached_len, a_store.reshape(stores * rank, width), first_pages[-1], *[got[j] for j in order])
    partials = [partial] + [swap(partial, "mp", j) for j in range(1, shards)]

    last_pages = stage_pages(last, partial)
    queries = pl.pallas_call(
        functools.partial(query_kernel, dims, shards),
        out_shape=[shape((own_cap * depth, LANES), bf16)] * groups,
        in_specs=[IN_SMEM, IN_VMEM, IN_PLACE] + [IN_VMEM] * (shards + groups),
        out_specs=[IN_VMEM] * groups,
        scratch_shapes=[pltpu.VMEM((number * depth, LANES), f32)],
        compiler_params=PARAMS,
        name="queries",
        cost_estimate=lasts(0.1),
    )(told, b_store.reshape(stores * rank, width), last_pages[-1], *partials, *got)
    queries = [queries[0]] + [swap(queries[j], "req", j) for j in range(1, groups)]
    send_pages(last, last_pages)

    cache, kv = pl.pallas_call(
        functools.partial(place_kernel, dims),
        out_shape=[shape((2, count, context, kv_width), bf16)] * 2,
        in_specs=[IN_SMEM] * 2 + [IN_PLACE] * (1 + len(first[:-1])),
        out_specs=[IN_PLACE] * 2,
        scratch_shapes=[pltpu.SemaphoreType.DMA((count,))] * 2,
        compiler_params=PARAMS,
        name="place_pages",
        cost_estimate=lasts(0.1),
    )(told, table, pool, *[pages[route] for route in first[:-1]])
    number_late = len(last) * move_cap
    attended, cache, *for_last = pl.pallas_call(
        functools.partial(early_kernel, dims, first, last),
        out_shape=[
            shape((count, depth, LANES), bf16),
            shape(cache.shape, bf16),
            shape((max(number_late, 1), depth, LANES), bf16),
            shape((max(number_late, 1), depth, context + 2 * count), f32),
            shape((2 * count, kv_width), bf16),
            shape((2 * count, kv_width), bf16),
        ],
        in_specs=[IN_SMEM] * 2 + [IN_VMEM] * 2 + [IN_PLACE] + [IN_VMEM] * (groups + len(first)),
        out_specs=[IN_VMEM, IN_PLACE] + [IN_VMEM] * 4,
        input_output_aliases={4: 1},
        scratch_shapes=[
            pltpu.VMEM((count, depth, LANES), bf16),
            pltpu.VMEM(fresh.shape, f32),
            pltpu.SemaphoreType.DMA((len(first) * move_cap,)),
        ],
        compiler_params=PARAMS,
        name="attend_early",
        cost_estimate=lasts(60),
    )(plan, told, kv, fresh, cache, *queries, *[pages[route] for route in first])

    if last:
        attended, cache = pl.pallas_call(
            functools.partial(late_kernel, dims, last),
            out_shape=[shape(attended.shape, bf16), shape(cache.shape, bf16)],
            in_specs=[IN_PLACE] + [IN_VMEM] * 4 + [IN_PLACE] * 2 + [IN_VMEM] * len(last),
            out_specs=[IN_PLACE, IN_PLACE],
            input_output_aliases={5: 0, 6: 1},
            scratch_shapes=[
                pltpu.SMEM(told.shape, i32),
                pltpu.VMEM((number_late, depth, LANES), bf16),
                pltpu.SemaphoreType.DMA,
                pltpu.SemaphoreType.DMA((number_late,)),
                pltpu.SemaphoreType.DMA((number_late,)),
            ],
            compiler_params=PARAMS,
            name="attend_arrived",
            cost_estimate=lasts(1),
        )(told, *for_last, attended, cache, *[pages[route] for route in last])
    return from_tiles(attended, steps), cache


def solution(mesh):
    placed = (
        P(("rep", "req"), None, "mp"),
        P(("rep", "req"), None, "mp"),
        P(("rep", "req"), None, None, "mp"),
        P(("rep", "req")),
        P("rep"),
        P(("rep", "req"), None, "mp"),
        P(("rep", "req"), None, "mp"),
        P(None, ("rep", "req"), None, "mp"),
        P(("rep", "req"), None),
        P(("rep", "req")),
        P(("rep", "req")),
    )
    return jax.shard_map(
        per_device,
        mesh=mesh,
        in_specs=placed,
        out_specs=(P(("rep", "req"), None, "mp"), P(None, ("rep", "req"), None, "mp")),
        check_vma=False,
    )
```

```python
import functools

import jax
import jax.numpy as jnp
from jax import lax
from jax.experimental import pallas as pl
from jax.experimental.pallas import tpu as pltpu
from jax.sharding import PartitionSpec as P

HEAD = 128
LANES = 128
TILE = 16
NEG_FILL = -1e30
VMEM_LIMIT = 40 * 1024 * 1024

IN_VMEM = pl.BlockSpec(memory_space=pltpu.VMEM)
IN_SMEM = pl.BlockSpec(memory_space=pltpu.SMEM)
IN_PLACE = pl.BlockSpec(memory_space=pl.ANY)
BYTES_A_MICROSECOND = 3_000_000
PARAMS = pltpu.CompilerParams(vmem_limit_bytes=VMEM_LIMIT)


def to_tiles(rows):
    count, steps, width = rows.shape
    split = rows.reshape(count, steps, width // LANES, LANES)
    return split.transpose(0, 2, 1, 3).reshape(count, width // LANES * steps, LANES)


def from_tiles(tiles, steps):
    count, depth, _ = tiles.shape
    split = tiles.reshape(count, depth // steps, steps, LANES)
    return split.transpose(0, 2, 1, 3).reshape(count, steps, depth // steps * LANES)


def stage_rows_kernel(dims, adapter_of, adapter_home, new_group, cached_len, hidden, frozen, *refs):
    groups, own_cap, move_cap, stores = dims
    messages, plan = refs[:groups], refs[groups]
    counts, picks, *held, held_sems = refs[groups + 1 :]
    count, depth, _ = hidden.shape
    lists = (adapter_home, adapter_of, new_group, cached_len, hidden, frozen)
    copies = [
        pltpu.make_async_copy(source, target, held_sems.at[i])
        for i, (source, target) in enumerate(zip(lists, held))
    ]
    for copy in copies:
        copy.start()
    adapter_home, adapter_of, new_group, cached_len, hidden, frozen = held
    me = lax.axis_index("req")
    for i in range(groups * (own_cap + move_cap)):
        plan[i] = -1
    for j in range(groups):
        counts[j] = 0
        counts[groups + j] = 0
        picks[j] = 0
    for copy in copies[:4]:
        copy.wait()
    for r in range(count):
        store = adapter_home[adapter_of[r]]
        j = jnp.bitwise_xor(store // stores, me)
        k = counts[j]
        plan[j * own_cap + k] = r
        counts[j] = k + 1
        picks[j] = store % stores
        to = jnp.bitwise_xor(new_group[r], me)

        @pl.when(to != 0)
        def _(to=to, r=r):
            at = counts[groups + to]
            plan[groups * own_cap + to * move_cap + at] = r
            counts[groups + to] = at + 1

    lane = lax.broadcasted_iota(jnp.int32, (TILE, LANES), 1)
    for j in range(groups):
        told = jnp.where(lane == 0, picks[j], 0)
        for k in range(move_cap):
            slot = plan[groups * own_cap + j * move_cap + k]
            length = cached_len[jnp.maximum(slot, 0)]
            told = jnp.where(lane == 1 + k, slot, told)
            told = jnp.where(lane == 1 + move_cap + k, length, told)
        messages[j][2 * own_cap * depth :, :] = told.astype(jnp.float32).astype(jnp.bfloat16)
    for part, rows in enumerate((hidden, frozen)):
        copies[4 + part].wait()
        for j in range(groups):
            for k in range(own_cap):
                source = jnp.maximum(plan[j * own_cap + k], 0)
                at = (part * own_cap + k) * depth
                messages[j][at : at + depth, :] = rows[source]


def page_routes(groups):
    half = groups // 2

    def across(j):
        return tuple(g ^ j for g in range(groups))

    between = [across(j) for j in range(1, groups - 1) if j != half]
    return between + [across(half)], [across(groups - 1)] if groups > 2 else []


def partner(route, me, arriving):
    if arriving:
        route = [route.index(g) if g in route else -1 for g in range(len(route))]
    codes = [g ^ other if other >= 0 else 0 for g, other in enumerate(route)]
    if len(set(codes)) == 1:
        return codes[0]
    chosen = 0
    for g, code in enumerate(codes):
        chosen = jnp.where(me == g, code, chosen)
    return chosen


def stage_pages_kernel(dims, routes, plan, table, pool, *refs):
    groups, own_cap, move_cap, _ = dims
    outs = refs[-len(routes) :]
    page = pool.shape[2]
    me = lax.axis_index("req")
    for i, route in enumerate(routes):
        j = partner(route, me, False)
        for k in range(move_cap):
            source = jnp.maximum(plan[groups * own_cap + j * move_cap + k], 0)
            for p in range(table.shape[0]):
                number = table[p, source]
                for half in range(2):
                    outs[i][k, half, p * page : (p + 1) * page, :] = pool[half, number]


def rank_kernel(dims, order, cached_len, a_ref, _, *refs):
    groups, own_cap, move_cap, _ = dims
    messages = [refs[order.index(j)] for j in range(groups)]
    partial, told = refs[groups : groups + 2]
    x, meta, meta_scalar, sem = refs[groups + 2 :]
    width = a_ref.shape[1]
    blocks = width // LANES
    depth = 2 * blocks
    per = own_cap * depth
    number = groups * own_cap
    for j in range(groups):
        x[j * per : (j + 1) * per, :] = messages[j][0:per, :].astype(jnp.float32)
        tile = messages[j][2 * per : 2 * per + TILE, :].astype(jnp.float32)
        meta[j : j + 1, :] = tile[0:1, :].astype(jnp.int32)
    copy = pltpu.make_async_copy(meta, meta_scalar, sem)
    copy.start()
    columns = [
        jnp.concatenate([x[pl.ds(2 * c + s, number, stride=depth), :] for s in range(2)], axis=0)
        for c in range(blocks)
    ]
    rows = jnp.concatenate(columns, axis=1).astype(jnp.bfloat16)
    partial[...] = lax.dot_general(
        rows, a_ref[...], (((1,), (1,)), ((), ())), preferred_element_type=jnp.float32
    )
    copy.wait()
    count = cached_len.shape[0]
    for r in range(count):
        told[groups + r] = 0
        told[groups + count + r] = 0
        told[groups + 2 * count + r] = cached_len[r]
    for j in range(groups):
        told[j] = meta_scalar[j, 0]
        for k in range(move_cap):
            slot = meta_scalar[j, 1 + k]
            told[groups + 3 * count + j * move_cap + k] = slot
            if j == 0:
                continue

            @pl.when(slot >= 0)
            def _(slot=slot, j=j, k=k):
                told[groups + slot] = j
                told[groups + count + slot] = k
                told[groups + 2 * count + slot] = meta_scalar[j, 1 + move_cap + k]


def pair_sum(parts):
    while len(parts) > 1:
        parts = [parts[i] + parts[i + 1] for i in range(0, len(parts), 2)]
    return parts[0]


def query_kernel(dims, n_parts, told, b_ref, _, *refs):
    groups, own_cap, _, stores = dims
    partials, messages = refs[:n_parts], refs[n_parts : n_parts + groups]
    outs, x = refs[n_parts + groups : n_parts + 2 * groups], refs[n_parts + 2 * groups]
    width = b_ref.shape[1]
    rank = b_ref.shape[0] // stores
    blocks = width // LANES
    depth = 2 * blocks
    per = own_cap * depth
    number = groups * own_cap
    full = pair_sum([p[...] for p in partials]).astype(jnp.bfloat16)
    row = lax.broadcasted_iota(jnp.int32, full.shape, 0)
    group_of = (row % number) // own_cap
    pick = jnp.zeros(full.shape, jnp.int32)
    for j in range(groups):
        pick = jnp.where(group_of == j, told[j], pick)
    chosen = lax.broadcasted_iota(jnp.int32, full.shape, 1) // rank == pick
    full = jnp.where(chosen, full.astype(jnp.float32), 0.0).astype(jnp.bfloat16)
    delta = jnp.dot(full, b_ref[...], preferred_element_type=jnp.float32)
    for c in range(blocks):
        for s in range(2):
            x[pl.ds(2 * c + s, number, stride=depth), :] = delta[
                s * number : (s + 1) * number, c * LANES : (c + 1) * LANES
            ]
    for j in range(groups):
        base = messages[j][per : 2 * per, :].astype(jnp.float32)
        outs[j][...] = (base + x[j * per : (j + 1) * per, :]).astype(jnp.bfloat16)


def fresh_rows(new_kv, x, heads):
    x[...] = new_kv[...].astype(jnp.float32)
    number = x.shape[0] // (2 * heads)
    return [
        jnp.concatenate(
            [x[pl.ds(2 * h + part, number, stride=2 * heads), :] for h in range(heads)], axis=1
        ).astype(jnp.bfloat16)
        for part in range(2)
    ]


def by_head(query, heads):
    per = query.shape[0] // heads
    blank = jnp.zeros((per, HEAD), query.dtype)
    return jnp.concatenate(
        [
            jnp.concatenate(
                [query[h * per : (h + 1) * per] if i == h else blank for i in range(heads)], axis=1
            )
            for h in range(heads)
        ],
        axis=0,
    )


def visible(depth, context, count, length, slot):
    column = lax.broadcasted_iota(jnp.int32, (depth, context + 2 * count), 1)
    step = lax.broadcasted_iota(jnp.int32, (depth, context + 2 * count), 0) % 2
    fresh_at = column - context - 2 * slot
    return (column < length) | ((fresh_at >= 0) & (fresh_at <= step))


def attend(queries, keys, values, fresh, masks):
    depth = queries[0].shape[0]
    heads = keys[0].shape[1] // HEAD
    per = depth // heads
    scale = HEAD**-0.5
    scores = []
    for query, key, mask in zip(queries, keys, masks):
        product = lax.dot_general(
            by_head(query, heads),
            jnp.concatenate([key, fresh[0]], axis=0),
            (((1,), (1,)), ((), ())),
            preferred_element_type=jnp.float32,
        )
        scores.append(jnp.where(mask, product * scale, NEG_FILL))
    scores = jnp.concatenate(scores, axis=0)
    weights = jnp.exp(scores - jnp.max(scores, axis=1, keepdims=True))
    chances = (weights / jnp.sum(weights, axis=1, keepdims=True)).astype(jnp.bfloat16)
    results = []
    for n, value in enumerate(values):
        out = jnp.dot(
            chances[n * depth : (n + 1) * depth],
            jnp.concatenate([value, fresh[1]], axis=0),
            preferred_element_type=jnp.float32,
        )
        out = jnp.concatenate(
            [out[h * per : (h + 1) * per, h * HEAD : (h + 1) * HEAD] for h in range(heads)], axis=0
        )
        results.append(out.astype(jnp.bfloat16))
    return results


def place_kernel(dims, told, table, pool, *refs):
    cache, kv, kv_sems, out_sems = refs[-4:]
    groups = dims[0]
    count = kv.shape[1]
    page = pool.shape[2]
    for r in range(count):

        @pl.when(told[groups + r] == 0)
        def _(r=r):
            for p in range(table.shape[0]):
                pltpu.make_async_copy(
                    pool.at[:, table[p, r]], kv.at[:, r, pl.ds(p * page, page)], kv_sems.at[r]
                ).start()

    for r in range(count):

        @pl.when(told[groups + r] == 0)
        def _(r=r):
            pltpu.make_async_copy(kv.at[:, r], kv.at[:, r], kv_sems.at[r]).wait()
            pltpu.make_async_copy(kv.at[:, r], cache.at[:, r], out_sems.at[r]).start()

    for r in range(count):

        @pl.when(told[groups + r] == 0)
        def _(r=r):
            pltpu.make_async_copy(kv.at[:, r], cache.at[:, r], out_sems.at[r]).wait()


def arrivals(dims, routes, told, count):
    groups, _, move_cap, _ = dims
    me = lax.axis_index("req")
    slots = []
    for route in routes:
        j = partner(route, me, True)
        slots += [told[groups + 3 * count + j * move_cap + k] for k in range(move_cap)]
    return slots, [jnp.maximum(slot, 0) for slot in slots]


def early_kernel(dims, routes, later, plan, told, kv, new_kv, cache_in, *refs):
    groups, own_cap, move_cap, _ = dims
    queries, refs = refs[:groups], refs[groups:]
    pages, refs = refs[: len(routes)], refs[len(routes) :]
    attended, cache, late_queries, late_masks, new_keys, new_values = refs[:6]
    sorted_queries, x, page_sems = refs[6:]
    count, depth, _ = attended.shape
    _, _, context, width = kv.shape
    blocks = [ref.at[k] for ref in pages for k in range(move_cap)]
    slots, places = arrivals(dims, routes, told, count)
    copies = [
        pltpu.make_async_copy(block, cache.at[:, at], page_sems.at[n])
        for n, (block, at) in enumerate(zip(blocks, places))
    ]
    for slot, copy in zip(slots, copies):
        pl.when(slot >= 0)(copy.start)
    for j in range(groups):
        for k in range(own_cap):
            slot = plan[j * own_cap + k]

            @pl.when(slot >= 0)
            def _(j=j, k=k, slot=slot):
                sorted_queries[slot] = queries[j][k * depth : (k + 1) * depth, :]

    def mask(at):
        return visible(depth, context, count, told[groups + 2 * count + at], at)

    every = list(range(count))
    fresh = fresh_rows(new_kv, x, width // HEAD)
    results = attend(
        [sorted_queries[at] for at in every + places],
        [kv[0, r] for r in every] + [block[0] for block in blocks],
        [kv[1, r] for r in every] + [block[1] for block in blocks],
        fresh,
        [mask(at) for at in every + places],
    )
    for r in every:
        attended[r] = results[r]
    for n, (slot, at) in enumerate(zip(slots, places)):

        @pl.when(slot >= 0)
        def _(n=n, at=at):
            attended[at] = results[count + n]

    new_keys[...], new_values[...] = fresh
    for n, at in enumerate(arrivals(dims, later, told, count)[1]):
        late_queries[n] = sorted_queries[at]
        late_masks[n] = jnp.where(mask(at), 1.0, 0.0)
    for slot, copy in zip(slots, copies):
        pl.when(slot >= 0)(copy.wait)


def late_kernel(
    dims, routes, told, queries, masks, new_keys, new_values, attended_in, cache_in, *refs
):
    pages, refs = refs[: len(routes)], refs[len(routes) :]
    attended, cache, slots_held, results, told_sem, page_sems, out_sems = refs
    number, count = queries.shape[0], attended.shape[0]
    blocks = [ref.at[k] for ref in pages for k in range(dims[2])]
    told_copy = pltpu.make_async_copy(told, slots_held, told_sem)
    told_copy.start()
    outs = attend(
        [queries[n] for n in range(number)],
        [block[0] for block in blocks],
        [block[1] for block in blocks],
        (new_keys[...], new_values[...]),
        [masks[n] > 0.5 for n in range(number)],
    )
    told_copy.wait()
    slots, places = arrivals(dims, routes, slots_held, count)
    copies = [
        (
            pltpu.make_async_copy(block, cache.at[:, at], page_sems.at[n]),
            pltpu.make_async_copy(results.at[n], attended.at[at], out_sems.at[n]),
        )
        for n, (block, at) in enumerate(zip(blocks, places))
    ]
    for slot, (copy, _) in zip(slots, copies):
        pl.when(slot >= 0)(copy.start)
    for n, out in enumerate(outs):
        results[n] = out
    for slot, (_, copy) in zip(slots, copies):
        pl.when(slot >= 0)(copy.start)
    for slot, pair in zip(slots, copies):

        @pl.when(slot >= 0)
        def _(pair=pair):
            for copy in pair:
                copy.wait()


def lasts(microseconds):
    return pl.CostEstimate(
        flops=int(microseconds * 1e9), transcendentals=0, bytes_accessed=int(microseconds * BYTES_A_MICROSECOND)
    )


def in_hbm(*arrays):
    return [pltpu.with_memory_space_constraint(x, pltpu.HBM) for x in arrays]


def swap(x, axis, j):
    return lax.ppermute(x, axis, [(i, i ^ j) for i in range(lax.axis_size(axis))])


def per_device(
    hidden_in,
    frozen_query_rows,
    new_kv,
    adapter_of,
    adapter_home,
    a_store,
    b_store,
    kv_pool,
    page_table,
    cached_len,
    new_group,
):
    groups = lax.axis_size("req")
    shards = lax.axis_size("mp")
    count, steps, width = hidden_in.shape
    stores, rank, _ = a_store.shape
    _, _, page, kv_width = kv_pool.shape
    context = page_table.shape[1] * page
    heads = kv_width // HEAD
    own_cap = -(-count // min(16, groups))
    move_cap = -(-(count - count // 4) // groups)
    dims = (groups, own_cap, move_cap, stores)
    depth = width // LANES * steps
    number = groups * own_cap
    half = max(groups // 2, 1)
    first, last = page_routes(groups)
    hidden, frozen = to_tiles(hidden_in), to_tiles(frozen_query_rows)
    table, pool = in_hbm(page_table.T, kv_pool)
    fresh = (
        new_kv.reshape(count, steps, 2, heads, HEAD)
        .transpose(0, 1, 3, 2, 4)
        .reshape(count * steps * heads * 2, HEAD)
    )
    bf16, f32, i32 = jnp.bfloat16, jnp.float32, jnp.int32
    shape = jax.ShapeDtypeStruct

    message = shape((2 * own_cap * depth + TILE, LANES), bf16)
    *messages, plan = pl.pallas_call(
        functools.partial(stage_rows_kernel, dims),
        out_shape=[message] * groups + [shape((groups * (own_cap + move_cap),), i32)],
        in_specs=[IN_PLACE] * 6,
        out_specs=[IN_VMEM] * groups + [IN_SMEM],
        scratch_shapes=[
            pltpu.SMEM((2 * groups,), i32),
            pltpu.SMEM((groups,), i32),
            *[
                pltpu.SMEM(held.shape, i32)
                for held in (adapter_home, adapter_of, new_group, cached_len)
            ],
            pltpu.VMEM(hidden.shape, bf16),
            pltpu.VMEM(frozen.shape, bf16),
            pltpu.SemaphoreType.DMA((6,)),
        ],
        compiler_params=PARAMS,
        name="stage_rows",
        cost_estimate=lasts(1),
    )(*in_hbm(adapter_of, adapter_home, new_group, cached_len, hidden, frozen))
    got = {0: messages[0]}
    order = [half] + [j for j in range(1, groups) if j != half] + [0]
    for j in order[:-1]:
        got[j] = swap(messages[j], "req", j)
    got = [got[j] for j in range(groups)]

    def stage_pages(routes, *after):
        return pl.pallas_call(
            functools.partial(stage_pages_kernel, dims, routes),
            out_shape=[shape((move_cap, 2, context, kv_width), bf16)] * len(routes),
            in_specs=[IN_SMEM] * 2 + [IN_VMEM] + [IN_PLACE] * len(after),
            out_specs=[IN_VMEM] * len(routes),
            compiler_params=PARAMS,
            name="stage_pages",
            cost_estimate=lasts(0.1),
        )(plan, page_table.T, kv_pool, *after)

    def send_pages(routes, staged):
        for route, x in zip(routes, staged):
            pairs = [(g, other) for g, other in enumerate(route) if other >= 0]
            pages[route] = lax.ppermute(x, "req", pairs)

    pages = {}
    first_pages = stage_pages(first) if first else [hidden]
    send_pages(first, first_pages)

    partial, told = pl.pallas_call(
        functools.partial(rank_kernel, dims, order),
        out_shape=[
            shape((2 * number, stores * rank), f32),
            shape((groups + 3 * count + groups * move_cap,), i32),
        ],
        in_specs=[IN_SMEM, IN_VMEM, IN_PLACE] + [IN_VMEM] * groups,
        out_specs=[IN_VMEM, IN_SMEM],
        scratch_shapes=[
            pltpu.VMEM((number * depth, LANES), f32),
            pltpu.VMEM((max(groups, 8), LANES), i32),
            pltpu.SMEM((max(groups, 8), LANES), i32),
            pltpu.SemaphoreType.DMA,
        ],
        compiler_params=PARAMS,
        name="rank_products",
        cost_estimate=lasts(10),
    )(cached_len, a_store.reshape(stores * rank, width), first_pages[-1], *[got[j] for j in order])
    partials = [partial] + [swap(partial, "mp", j) for j in range(1, shards)]

    last_pages = stage_pages(last, partial)
    queries = pl.pallas_call(
        functools.partial(query_kernel, dims, shards),
        out_shape=[shape((own_cap * depth, LANES), bf16)] * groups,
        in_specs=[IN_SMEM, IN_VMEM, IN_PLACE] + [IN_VMEM] * (shards + groups),
        out_specs=[IN_VMEM] * groups,
        scratch_shapes=[pltpu.VMEM((number * depth, LANES), f32)],
        compiler_params=PARAMS,
        name="queries",
        cost_estimate=lasts(0.1),
    )(told, b_store.reshape(stores * rank, width), last_pages[-1], *partials, *got)
    queries = [queries[0]] + [swap(queries[j], "req", j) for j in range(1, groups)]
    send_pages(last, last_pages)

    cache, kv = pl.pallas_call(
        functools.partial(place_kernel, dims),
        out_shape=[shape((2, count, context, kv_width), bf16)] * 2,
        in_specs=[IN_SMEM] * 2 + [IN_PLACE] * (1 + len(first[:-1])),
        out_specs=[IN_PLACE] * 2,
        scratch_shapes=[pltpu.SemaphoreType.DMA((count,))] * 2,
        compiler_params=PARAMS,
        name="place_pages",
        cost_estimate=lasts(0.1),
    )(told, table, pool, *[pages[route] for route in first[:-1]])
    number_late = len(last) * move_cap
    attended, cache, *for_last = pl.pallas_call(
        functools.partial(early_kernel, dims, first, last),
        out_shape=[
            shape((count, depth, LANES), bf16),
            shape(cache.shape, bf16),
            shape((max(number_late, 1), depth, LANES), bf16),
            shape((max(number_late, 1), depth, context + 2 * count), f32),
            shape((2 * count, kv_width), bf16),
            shape((2 * count, kv_width), bf16),
        ],
        in_specs=[IN_SMEM] * 2 + [IN_VMEM] * 2 + [IN_PLACE] + [IN_VMEM] * (groups + len(first)),
        out_specs=[IN_VMEM, IN_PLACE] + [IN_VMEM] * 4,
        input_output_aliases={4: 1},
        scratch_shapes=[
            pltpu.VMEM((count, depth, LANES), bf16),
            pltpu.VMEM(fresh.shape, f32),
            pltpu.SemaphoreType.DMA((len(first) * move_cap,)),
        ],
        compiler_params=PARAMS,
        name="attend_early",
        cost_estimate=lasts(60),
    )(plan, told, kv, fresh, cache, *queries, *[pages[route] for route in first])

    if last:
        attended, cache = pl.pallas_call(
            functools.partial(late_kernel, dims, last),
            out_shape=[shape(attended.shape, bf16), shape(cache.shape, bf16)],
            in_specs=[IN_PLACE] + [IN_VMEM] * 4 + [IN_PLACE] * 2 + [IN_VMEM] * len(last),
            out_specs=[IN_PLACE, IN_PLACE],
            input_output_aliases={5: 0, 6: 1},
            scratch_shapes=[
                pltpu.SMEM(told.shape, i32),
                pltpu.VMEM((number_late, depth, LANES), bf16),
                pltpu.SemaphoreType.DMA,
                pltpu.SemaphoreType.DMA((number_late,)),
                pltpu.SemaphoreType.DMA((number_late,)),
            ],
            compiler_params=PARAMS,
            name="attend_arrived",
            cost_estimate=lasts(1),
        )(told, *for_last, attended, cache, *[pages[route] for route in last])
    return from_tiles(attended, steps), cache


def solution(mesh):
    placed = (
        P(("rep", "req"), None, "mp"),
        P(("rep", "req"), None, "mp"),
        P(("rep", "req"), None, None, "mp"),
        P(("rep", "req")),
        P("rep"),
        P(("rep", "req"), None, "mp"),
        P(("rep", "req"), None, "mp"),
        P(None, ("rep", "req"), None, "mp"),
        P(("rep", "req"), None),
        P(("rep", "req")),
        P(("rep", "req")),
    )
    return jax.shard_map(
        per_device,
        mesh=mesh,
        in_specs=placed,
        out_specs=(P(("rep", "req"), None, "mp"), P(None, ("rep", "req"), None, "mp")),
        check_vma=False,
    )
```

```python
import functools

import jax
import jax.numpy as jnp
from jax import lax
from jax.experimental import pallas as pl
from jax.experimental.pallas import tpu as pltpu
from jax.sharding import PartitionSpec as P

HEAD = 128
LANES = 128
TILE = 16
NEG_FILL = -1e30
VMEM_LIMIT = 40 * 1024 * 1024

IN_VMEM = pl.BlockSpec(memory_space=pltpu.VMEM)
IN_SMEM = pl.BlockSpec(memory_space=pltpu.SMEM)
IN_PLACE = pl.BlockSpec(memory_space=pl.ANY)
BYTES_A_MICROSECOND = 3_000_000
PARAMS = pltpu.CompilerParams(vmem_limit_bytes=VMEM_LIMIT)


def to_tiles(rows):
    count, steps, width = rows.shape
    split = rows.reshape(count, steps, width // LANES, LANES)
    return split.transpose(0, 2, 1, 3).reshape(count, width // LANES * steps, LANES)


def from_tiles(tiles, steps):
    count, depth, _ = tiles.shape
    split = tiles.reshape(count, depth // steps, steps, LANES)
    return split.transpose(0, 2, 1, 3).reshape(count, steps, depth // steps * LANES)


def stage_rows_kernel(dims, adapter_of, adapter_home, new_group, cached_len, hidden, frozen, *refs):
    groups, own_cap, move_cap, stores = dims
    messages, plan = refs[:groups], refs[groups]
    counts, picks, *held, held_sems = refs[groups + 1 :]
    count, depth, _ = hidden.shape
    lists = (adapter_home, adapter_of, new_group, cached_len, hidden, frozen)
    copies = [
        pltpu.make_async_copy(source, target, held_sems.at[i])
        for i, (source, target) in enumerate(zip(lists, held))
    ]
    for copy in copies:
        copy.start()
    adapter_home, adapter_of, new_group, cached_len, hidden, frozen = held
    me = lax.axis_index("req")
    for i in range(groups * (own_cap + move_cap)):
        plan[i] = -1
    for j in range(groups):
        counts[j] = 0
        counts[groups + j] = 0
        picks[j] = 0
    for copy in copies[:4]:
        copy.wait()
    for r in range(count):
        store = adapter_home[adapter_of[r]]
        j = jnp.bitwise_xor(store // stores, me)
        k = counts[j]
        plan[j * own_cap + k] = r
        counts[j] = k + 1
        picks[j] = store % stores
        to = jnp.bitwise_xor(new_group[r], me)

        @pl.when(to != 0)
        def _(to=to, r=r):
            at = counts[groups + to]
            plan[groups * own_cap + to * move_cap + at] = r
            counts[groups + to] = at + 1

    lane = lax.broadcasted_iota(jnp.int32, (TILE, LANES), 1)
    for j in range(groups):
        told = jnp.where(lane == 0, picks[j], 0)
        for k in range(move_cap):
            slot = plan[groups * own_cap + j * move_cap + k]
            length = cached_len[jnp.maximum(slot, 0)]
            told = jnp.where(lane == 1 + k, slot, told)
            told = jnp.where(lane == 1 + move_cap + k, length, told)
        messages[j][2 * own_cap * depth :, :] = told.astype(jnp.float32).astype(jnp.bfloat16)
    for part, rows in enumerate((hidden, frozen)):
        copies[4 + part].wait()
        for j in range(groups):
            for k in range(own_cap):
                source = jnp.maximum(plan[j * own_cap + k], 0)
                at = (part * own_cap + k) * depth
                messages[j][at : at + depth, :] = rows[source]


def page_routes(groups):
    half = groups // 2

    def across(j):
        return tuple(g ^ j for g in range(groups))

    between = [across(j) for j in range(1, groups - 1) if j != half]
    return between + [across(half)], [across(groups - 1)] if groups > 2 else []


def partner(route, me, arriving):
    if arriving:
        route = [route.index(g) if g in route else -1 for g in range(len(route))]
    codes = [g ^ other if other >= 0 else 0 for g, other in enumerate(route)]
    if len(set(codes)) == 1:
        return codes[0]
    chosen = 0
    for g, code in enumerate(codes):
        chosen = jnp.where(me == g, code, chosen)
    return chosen


def stage_pages_kernel(dims, routes, plan, table, pool, *refs):
    groups, own_cap, move_cap, _ = dims
    outs = refs[-len(routes) :]
    page = pool.shape[2]
    me = lax.axis_index("req")
    for i, route in enumerate(routes):
        j = partner(route, me, False)
        for k in range(move_cap):
            source = jnp.maximum(plan[groups * own_cap + j * move_cap + k], 0)
            for p in range(table.shape[0]):
                number = table[p, source]
                for half in range(2):
                    outs[i][k, half, p * page : (p + 1) * page, :] = pool[half, number]


def rank_kernel(dims, order, cached_len, a_ref, _, *refs):
    groups, own_cap, move_cap, _ = dims
    messages = [refs[order.index(j)] for j in range(groups)]
    partial, told = refs[groups : groups + 2]
    x, meta, meta_scalar, sem = refs[groups + 2 :]
    width = a_ref.shape[1]
    blocks = width // LANES
    depth = 2 * blocks
    per = own_cap * depth
    number = groups * own_cap
    for j in range(groups):
        x[j * per : (j + 1) * per, :] = messages[j][0:per, :].astype(jnp.float32)
        tile = messages[j][2 * per : 2 * per + TILE, :].astype(jnp.float32)
        meta[j : j + 1, :] = tile[0:1, :].astype(jnp.int32)
    copy = pltpu.make_async_copy(meta, meta_scalar, sem)
    copy.start()
    columns = [
        jnp.concatenate([x[pl.ds(2 * c + s, number, stride=depth), :] for s in range(2)], axis=0)
        for c in range(blocks)
    ]
    rows = jnp.concatenate(columns, axis=1).astype(jnp.bfloat16)
    partial[...] = lax.dot_general(
        rows, a_ref[...], (((1,), (1,)), ((), ())), preferred_element_type=jnp.float32
    )
    copy.wait()
    count = cached_len.shape[0]
    for r in range(count):
        told[groups + r] = 0
        told[groups + count + r] = 0
        told[groups + 2 * count + r] = cached_len[r]
    for j in range(groups):
        told[j] = meta_scalar[j, 0]
        for k in range(move_cap):
            slot = meta_scalar[j, 1 + k]
            told[groups + 3 * count + j * move_cap + k] = slot
            if j == 0:
                continue

            @pl.when(slot >= 0)
            def _(slot=slot, j=j, k=k):
                told[groups + slot] = j
                told[groups + count + slot] = k
                told[groups + 2 * count + slot] = meta_scalar[j, 1 + move_cap + k]


def pair_sum(parts):
    while len(parts) > 1:
        parts = [parts[i] + parts[i + 1] for i in range(0, len(parts), 2)]
    return parts[0]


def query_kernel(dims, n_parts, told, b_ref, _, *refs):
    groups, own_cap, _, stores = dims
    partials, messages = refs[:n_parts], refs[n_parts : n_parts + groups]
    outs, x = refs[n_parts + groups : n_parts + 2 * groups], refs[n_parts + 2 * groups]
    width = b_ref.shape[1]
    rank = b_ref.shape[0] // stores
    blocks = width // LANES
    depth = 2 * blocks
    per = own_cap * depth
    number = groups * own_cap
    full = pair_sum([p[...] for p in partials]).astype(jnp.bfloat16)
    row = lax.broadcasted_iota(jnp.int32, full.shape, 0)
    group_of = (row % number) // own_cap
    pick = jnp.zeros(full.shape, jnp.int32)
    for j in range(groups):
        pick = jnp.where(group_of == j, told[j], pick)
    chosen = lax.broadcasted_iota(jnp.int32, full.shape, 1) // rank == pick
    full = jnp.where(chosen, full.astype(jnp.float32), 0.0).astype(jnp.bfloat16)
    delta = jnp.dot(full, b_ref[...], preferred_element_type=jnp.float32)
    for c in range(blocks):
        for s in range(2):
            x[pl.ds(2 * c + s, number, stride=depth), :] = delta[
                s * number : (s + 1) * number, c * LANES : (c + 1) * LANES
            ]
    for j in range(groups):
        base = messages[j][per : 2 * per, :].astype(jnp.float32)
        outs[j][...] = (base + x[j * per : (j + 1) * per, :]).astype(jnp.bfloat16)


def fresh_rows(new_kv, x, heads):
    x[...] = new_kv[...].astype(jnp.float32)
    number = x.shape[0] // (2 * heads)
    return [
        jnp.concatenate(
            [x[pl.ds(2 * h + part, number, stride=2 * heads), :] for h in range(heads)], axis=1
        ).astype(jnp.bfloat16)
        for part in range(2)
    ]


def by_head(query, heads):
    per = query.shape[0] // heads
    blank = jnp.zeros((per, HEAD), query.dtype)
    return jnp.concatenate(
        [
            jnp.concatenate(
                [query[h * per : (h + 1) * per] if i == h else blank for i in range(heads)], axis=1
            )
            for h in range(heads)
        ],
        axis=0,
    )


def visible(depth, context, count, length, slot):
    column = lax.broadcasted_iota(jnp.int32, (depth, context + 2 * count), 1)
    step = lax.broadcasted_iota(jnp.int32, (depth, context + 2 * count), 0) % 2
    fresh_at = column - context - 2 * slot
    return (column < length) | ((fresh_at >= 0) & (fresh_at <= step))


def attend(queries, keys, values, fresh, masks):
    depth = queries[0].shape[0]
    heads = keys[0].shape[1] // HEAD
    per = depth // heads
    scale = HEAD**-0.5
    scores = []
    for query, key, mask in zip(queries, keys, masks):
        product = lax.dot_general(
            by_head(query, heads),
            jnp.concatenate([key, fresh[0]], axis=0),
            (((1,), (1,)), ((), ())),
            preferred_element_type=jnp.float32,
        )
        scores.append(jnp.where(mask, product * scale, NEG_FILL))
    scores = jnp.concatenate(scores, axis=0)
    weights = jnp.exp(scores - jnp.max(scores, axis=1, keepdims=True))
    chances = (weights / jnp.sum(weights, axis=1, keepdims=True)).astype(jnp.bfloat16)
    results = []
    for n, value in enumerate(values):
        out = jnp.dot(
            chances[n * depth : (n + 1) * depth],
            jnp.concatenate([value, fresh[1]], axis=0),
            preferred_element_type=jnp.float32,
        )
        out = jnp.concatenate(
            [out[h * per : (h + 1) * per, h * HEAD : (h + 1) * HEAD] for h in range(heads)], axis=0
        )
        results.append(out.astype(jnp.bfloat16))
    return results


def place_kernel(dims, told, table, pool, *refs):
    cache, kv, kv_sems, out_sems = refs[-4:]
    groups = dims[0]
    count = kv.shape[1]
    page = pool.shape[2]
    for r in range(count):

        @pl.when(told[groups + r] == 0)
        def _(r=r):
            for p in range(table.shape[0]):
                pltpu.make_async_copy(
                    pool.at[:, table[p, r]], kv.at[:, r, pl.ds(p * page, page)], kv_sems.at[r]
                ).start()

    for r in range(count):

        @pl.when(told[groups + r] == 0)
        def _(r=r):
            pltpu.make_async_copy(kv.at[:, r], kv.at[:, r], kv_sems.at[r]).wait()
            pltpu.make_async_copy(kv.at[:, r], cache.at[:, r], out_sems.at[r]).start()

    for r in range(count):

        @pl.when(told[groups + r] == 0)
        def _(r=r):
            pltpu.make_async_copy(kv.at[:, r], cache.at[:, r], out_sems.at[r]).wait()


def arrivals(dims, routes, told, count):
    groups, _, move_cap, _ = dims
    me = lax.axis_index("req")
    slots = []
    for route in routes:
        j = partner(route, me, True)
        slots += [told[groups + 3 * count + j * move_cap + k] for k in range(move_cap)]
    return slots, [jnp.maximum(slot, 0) for slot in slots]


def early_kernel(dims, routes, later, plan, told, kv, new_kv, cache_in, *refs):
    groups, own_cap, move_cap, _ = dims
    queries, refs = refs[:groups], refs[groups:]
    pages, refs = refs[: len(routes)], refs[len(routes) :]
    attended, cache, late_queries, late_masks, new_keys, new_values = refs[:6]
    sorted_queries, x, page_sems = refs[6:]
    count, depth, _ = attended.shape
    _, _, context, width = kv.shape
    blocks = [ref.at[k] for ref in pages for k in range(move_cap)]
    slots, places = arrivals(dims, routes, told, count)
    copies = [
        pltpu.make_async_copy(block, cache.at[:, at], page_sems.at[n])
        for n, (block, at) in enumerate(zip(blocks, places))
    ]
    for slot, copy in zip(slots, copies):
        pl.when(slot >= 0)(copy.start)
    for j in range(groups):
        for k in range(own_cap):
            slot = plan[j * own_cap + k]

            @pl.when(slot >= 0)
            def _(j=j, k=k, slot=slot):
                sorted_queries[slot] = queries[j][k * depth : (k + 1) * depth, :]

    def mask(at):
        return visible(depth, context, count, told[groups + 2 * count + at], at)

    every = list(range(count))
    fresh = fresh_rows(new_kv, x, width // HEAD)
    results = attend(
        [sorted_queries[at] for at in every + places],
        [kv[0, r] for r in every] + [block[0] for block in blocks],
        [kv[1, r] for r in every] + [block[1] for block in blocks],
        fresh,
        [mask(at) for at in every + places],
    )
    for r in every:
        attended[r] = results[r]
    for n, (slot, at) in enumerate(zip(slots, places)):

        @pl.when(slot >= 0)
        def _(n=n, at=at):
            attended[at] = results[count + n]

    new_keys[...], new_values[...] = fresh
    for n, at in enumerate(arrivals(dims, later, told, count)[1]):
        late_queries[n] = sorted_queries[at]
        late_masks[n] = jnp.where(mask(at), 1.0, 0.0)
    for slot, copy in zip(slots, copies):
        pl.when(slot >= 0)(copy.wait)


def late_kernel(
    dims, routes, told, queries, masks, new_keys, new_values, attended_in, cache_in, *refs
):
    pages, refs = refs[: len(routes)], refs[len(routes) :]
    attended, cache, slots_held, results, told_sem, page_sems, out_sems = refs
    number, count = queries.shape[0], attended.shape[0]
    blocks = [ref.at[k] for ref in pages for k in range(dims[2])]
    told_copy = pltpu.make_async_copy(told, slots_held, told_sem)
    told_copy.start()
    outs = attend(
        [queries[n] for n in range(number)],
        [block[0] for block in blocks],
        [block[1] for block in blocks],
        (new_keys[...], new_values[...]),
        [masks[n] > 0.5 for n in range(number)],
    )
    told_copy.wait()
    slots, places = arrivals(dims, routes, slots_held, count)
    copies = [
        (
            pltpu.make_async_copy(block, cache.at[:, at], page_sems.at[n]),
            pltpu.make_async_copy(results.at[n], attended.at[at], out_sems.at[n]),
        )
        for n, (block, at) in enumerate(zip(blocks, places))
    ]
    for slot, (copy, _) in zip(slots, copies):
        pl.when(slot >= 0)(copy.start)
    for n, out in enumerate(outs):
        results[n] = out
    for slot, (_, copy) in zip(slots, copies):
        pl.when(slot >= 0)(copy.start)
    for slot, pair in zip(slots, copies):

        @pl.when(slot >= 0)
        def _(pair=pair):
            for copy in pair:
                copy.wait()


def lasts(microseconds):
    return pl.CostEstimate(
        flops=int(microseconds * 1e9), transcendentals=0, bytes_accessed=int(microseconds * BYTES_A_MICROSECOND)
    )


def in_hbm(*arrays):
    return [pltpu.with_memory_space_constraint(x, pltpu.HBM) for x in arrays]


def swap(x, axis, j):
    return lax.ppermute(x, axis, [(i, i ^ j) for i in range(lax.axis_size(axis))])


def per_device(
    hidden_in,
    frozen_query_rows,
    new_kv,
    adapter_of,
    adapter_home,
    a_store,
    b_store,
    kv_pool,
    page_table,
    cached_len,
    new_group,
):
    groups = lax.axis_size("req")
    shards = lax.axis_size("mp")
    count, steps, width = hidden_in.shape
    stores, rank, _ = a_store.shape
    _, _, page, kv_width = kv_pool.shape
    context = page_table.shape[1] * page
    heads = kv_width // HEAD
    own_cap = -(-count // min(16, groups))
    move_cap = -(-(count - count // 4) // groups)
    dims = (groups, own_cap, move_cap, stores)
    depth = width // LANES * steps
    number = groups * own_cap
    half = max(groups // 2, 1)
    first, last = page_routes(groups)
    hidden, frozen = to_tiles(hidden_in), to_tiles(frozen_query_rows)
    table, pool = in_hbm(page_table.T, kv_pool)
    fresh = (
        new_kv.reshape(count, steps, 2, heads, HEAD)
        .transpose(0, 1, 3, 2, 4)
        .reshape(count * steps * heads * 2, HEAD)
    )
    bf16, f32, i32 = jnp.bfloat16, jnp.float32, jnp.int32
    shape = jax.ShapeDtypeStruct

    message = shape((2 * own_cap * depth + TILE, LANES), bf16)
    *messages, plan = pl.pallas_call(
        functools.partial(stage_rows_kernel, dims),
        out_shape=[message] * groups + [shape((groups * (own_cap + move_cap),), i32)],
        in_specs=[IN_PLACE] * 6,
        out_specs=[IN_VMEM] * groups + [IN_SMEM],
        scratch_shapes=[
            pltpu.SMEM((2 * groups,), i32),
            pltpu.SMEM((groups,), i32),
            *[
                pltpu.SMEM(held.shape, i32)
                for held in (adapter_home, adapter_of, new_group, cached_len)
            ],
            pltpu.VMEM(hidden.shape, bf16),
            pltpu.VMEM(frozen.shape, bf16),
            pltpu.SemaphoreType.DMA((6,)),
        ],
        compiler_params=PARAMS,
        name="stage_rows",
        cost_estimate=lasts(1),
    )(*in_hbm(adapter_of, adapter_home, new_group, cached_len, hidden, frozen))
    got = {0: messages[0]}
    between = [j for j in range(1, groups - 1) if j != half]
    order = list(dict.fromkeys([groups - 1, *between, half, 0]))
    for j in order[:-1]:
        got[j] = swap(messages[j], "req", j)
    got = [got[j] for j in range(groups)]

    def stage_pages(routes, *after):
        return pl.pallas_call(
            functools.partial(stage_pages_kernel, dims, routes),
            out_shape=[shape((move_cap, 2, context, kv_width), bf16)] * len(routes),
            in_specs=[IN_SMEM] * 2 + [IN_VMEM] + [IN_PLACE] * len(after),
            out_specs=[IN_VMEM] * len(routes),
            compiler_params=PARAMS,
            name="stage_pages",
            cost_estimate=lasts(0.1),
        )(plan, page_table.T, kv_pool, *after)

    def send_pages(routes, staged):
        for route, x in zip(routes, staged):
            pairs = [(g, other) for g, other in enumerate(route) if other >= 0]
            pages[route] = lax.ppermute(x, "req", pairs)

    pages = {}
    first_pages = stage_pages(first) if first else [hidden]
    send_pages(first, first_pages)

    partial, told = pl.pallas_call(
        functools.partial(rank_kernel, dims, order),
        out_shape=[
            shape((2 * number, stores * rank), f32),
            shape((groups + 3 * count + groups * move_cap,), i32),
        ],
        in_specs=[IN_SMEM, IN_VMEM, IN_PLACE] + [IN_VMEM] * groups,
        out_specs=[IN_VMEM, IN_SMEM],
        scratch_shapes=[
            pltpu.VMEM((number * depth, LANES), f32),
            pltpu.VMEM((max(groups, 8), LANES), i32),
            pltpu.SMEM((max(groups, 8), LANES), i32),
            pltpu.SemaphoreType.DMA,
        ],
        compiler_params=PARAMS,
        name="rank_products",
        cost_estimate=lasts(10),
    )(cached_len, a_store.reshape(stores * rank, width), first_pages[-1], *[got[j] for j in order])
    partials = [partial] + [swap(partial, "mp", j) for j in range(1, shards)]

    last_pages = stage_pages(last, partial)
    queries = pl.pallas_call(
        functools.partial(query_kernel, dims, shards),
        out_shape=[shape((own_cap * depth, LANES), bf16)] * groups,
        in_specs=[IN_SMEM, IN_VMEM, IN_PLACE] + [IN_VMEM] * (shards + groups),
        out_specs=[IN_VMEM] * groups,
        scratch_shapes=[pltpu.VMEM((number * depth, LANES), f32)],
        compiler_params=PARAMS,
        name="queries",
        cost_estimate=lasts(0.1),
    )(told, b_store.reshape(stores * rank, width), last_pages[-1], *partials, *got)
    queries = [queries[0]] + [swap(queries[j], "req", j) for j in range(1, groups)]
    send_pages(last, last_pages)

    cache, kv = pl.pallas_call(
        functools.partial(place_kernel, dims),
        out_shape=[shape((2, count, context, kv_width), bf16)] * 2,
        in_specs=[IN_SMEM] * 2 + [IN_PLACE] * 2,
        out_specs=[IN_PLACE] * 2,
        scratch_shapes=[pltpu.SemaphoreType.DMA((count,))] * 2,
        compiler_params=PARAMS,
        name="place_pages",
        cost_estimate=lasts(0.1),
    )(told, table, pool, queries[1])
    number_late = len(last) * move_cap
    attended, cache, *for_last = pl.pallas_call(
        functools.partial(early_kernel, dims, first, last),
        out_shape=[
            shape((count, depth, LANES), bf16),
            shape(cache.shape, bf16),
            shape((max(number_late, 1), depth, LANES), bf16),
            shape((max(number_late, 1), depth, context + 2 * count), f32),
            shape((2 * count, kv_width), bf16),
            shape((2 * count, kv_width), bf16),
        ],
        in_specs=[IN_SMEM] * 2 + [IN_VMEM] * 2 + [IN_PLACE] + [IN_VMEM] * (groups + len(first)),
        out_specs=[IN_VMEM, IN_PLACE] + [IN_VMEM] * 4,
        input_output_aliases={4: 1},
        scratch_shapes=[
            pltpu.VMEM((count, depth, LANES), bf16),
            pltpu.VMEM(fresh.shape, f32),
            pltpu.SemaphoreType.DMA((len(first) * move_cap,)),
        ],
        compiler_params=PARAMS,
        name="attend_early",
        cost_estimate=lasts(60),
    )(plan, told, kv, fresh, cache, *queries, *[pages[route] for route in first])

    if last:
        attended, cache = pl.pallas_call(
            functools.partial(late_kernel, dims, last),
            out_shape=[shape(attended.shape, bf16), shape(cache.shape, bf16)],
            in_specs=[IN_PLACE] + [IN_VMEM] * 4 + [IN_PLACE] * 2 + [IN_VMEM] * len(last),
            out_specs=[IN_PLACE, IN_PLACE],
            input_output_aliases={5: 0, 6: 1},
            scratch_shapes=[
                pltpu.SMEM(told.shape, i32),
                pltpu.VMEM((number_late, depth, LANES), bf16),
                pltpu.SemaphoreType.DMA,
                pltpu.SemaphoreType.DMA((number_late,)),
                pltpu.SemaphoreType.DMA((number_late,)),
            ],
            compiler_params=PARAMS,
            name="attend_arrived",
            cost_estimate=lasts(1),
        )(told, *for_last, attended, cache, *[pages[route] for route in last])
    return from_tiles(attended, steps), cache


def solution(mesh):
    placed = (
        P(("rep", "req"), None, "mp"),
        P(("rep", "req"), None, "mp"),
        P(("rep", "req"), None, None, "mp"),
        P(("rep", "req")),
        P("rep"),
        P(("rep", "req"), None, "mp"),
        P(("rep", "req"), None, "mp"),
        P(None, ("rep", "req"), None, "mp"),
        P(("rep", "req"), None),
        P(("rep", "req")),
        P(("rep", "req")),
    )
    return jax.shard_map(
        per_device,
        mesh=mesh,
        in_specs=placed,
        out_specs=(P(("rep", "req"), None, "mp"), P(None, ("rep", "req"), None, "mp")),
        check_vma=False,
    )
```

```python
import functools

import jax
import jax.numpy as jnp
from jax import lax
from jax.experimental import pallas as pl
from jax.experimental.pallas import tpu as pltpu
from jax.sharding import PartitionSpec as P

HEAD = 128
LANES = 128
TILE = 16
NEG_FILL = -1e30
VMEM_LIMIT = 40 * 1024 * 1024

IN_VMEM = pl.BlockSpec(memory_space=pltpu.VMEM)
IN_SMEM = pl.BlockSpec(memory_space=pltpu.SMEM)
IN_PLACE = pl.BlockSpec(memory_space=pl.ANY)
BYTES_A_MICROSECOND = 3_000_000
PARAMS = pltpu.CompilerParams(vmem_limit_bytes=VMEM_LIMIT)


def to_tiles(rows):
    count, steps, width = rows.shape
    split = rows.reshape(count, steps, width // LANES, LANES)
    return split.transpose(0, 2, 1, 3).reshape(count, width // LANES * steps, LANES)


def from_tiles(tiles, steps):
    count, depth, _ = tiles.shape
    split = tiles.reshape(count, depth // steps, steps, LANES)
    return split.transpose(0, 2, 1, 3).reshape(count, steps, depth // steps * LANES)


def stage_rows_kernel(dims, adapter_of, adapter_home, new_group, cached_len, hidden, frozen, *refs):
    groups, own_cap, move_cap, stores = dims
    messages, plan_out = refs[:groups], refs[groups]
    plan, counts, picks, *held, held_sems = refs[groups + 1 :]
    count, depth, _ = hidden.shape
    lists = (adapter_home, adapter_of, new_group, cached_len, hidden, frozen)
    copies = [
        pltpu.make_async_copy(source, target, held_sems.at[i])
        for i, (source, target) in enumerate(zip(lists, held))
    ]
    for copy in copies:
        copy.start()
    adapter_home, adapter_of, new_group, cached_len, hidden, frozen = held
    me = lax.axis_index("req")
    for i in range(groups * (own_cap + move_cap)):
        plan[i] = -1
    for j in range(groups):
        counts[j] = 0
        counts[groups + j] = 0
        picks[j] = 0
    for copy in copies[:4]:
        copy.wait()
    for r in range(count):
        store = adapter_home[adapter_of[r]]
        j = jnp.bitwise_xor(store // stores, me)
        k = counts[j]
        plan[j * own_cap + k] = r
        counts[j] = k + 1
        picks[j] = store % stores
        to = jnp.bitwise_xor(new_group[r], me)

        @pl.when(to != 0)
        def _(to=to, r=r):
            at = counts[groups + to]
            plan[groups * own_cap + to * move_cap + at] = r
            counts[groups + to] = at + 1

    plan_copy = pltpu.make_async_copy(plan, plan_out, held_sems.at[6])
    plan_copy.start()
    lane = lax.broadcasted_iota(jnp.int32, (TILE, LANES), 1)
    for j in range(groups):
        told = jnp.where(lane == 0, picks[j], 0)
        for k in range(move_cap):
            slot = plan[groups * own_cap + j * move_cap + k]
            length = cached_len[jnp.maximum(slot, 0)]
            told = jnp.where(lane == 1 + k, slot, told)
            told = jnp.where(lane == 1 + move_cap + k, length, told)
        messages[j][2 * own_cap * depth :, :] = told.astype(jnp.float32).astype(jnp.bfloat16)
    for part, rows in enumerate((hidden, frozen)):
        copies[4 + part].wait()
        for j in range(groups):
            for k in range(own_cap):
                source = jnp.maximum(plan[j * own_cap + k], 0)
                at = (part * own_cap + k) * depth
                messages[j][at : at + depth, :] = rows[source]
    plan_copy.wait()


def page_routes(groups):
    half = groups // 2

    def across(j):
        return tuple(g ^ j for g in range(groups))

    between = [across(j) for j in range(1, groups - 1) if j != half]
    return between + [across(half)], [across(groups - 1)] if groups > 2 else []


def partner(route, me, arriving):
    if arriving:
        route = [route.index(g) if g in route else -1 for g in range(len(route))]
    codes = [g ^ other if other >= 0 else 0 for g, other in enumerate(route)]
    if len(set(codes)) == 1:
        return codes[0]
    chosen = 0
    for g, code in enumerate(codes):
        chosen = jnp.where(me == g, code, chosen)
    return chosen


def stage_pages_kernel(dims, routes, plan, table, pool, *refs):
    groups, own_cap, move_cap, _ = dims
    outs = refs[-len(routes) :]
    page = pool.shape[2]
    me = lax.axis_index("req")
    for i, route in enumerate(routes):
        j = partner(route, me, False)
        for k in range(move_cap):
            source = jnp.maximum(plan[groups * own_cap + j * move_cap + k], 0)
            for p in range(table.shape[0]):
                number = table[p, source]
                for half in range(2):
                    outs[i][k, half, p * page : (p + 1) * page, :] = pool[half, number]


def rank_kernel(dims, order, cached_len, a_ref, _, *refs):
    groups, own_cap, move_cap, _ = dims
    messages = [refs[order.index(j)] for j in range(groups)]
    partial, told = refs[groups : groups + 2]
    x, meta, meta_scalar, sem = refs[groups + 2 :]
    width = a_ref.shape[1]
    blocks = width // LANES
    depth = 2 * blocks
    per = own_cap * depth
    number = groups * own_cap
    for j in range(groups):
        x[j * per : (j + 1) * per, :] = messages[j][0:per, :].astype(jnp.float32)
        tile = messages[j][2 * per : 2 * per + TILE, :].astype(jnp.float32)
        meta[j : j + 1, :] = tile[0:1, :].astype(jnp.int32)
    copy = pltpu.make_async_copy(meta, meta_scalar, sem)
    copy.start()
    columns = [
        jnp.concatenate([x[pl.ds(2 * c + s, number, stride=depth), :] for s in range(2)], axis=0)
        for c in range(blocks)
    ]
    rows = jnp.concatenate(columns, axis=1).astype(jnp.bfloat16)
    partial[...] = lax.dot_general(
        rows, a_ref[...], (((1,), (1,)), ((), ())), preferred_element_type=jnp.float32
    )
    copy.wait()
    count = cached_len.shape[0]
    for r in range(count):
        told[groups + r] = 0
        told[groups + count + r] = 0
        told[groups + 2 * count + r] = cached_len[r]
    for j in range(groups):
        told[j] = meta_scalar[j, 0]
        for k in range(move_cap):
            slot = meta_scalar[j, 1 + k]
            told[groups + 3 * count + j * move_cap + k] = slot
            if j == 0:
                continue

            @pl.when(slot >= 0)
            def _(slot=slot, j=j, k=k):
                told[groups + slot] = j
                told[groups + count + slot] = k
                told[groups + 2 * count + slot] = meta_scalar[j, 1 + move_cap + k]


def pair_sum(parts):
    while len(parts) > 1:
        parts = [parts[i] + parts[i + 1] for i in range(0, len(parts), 2)]
    return parts[0]


def query_kernel(dims, n_parts, told, b_ref, _, *refs):
    groups, own_cap, _, stores = dims
    partials, messages = refs[:n_parts], refs[n_parts : n_parts + groups]
    outs, x = refs[n_parts + groups : n_parts + 2 * groups], refs[n_parts + 2 * groups]
    width = b_ref.shape[1]
    rank = b_ref.shape[0] // stores
    blocks = width // LANES
    depth = 2 * blocks
    per = own_cap * depth
    number = groups * own_cap
    full = pair_sum([p[...] for p in partials]).astype(jnp.bfloat16)
    row = lax.broadcasted_iota(jnp.int32, full.shape, 0)
    group_of = (row % number) // own_cap
    pick = jnp.zeros(full.shape, jnp.int32)
    for j in range(groups):
        pick = jnp.where(group_of == j, told[j], pick)
    chosen = lax.broadcasted_iota(jnp.int32, full.shape, 1) // rank == pick
    full = jnp.where(chosen, full.astype(jnp.float32), 0.0).astype(jnp.bfloat16)
    delta = jnp.dot(full, b_ref[...], preferred_element_type=jnp.float32)
    for c in range(blocks):
        for s in range(2):
            x[pl.ds(2 * c + s, number, stride=depth), :] = delta[
                s * number : (s + 1) * number, c * LANES : (c + 1) * LANES
            ]
    for j in range(groups):
        base = messages[j][per : 2 * per, :].astype(jnp.float32)
        outs[j][...] = (base + x[j * per : (j + 1) * per, :]).astype(jnp.bfloat16)


def fresh_rows(new_kv, x, heads):
    x[...] = new_kv[...].astype(jnp.float32)
    number = x.shape[0] // (2 * heads)
    return [
        jnp.concatenate(
            [x[pl.ds(2 * h + part, number, stride=2 * heads), :] for h in range(heads)], axis=1
        ).astype(jnp.bfloat16)
        for part in range(2)
    ]


def by_head(query, heads):
    per = query.shape[0] // heads
    blank = jnp.zeros((per, HEAD), query.dtype)
    return jnp.concatenate(
        [
            jnp.concatenate(
                [query[h * per : (h + 1) * per] if i == h else blank for i in range(heads)], axis=1
            )
            for h in range(heads)
        ],
        axis=0,
    )


def visible(depth, context, count, length, slot):
    column = lax.broadcasted_iota(jnp.int32, (depth, context + 2 * count), 1)
    step = lax.broadcasted_iota(jnp.int32, (depth, context + 2 * count), 0) % 2
    fresh_at = column - context - 2 * slot
    return (column < length) | ((fresh_at >= 0) & (fresh_at <= step))


def attend(queries, keys, values, fresh, masks):
    depth = queries[0].shape[0]
    heads = keys[0].shape[1] // HEAD
    per = depth // heads
    scale = HEAD**-0.5
    scores = []
    for query, key, mask in zip(queries, keys, masks):
        product = lax.dot_general(
            by_head(query, heads),
            jnp.concatenate([key, fresh[0]], axis=0),
            (((1,), (1,)), ((), ())),
            preferred_element_type=jnp.float32,
        )
        scores.append(jnp.where(mask, product * scale, NEG_FILL))
    scores = jnp.concatenate(scores, axis=0)
    weights = jnp.exp(scores - jnp.max(scores, axis=1, keepdims=True))
    chances = (weights / jnp.sum(weights, axis=1, keepdims=True)).astype(jnp.bfloat16)
    results = []
    for n, value in enumerate(values):
        out = jnp.dot(
            chances[n * depth : (n + 1) * depth],
            jnp.concatenate([value, fresh[1]], axis=0),
            preferred_element_type=jnp.float32,
        )
        out = jnp.concatenate(
            [out[h * per : (h + 1) * per, h * HEAD : (h + 1) * HEAD] for h in range(heads)], axis=0
        )
        results.append(out.astype(jnp.bfloat16))
    return results


def place_kernel(dims, told, table, pool, *refs):
    cache, kv, kv_sems, out_sems = refs[-4:]
    groups = dims[0]
    count = kv.shape[1]
    page = pool.shape[2]
    for r in range(count):

        @pl.when(told[groups + r] == 0)
        def _(r=r):
            for p in range(table.shape[0]):
                pltpu.make_async_copy(
                    pool.at[:, table[p, r]], kv.at[:, r, pl.ds(p * page, page)], kv_sems.at[r]
                ).start()

    for r in range(count):

        @pl.when(told[groups + r] == 0)
        def _(r=r):
            pltpu.make_async_copy(kv.at[:, r], kv.at[:, r], kv_sems.at[r]).wait()
            pltpu.make_async_copy(kv.at[:, r], cache.at[:, r], out_sems.at[r]).start()

    for r in range(count):

        @pl.when(told[groups + r] == 0)
        def _(r=r):
            pltpu.make_async_copy(kv.at[:, r], cache.at[:, r], out_sems.at[r]).wait()


def arrivals(dims, routes, told, count):
    groups, _, move_cap, _ = dims
    me = lax.axis_index("req")
    slots = []
    for route in routes:
        j = partner(route, me, True)
        slots += [told[groups + 3 * count + j * move_cap + k] for k in range(move_cap)]
    return slots, [jnp.maximum(slot, 0) for slot in slots]


def early_kernel(dims, routes, later, plan, told, kv, new_kv, cache_in, *refs):
    groups, own_cap, move_cap, _ = dims
    queries, refs = refs[:groups], refs[groups:]
    pages, refs = refs[: len(routes)], refs[len(routes) :]
    attended, cache, late_queries, late_masks, new_keys, new_values = refs[:6]
    sorted_queries, x, page_sems = refs[6:]
    count, depth, _ = attended.shape
    _, _, context, width = kv.shape
    blocks = [ref.at[k] for ref in pages for k in range(move_cap)]
    slots, places = arrivals(dims, routes, told, count)
    copies = [
        pltpu.make_async_copy(block, cache.at[:, at], page_sems.at[n])
        for n, (block, at) in enumerate(zip(blocks, places))
    ]
    for slot, copy in zip(slots, copies):
        pl.when(slot >= 0)(copy.start)
    for j in range(groups):
        for k in range(own_cap):
            slot = plan[j * own_cap + k]

            @pl.when(slot >= 0)
            def _(j=j, k=k, slot=slot):
                sorted_queries[slot] = queries[j][k * depth : (k + 1) * depth, :]

    def mask(at):
        return visible(depth, context, count, told[groups + 2 * count + at], at)

    every = list(range(count))
    fresh = fresh_rows(new_kv, x, width // HEAD)
    results = attend(
        [sorted_queries[at] for at in every + places],
        [kv[0, r] for r in every] + [block[0] for block in blocks],
        [kv[1, r] for r in every] + [block[1] for block in blocks],
        fresh,
        [mask(at) for at in every + places],
    )
    for r in every:
        attended[r] = results[r]
    for n, (slot, at) in enumerate(zip(slots, places)):

        @pl.when(slot >= 0)
        def _(n=n, at=at):
            attended[at] = results[count + n]

    new_keys[...], new_values[...] = fresh
    for n, at in enumerate(arrivals(dims, later, told, count)[1]):
        late_queries[n] = sorted_queries[at]
        late_masks[n] = jnp.where(mask(at), 1.0, 0.0)
    for slot, copy in zip(slots, copies):
        pl.when(slot >= 0)(copy.wait)


def late_kernel(
    dims, routes, told, queries, masks, new_keys, new_values, attended_in, cache_in, *refs
):
    pages, refs = refs[: len(routes)], refs[len(routes) :]
    attended, cache, slots_held, results, told_sem, page_sems, out_sems = refs
    number, count = queries.shape[0], attended.shape[0]
    blocks = [ref.at[k] for ref in pages for k in range(dims[2])]
    told_copy = pltpu.make_async_copy(told, slots_held, told_sem)
    told_copy.start()
    outs = attend(
        [queries[n] for n in range(number)],
        [block[0] for block in blocks],
        [block[1] for block in blocks],
        (new_keys[...], new_values[...]),
        [masks[n] > 0.5 for n in range(number)],
    )
    told_copy.wait()
    slots, places = arrivals(dims, routes, slots_held, count)
    copies = [
        (
            pltpu.make_async_copy(block, cache.at[:, at], page_sems.at[n]),
            pltpu.make_async_copy(results.at[n], attended.at[at], out_sems.at[n]),
        )
        for n, (block, at) in enumerate(zip(blocks, places))
    ]
    for slot, (copy, _) in zip(slots, copies):
        pl.when(slot >= 0)(copy.start)
    for n, out in enumerate(outs):
        results[n] = out
    for slot, (_, copy) in zip(slots, copies):
        pl.when(slot >= 0)(copy.start)
    for slot, pair in zip(slots, copies):

        @pl.when(slot >= 0)
        def _(pair=pair):
            for copy in pair:
                copy.wait()


def lasts(microseconds):
    return pl.CostEstimate(
        flops=int(microseconds * 1e9), transcendentals=0, bytes_accessed=int(microseconds * BYTES_A_MICROSECOND)
    )


def in_hbm(*arrays):
    return [pltpu.with_memory_space_constraint(x, pltpu.HBM) for x in arrays]


def swap(x, axis, j):
    return lax.ppermute(x, axis, [(i, i ^ j) for i in range(lax.axis_size(axis))])


def per_device(
    hidden_in,
    frozen_query_rows,
    new_kv,
    adapter_of,
    adapter_home,
    a_store,
    b_store,
    kv_pool,
    page_table,
    cached_len,
    new_group,
):
    groups = lax.axis_size("req")
    shards = lax.axis_size("mp")
    count, steps, width = hidden_in.shape
    stores, rank, _ = a_store.shape
    _, _, page, kv_width = kv_pool.shape
    context = page_table.shape[1] * page
    heads = kv_width // HEAD
    own_cap = -(-count // min(16, groups))
    move_cap = -(-(count - count // 4) // groups)
    dims = (groups, own_cap, move_cap, stores)
    depth = width // LANES * steps
    number = groups * own_cap
    half = max(groups // 2, 1)
    first, last = page_routes(groups)
    hidden, frozen = to_tiles(hidden_in), to_tiles(frozen_query_rows)
    table, pool = in_hbm(page_table.T, kv_pool)
    fresh = (
        new_kv.reshape(count, steps, 2, heads, HEAD)
        .transpose(0, 1, 3, 2, 4)
        .reshape(count * steps * heads * 2, HEAD)
    )
    bf16, f32, i32 = jnp.bfloat16, jnp.float32, jnp.int32
    shape = jax.ShapeDtypeStruct

    message = shape((2 * own_cap * depth + TILE, LANES), bf16)
    *messages, plan = pl.pallas_call(
        functools.partial(stage_rows_kernel, dims),
        out_shape=[message] * groups + [shape((groups * (own_cap + move_cap),), i32)],
        in_specs=[IN_PLACE] * 6,
        out_specs=[IN_VMEM] * groups + [IN_PLACE],
        scratch_shapes=[
            pltpu.SMEM((groups * (own_cap + move_cap),), i32),
            pltpu.SMEM((2 * groups,), i32),
            pltpu.SMEM((groups,), i32),
            *[
                pltpu.SMEM(held.shape, i32)
                for held in (adapter_home, adapter_of, new_group, cached_len)
            ],
            pltpu.VMEM(hidden.shape, bf16),
            pltpu.VMEM(frozen.shape, bf16),
            pltpu.SemaphoreType.DMA((7,)),
        ],
        compiler_params=PARAMS,
        name="stage_rows",
        cost_estimate=lasts(1),
    )(*in_hbm(adapter_of, adapter_home, new_group, cached_len, hidden, frozen))
    got = {0: messages[0]}
    between = [j for j in range(1, groups - 1) if j != half]
    order = list(dict.fromkeys([groups - 1, *between, half, 0]))
    for j in order[:-1]:
        got[j] = swap(messages[j], "req", j)
    got = [got[j] for j in range(groups)]

    def stage_pages(routes, *after):
        return pl.pallas_call(
            functools.partial(stage_pages_kernel, dims, routes),
            out_shape=[shape((move_cap, 2, context, kv_width), bf16)] * len(routes),
            in_specs=[IN_SMEM] * 2 + [IN_VMEM] + [IN_PLACE] * len(after),
            out_specs=[IN_VMEM] * len(routes),
            compiler_params=PARAMS,
            name="stage_pages",
            cost_estimate=lasts(0.1),
        )(plan, page_table.T, kv_pool, *after)

    def send_pages(routes, staged):
        for route, x in zip(routes, staged):
            pairs = [(g, other) for g, other in enumerate(route) if other >= 0]
            pages[route] = lax.ppermute(x, "req", pairs)

    pages = {}
    first_pages = stage_pages(first) if first else [hidden]
    send_pages(first, first_pages)

    partial, told = pl.pallas_call(
        functools.partial(rank_kernel, dims, order),
        out_shape=[
            shape((2 * number, stores * rank), f32),
            shape((groups + 3 * count + groups * move_cap,), i32),
        ],
        in_specs=[IN_SMEM, IN_VMEM, IN_PLACE] + [IN_VMEM] * groups,
        out_specs=[IN_VMEM, IN_SMEM],
        scratch_shapes=[
            pltpu.VMEM((number * depth, LANES), f32),
            pltpu.VMEM((max(groups, 8), LANES), i32),
            pltpu.SMEM((max(groups, 8), LANES), i32),
            pltpu.SemaphoreType.DMA,
        ],
        compiler_params=PARAMS,
        name="rank_products",
        cost_estimate=lasts(10),
    )(cached_len, a_store.reshape(stores * rank, width), first_pages[-1], *[got[j] for j in order])
    partials = [partial] + [swap(partial, "mp", j) for j in range(1, shards)]

    last_pages = stage_pages(last, partial)
    queries = pl.pallas_call(
        functools.partial(query_kernel, dims, shards),
        out_shape=[shape((own_cap * depth, LANES), bf16)] * groups,
        in_specs=[IN_SMEM, IN_VMEM, IN_PLACE] + [IN_VMEM] * (shards + groups),
        out_specs=[IN_VMEM] * groups,
        scratch_shapes=[pltpu.VMEM((number * depth, LANES), f32)],
        compiler_params=PARAMS,
        name="queries",
        cost_estimate=lasts(0.1),
    )(told, b_store.reshape(stores * rank, width), last_pages[-1], *partials, *got)
    queries = [queries[0]] + [swap(queries[j], "req", j) for j in range(1, groups)]
    send_pages(last, last_pages)

    cache, kv = pl.pallas_call(
        functools.partial(place_kernel, dims),
        out_shape=[shape((2, count, context, kv_width), bf16)] * 2,
        in_specs=[IN_SMEM] * 2 + [IN_PLACE] * 2,
        out_specs=[IN_PLACE] * 2,
        scratch_shapes=[pltpu.SemaphoreType.DMA((count,))] * 2,
        compiler_params=PARAMS,
        name="place_pages",
        cost_estimate=lasts(0.1),
    )(told, page_table.T, kv_pool, queries[1])
    number_late = len(last) * move_cap
    attended, cache, *for_last = pl.pallas_call(
        functools.partial(early_kernel, dims, first, last),
        out_shape=[
            shape((count, depth, LANES), bf16),
            shape(cache.shape, bf16),
            shape((max(number_late, 1), depth, LANES), bf16),
            shape((max(number_late, 1), depth, context + 2 * count), f32),
            shape((2 * count, kv_width), bf16),
            shape((2 * count, kv_width), bf16),
        ],
        in_specs=[IN_SMEM] * 2 + [IN_VMEM] * 2 + [IN_PLACE] + [IN_VMEM] * (groups + len(first)),
        out_specs=[IN_VMEM, IN_PLACE] + [IN_VMEM] * 4,
        input_output_aliases={4: 1},
        scratch_shapes=[
            pltpu.VMEM((count, depth, LANES), bf16),
            pltpu.VMEM(fresh.shape, f32),
            pltpu.SemaphoreType.DMA((len(first) * move_cap,)),
        ],
        compiler_params=PARAMS,
        name="attend_early",
        cost_estimate=lasts(60),
    )(plan, told, kv, fresh, cache, *queries, *[pages[route] for route in first])

    if last:
        attended, cache = pl.pallas_call(
            functools.partial(late_kernel, dims, last),
            out_shape=[shape(attended.shape, bf16), shape(cache.shape, bf16)],
            in_specs=[IN_PLACE] + [IN_VMEM] * 4 + [IN_PLACE] * 2 + [IN_VMEM] * len(last),
            out_specs=[IN_PLACE, IN_PLACE],
            input_output_aliases={5: 0, 6: 1},
            scratch_shapes=[
                pltpu.SMEM(told.shape, i32),
                pltpu.VMEM((number_late, depth, LANES), bf16),
                pltpu.SemaphoreType.DMA,
                pltpu.SemaphoreType.DMA((number_late,)),
                pltpu.SemaphoreType.DMA((number_late,)),
            ],
            compiler_params=PARAMS,
            name="attend_arrived",
            cost_estimate=lasts(1),
        )(told, *for_last, attended, cache, *[pages[route] for route in last])
    return from_tiles(attended, steps), cache


def solution(mesh):
    placed = (
        P(("rep", "req"), None, "mp"),
        P(("rep", "req"), None, "mp"),
        P(("rep", "req"), None, None, "mp"),
        P(("rep", "req")),
        P("rep"),
        P(("rep", "req"), None, "mp"),
        P(("rep", "req"), None, "mp"),
        P(None, ("rep", "req"), None, "mp"),
        P(("rep", "req"), None),
        P(("rep", "req")),
        P(("rep", "req")),
    )
    return jax.shard_map(
        per_device,
        mesh=mesh,
        in_specs=placed,
        out_specs=(P(("rep", "req"), None, "mp"), P(None, ("rep", "req"), None, "mp")),
        check_vma=False,
    )
```

```python
import functools

import jax
import jax.numpy as jnp
from jax import lax
from jax.experimental import pallas as pl
from jax.experimental.pallas import tpu as pltpu
from jax.sharding import PartitionSpec as P

HEAD = 128
LANES = 128
TILE = 16
NEG_FILL = -1e30
VMEM_LIMIT = 40 * 1024 * 1024

IN_VMEM = pl.BlockSpec(memory_space=pltpu.VMEM)
IN_SMEM = pl.BlockSpec(memory_space=pltpu.SMEM)
IN_PLACE = pl.BlockSpec(memory_space=pl.ANY)
BYTES_A_MICROSECOND = 3_000_000
PARAMS = pltpu.CompilerParams(vmem_limit_bytes=VMEM_LIMIT)


def to_tiles(rows):
    count, steps, width = rows.shape
    split = rows.reshape(count, steps, width // LANES, LANES)
    return split.transpose(0, 2, 1, 3).reshape(count, width // LANES * steps, LANES)


def from_tiles(tiles, steps):
    count, depth, _ = tiles.shape
    split = tiles.reshape(count, depth // steps, steps, LANES)
    return split.transpose(0, 2, 1, 3).reshape(count, steps, depth // steps * LANES)


def stage_rows_kernel(dims, adapter_of, adapter_home, new_group, cached_len, hidden, frozen, *refs):
    groups, own_cap, move_cap, stores = dims
    messages, plan = refs[:groups], refs[groups]
    counts, picks, *held, held_sems = refs[groups + 1 :]
    count, depth, _ = hidden.shape
    lists = (adapter_home, adapter_of, new_group, cached_len, hidden, frozen)
    copies = [
        pltpu.make_async_copy(source, target, held_sems.at[i])
        for i, (source, target) in enumerate(zip(lists, held))
    ]
    for copy in copies:
        copy.start()
    adapter_home, adapter_of, new_group, cached_len, hidden, frozen = held
    me = lax.axis_index("req")
    for i in range(groups * (own_cap + move_cap)):
        plan[i] = -1
    for j in range(groups):
        counts[j] = 0
        counts[groups + j] = 0
        picks[j] = 0
    for copy in copies[:4]:
        copy.wait()
    for r in range(count):
        store = adapter_home[adapter_of[r]]
        j = jnp.bitwise_xor(store // stores, me)
        k = counts[j]
        plan[j * own_cap + k] = r
        counts[j] = k + 1
        picks[j] = store % stores
        to = jnp.bitwise_xor(new_group[r], me)

        @pl.when(to != 0)
        def _(to=to, r=r):
            at = counts[groups + to]
            plan[groups * own_cap + to * move_cap + at] = r
            counts[groups + to] = at + 1

    lane = lax.broadcasted_iota(jnp.int32, (TILE, LANES), 1)
    for j in range(groups):
        told = jnp.where(lane == 0, picks[j], 0)
        for k in range(move_cap):
            slot = plan[groups * own_cap + j * move_cap + k]
            length = cached_len[jnp.maximum(slot, 0)]
            told = jnp.where(lane == 1 + k, slot, told)
            told = jnp.where(lane == 1 + move_cap + k, length, told)
        messages[j][2 * own_cap * depth :, :] = told.astype(jnp.float32).astype(jnp.bfloat16)
    for part, rows in enumerate((hidden, frozen)):
        copies[4 + part].wait()
        for j in range(groups):
            for k in range(own_cap):
                source = jnp.maximum(plan[j * own_cap + k], 0)
                at = (part * own_cap + k) * depth
                messages[j][at : at + depth, :] = rows[source]


def page_routes(groups):
    half = groups // 2

    def across(j):
        return tuple(g ^ j for g in range(groups))

    between = [across(j) for j in range(1, groups - 1) if j != half]
    return between + [across(half)], [across(groups - 1)] if groups > 2 else []


def partner(route, me, arriving):
    if arriving:
        route = [route.index(g) if g in route else -1 for g in range(len(route))]
    codes = [g ^ other if other >= 0 else 0 for g, other in enumerate(route)]
    if len(set(codes)) == 1:
        return codes[0]
    chosen = 0
    for g, code in enumerate(codes):
        chosen = jnp.where(me == g, code, chosen)
    return chosen


def stage_pages_kernel(dims, routes, plan, table, pool, *refs):
    groups, own_cap, move_cap, _ = dims
    outs = refs[-len(routes) :]
    page = pool.shape[2]
    me = lax.axis_index("req")
    for i, route in enumerate(routes):
        j = partner(route, me, False)
        for k in range(move_cap):
            source = jnp.maximum(plan[groups * own_cap + j * move_cap + k], 0)
            for p in range(table.shape[0]):
                number = table[p, source]
                for half in range(2):
                    outs[i][k, half, p * page : (p + 1) * page, :] = pool[half, number]


def rank_kernel(dims, order, cached_len, a_ref, _, *refs):
    groups, own_cap, move_cap, _ = dims
    messages = [refs[order.index(j)] for j in range(groups)]
    partial, told = refs[groups : groups + 2]
    x, meta, meta_scalar, sem = refs[groups + 2 :]
    width = a_ref.shape[1]
    blocks = width // LANES
    depth = 2 * blocks
    per = own_cap * depth
    number = groups * own_cap
    for j in range(groups):
        x[j * per : (j + 1) * per, :] = messages[j][0:per, :].astype(jnp.float32)
        tile = messages[j][2 * per : 2 * per + TILE, :].astype(jnp.float32)
        meta[j : j + 1, :] = tile[0:1, :].astype(jnp.int32)
    copy = pltpu.make_async_copy(meta, meta_scalar, sem)
    copy.start()
    columns = [
        jnp.concatenate([x[pl.ds(2 * c + s, number, stride=depth), :] for s in range(2)], axis=0)
        for c in range(blocks)
    ]
    rows = jnp.concatenate(columns, axis=1).astype(jnp.bfloat16)
    partial[...] = lax.dot_general(
        rows, a_ref[...], (((1,), (1,)), ((), ())), preferred_element_type=jnp.float32
    )
    copy.wait()
    count = cached_len.shape[0]
    for r in range(count):
        told[groups + r] = 0
        told[groups + count + r] = 0
        told[groups + 2 * count + r] = cached_len[r]
    for j in range(groups):
        told[j] = meta_scalar[j, 0]
        for k in range(move_cap):
            slot = meta_scalar[j, 1 + k]
            told[groups + 3 * count + j * move_cap + k] = slot
            if j == 0:
                continue

            @pl.when(slot >= 0)
            def _(slot=slot, j=j, k=k):
                told[groups + slot] = j
                told[groups + count + slot] = k
                told[groups + 2 * count + slot] = meta_scalar[j, 1 + move_cap + k]


def pair_sum(parts):
    while len(parts) > 1:
        parts = [parts[i] + parts[i + 1] for i in range(0, len(parts), 2)]
    return parts[0]


def query_kernel(dims, n_parts, told, b_ref, _, *refs):
    groups, own_cap, _, stores = dims
    partials, messages = refs[:n_parts], refs[n_parts : n_parts + groups]
    outs, x = refs[n_parts + groups : n_parts + 2 * groups], refs[n_parts + 2 * groups]
    width = b_ref.shape[1]
    rank = b_ref.shape[0] // stores
    blocks = width // LANES
    depth = 2 * blocks
    per = own_cap * depth
    number = groups * own_cap
    full = pair_sum([p[...] for p in partials]).astype(jnp.bfloat16)
    row = lax.broadcasted_iota(jnp.int32, full.shape, 0)
    group_of = (row % number) // own_cap
    pick = jnp.zeros(full.shape, jnp.int32)
    for j in range(groups):
        pick = jnp.where(group_of == j, told[j], pick)
    chosen = lax.broadcasted_iota(jnp.int32, full.shape, 1) // rank == pick
    full = jnp.where(chosen, full.astype(jnp.float32), 0.0).astype(jnp.bfloat16)
    delta = jnp.dot(full, b_ref[...], preferred_element_type=jnp.float32)
    for c in range(blocks):
        for s in range(2):
            x[pl.ds(2 * c + s, number, stride=depth), :] = delta[
                s * number : (s + 1) * number, c * LANES : (c + 1) * LANES
            ]
    for j in range(groups):
        base = messages[j][per : 2 * per, :].astype(jnp.float32)
        outs[j][...] = (base + x[j * per : (j + 1) * per, :]).astype(jnp.bfloat16)


def fresh_rows(new_kv, x, heads):
    x[...] = new_kv[...].astype(jnp.float32)
    number = x.shape[0] // (2 * heads)
    return [
        jnp.concatenate(
            [x[pl.ds(2 * h + part, number, stride=2 * heads), :] for h in range(heads)], axis=1
        ).astype(jnp.bfloat16)
        for part in range(2)
    ]


def by_head(query, heads):
    per = query.shape[0] // heads
    blank = jnp.zeros((per, HEAD), query.dtype)
    return jnp.concatenate(
        [
            jnp.concatenate(
                [query[h * per : (h + 1) * per] if i == h else blank for i in range(heads)], axis=1
            )
            for h in range(heads)
        ],
        axis=0,
    )


def visible(depth, context, count, length, slot):
    column = lax.broadcasted_iota(jnp.int32, (depth, context + 2 * count), 1)
    step = lax.broadcasted_iota(jnp.int32, (depth, context + 2 * count), 0) % 2
    fresh_at = column - context - 2 * slot
    return (column < length) | ((fresh_at >= 0) & (fresh_at <= step))


def chances_of(queries, keys, fresh_keys, masks):
    heads = keys[0].shape[1] // HEAD
    scale = HEAD**-0.5
    scores = []
    for query, key, mask in zip(queries, keys, masks):
        product = lax.dot_general(
            by_head(query, heads),
            jnp.concatenate([key, fresh_keys], axis=0),
            (((1,), (1,)), ((), ())),
            preferred_element_type=jnp.float32,
        )
        scores.append(jnp.where(mask, product * scale, NEG_FILL))
    scores = jnp.concatenate(scores, axis=0)
    weights = jnp.exp(scores - jnp.max(scores, axis=1, keepdims=True))
    return (weights / jnp.sum(weights, axis=1, keepdims=True)).astype(jnp.bfloat16)


def mixed(chances, values, fresh_values):
    depth = chances.shape[0] // len(values)
    heads = values[0].shape[1] // HEAD
    per = depth // heads
    results = []
    for n, value in enumerate(values):
        out = jnp.dot(
            chances[n * depth : (n + 1) * depth],
            jnp.concatenate([value, fresh_values], axis=0),
            preferred_element_type=jnp.float32,
        )
        out = jnp.concatenate(
            [out[h * per : (h + 1) * per, h * HEAD : (h + 1) * HEAD] for h in range(heads)], axis=0
        )
        results.append(out.astype(jnp.bfloat16))
    return results


def place_kernel(dims, told, table, pool, *refs):
    cache, kv, kv_sems, out_sems = refs[-4:]
    groups = dims[0]
    count = kv.shape[1]
    page = pool.shape[2]
    for r in range(count):

        @pl.when(told[groups + r] == 0)
        def _(r=r):
            for p in range(table.shape[0]):
                pltpu.make_async_copy(
                    pool.at[:, table[p, r]], kv.at[:, r, pl.ds(p * page, page)], kv_sems.at[r]
                ).start()

    for r in range(count):

        @pl.when(told[groups + r] == 0)
        def _(r=r):
            pltpu.make_async_copy(kv.at[:, r], kv.at[:, r], kv_sems.at[r]).wait()
            pltpu.make_async_copy(kv.at[:, r], cache.at[:, r], out_sems.at[r]).start()

    for r in range(count):

        @pl.when(told[groups + r] == 0)
        def _(r=r):
            pltpu.make_async_copy(kv.at[:, r], cache.at[:, r], out_sems.at[r]).wait()


def arrivals(dims, routes, told, count):
    groups, _, move_cap, _ = dims
    me = lax.axis_index("req")
    slots = []
    for route in routes:
        j = partner(route, me, True)
        slots += [told[groups + 3 * count + j * move_cap + k] for k in range(move_cap)]
    return slots, [jnp.maximum(slot, 0) for slot in slots]


def early_kernel(dims, routes, later, plan, told, kv, new_kv, cache_in, *refs):
    groups, own_cap, move_cap, _ = dims
    queries, refs = refs[:groups], refs[groups:]
    pages, refs = refs[: len(routes)], refs[len(routes) :]
    attended, cache, late_queries, late_masks, new_keys, new_values = refs[:6]
    sorted_queries, x, page_sems = refs[6:]
    count, depth, _ = attended.shape
    _, _, context, width = kv.shape
    blocks = [ref.at[k] for ref in pages for k in range(move_cap)]
    slots, places = arrivals(dims, routes, told, count)
    copies = [
        pltpu.make_async_copy(block, cache.at[:, at], page_sems.at[n])
        for n, (block, at) in enumerate(zip(blocks, places))
    ]
    for slot, copy in zip(slots, copies):
        pl.when(slot >= 0)(copy.start)
    for j in range(groups):
        for k in range(own_cap):
            slot = plan[j * own_cap + k]

            @pl.when(slot >= 0)
            def _(j=j, k=k, slot=slot):
                sorted_queries[slot] = queries[j][k * depth : (k + 1) * depth, :]

    def mask(at):
        return visible(depth, context, count, told[groups + 2 * count + at], at)

    every = list(range(count))
    fresh = fresh_rows(new_kv, x, width // HEAD)
    chances = chances_of(
        [sorted_queries[at] for at in every + places],
        [kv[0, r] for r in every] + [block[0] for block in blocks],
        fresh[0],
        [mask(at) for at in every + places],
    )
    results = mixed(
        chances, [kv[1, r] for r in every] + [block[1] for block in blocks], fresh[1]
    )
    for r in every:
        attended[r] = results[r]
    for n, (slot, at) in enumerate(zip(slots, places)):

        @pl.when(slot >= 0)
        def _(n=n, at=at):
            attended[at] = results[count + n]

    new_keys[...], new_values[...] = fresh
    for n, at in enumerate(arrivals(dims, later, told, count)[1]):
        late_queries[n] = sorted_queries[at]
        late_masks[n] = jnp.where(mask(at), 1.0, 0.0)
    for slot, copy in zip(slots, copies):
        pl.when(slot >= 0)(copy.wait)


def late_kernel(
    dims, routes, told, queries, masks, new_keys, new_values, attended_in, cache_in, *refs
):
    pages, refs = refs[: len(routes)], refs[len(routes) :]
    attended, cache, slots_held, results, told_sem, page_sems, out_sems = refs
    number, count = queries.shape[0], attended.shape[0]
    blocks = [ref.at[k] for ref in pages for k in range(dims[2])]
    told_copy = pltpu.make_async_copy(told, slots_held, told_sem)
    told_copy.start()
    chances = chances_of(
        [queries[n] for n in range(number)],
        [block[0] for block in blocks],
        new_keys[...],
        [masks[n] > 0.5 for n in range(number)],
    )
    told_copy.wait()
    slots, places = arrivals(dims, routes, slots_held, count)
    copies = [
        (
            pltpu.make_async_copy(block, cache.at[:, at], page_sems.at[n]),
            pltpu.make_async_copy(results.at[n], attended.at[at], out_sems.at[n]),
        )
        for n, (block, at) in enumerate(zip(blocks, places))
    ]
    for slot, (copy, _) in zip(slots, copies):
        pl.when(slot >= 0)(copy.start)
    for n, out in enumerate(mixed(chances, [block[1] for block in blocks], new_values[...])):
        results[n] = out
    for slot, (_, copy) in zip(slots, copies):
        pl.when(slot >= 0)(copy.start)
    for slot, pair in zip(slots, copies):

        @pl.when(slot >= 0)
        def _(pair=pair):
            for copy in pair:
                copy.wait()


def lasts(microseconds):
    return pl.CostEstimate(
        flops=int(microseconds * 1e9), transcendentals=0, bytes_accessed=int(microseconds * BYTES_A_MICROSECOND)
    )


def in_hbm(*arrays):
    return [pltpu.with_memory_space_constraint(x, pltpu.HBM) for x in arrays]


def swap(x, axis, j):
    return lax.ppermute(x, axis, [(i, i ^ j) for i in range(lax.axis_size(axis))])


def per_device(
    hidden_in,
    frozen_query_rows,
    new_kv,
    adapter_of,
    adapter_home,
    a_store,
    b_store,
    kv_pool,
    page_table,
    cached_len,
    new_group,
):
    groups = lax.axis_size("req")
    shards = lax.axis_size("mp")
    count, steps, width = hidden_in.shape
    stores, rank, _ = a_store.shape
    _, _, page, kv_width = kv_pool.shape
    context = page_table.shape[1] * page
    heads = kv_width // HEAD
    own_cap = -(-count // min(16, groups))
    move_cap = -(-(count - count // 4) // groups)
    dims = (groups, own_cap, move_cap, stores)
    depth = width // LANES * steps
    number = groups * own_cap
    half = max(groups // 2, 1)
    first, last = page_routes(groups)
    hidden, frozen = to_tiles(hidden_in), to_tiles(frozen_query_rows)
    table, pool = in_hbm(page_table.T, kv_pool)
    fresh = (
        new_kv.reshape(count, steps, 2, heads, HEAD)
        .transpose(0, 1, 3, 2, 4)
        .reshape(count * steps * heads * 2, HEAD)
    )
    bf16, f32, i32 = jnp.bfloat16, jnp.float32, jnp.int32
    shape = jax.ShapeDtypeStruct

    message = shape((2 * own_cap * depth + TILE, LANES), bf16)
    *messages, plan = pl.pallas_call(
        functools.partial(stage_rows_kernel, dims),
        out_shape=[message] * groups + [shape((groups * (own_cap + move_cap),), i32)],
        in_specs=[IN_PLACE] * 6,
        out_specs=[IN_VMEM] * groups + [IN_SMEM],
        scratch_shapes=[
            pltpu.SMEM((2 * groups,), i32),
            pltpu.SMEM((groups,), i32),
            *[
                pltpu.SMEM(held.shape, i32)
                for held in (adapter_home, adapter_of, new_group, cached_len)
            ],
            pltpu.VMEM(hidden.shape, bf16),
            pltpu.VMEM(frozen.shape, bf16),
            pltpu.SemaphoreType.DMA((6,)),
        ],
        compiler_params=PARAMS,
        name="stage_rows",
        cost_estimate=lasts(1),
    )(*in_hbm(adapter_of, adapter_home, new_group, cached_len, hidden, frozen))
    got = {0: messages[0]}
    between = [j for j in range(1, groups - 1) if j != half]
    order = list(dict.fromkeys([groups - 1, *between, half, 0]))
    for j in order[:-1]:
        got[j] = swap(messages[j], "req", j)
    got = [got[j] for j in range(groups)]

    def stage_pages(routes, *after):
        return pl.pallas_call(
            functools.partial(stage_pages_kernel, dims, routes),
            out_shape=[shape((move_cap, 2, context, kv_width), bf16)] * len(routes),
            in_specs=[IN_SMEM] * 2 + [IN_VMEM] + [IN_PLACE] * len(after),
            out_specs=[IN_VMEM] * len(routes),
            compiler_params=PARAMS,
            name="stage_pages",
            cost_estimate=lasts(0.1),
        )(plan, page_table.T, kv_pool, *after)

    def send_pages(routes, staged):
        for route, x in zip(routes, staged):
            pairs = [(g, other) for g, other in enumerate(route) if other >= 0]
            pages[route] = lax.ppermute(x, "req", pairs)

    pages = {}
    first_pages = stage_pages(first) if first else [hidden]
    send_pages(first, first_pages)

    partial, told = pl.pallas_call(
        functools.partial(rank_kernel, dims, order),
        out_shape=[
            shape((2 * number, stores * rank), f32),
            shape((groups + 3 * count + groups * move_cap,), i32),
        ],
        in_specs=[IN_SMEM, IN_VMEM, IN_PLACE] + [IN_VMEM] * groups,
        out_specs=[IN_VMEM, IN_SMEM],
        scratch_shapes=[
            pltpu.VMEM((number * depth, LANES), f32),
            pltpu.VMEM((max(groups, 8), LANES), i32),
            pltpu.SMEM((max(groups, 8), LANES), i32),
            pltpu.SemaphoreType.DMA,
        ],
        compiler_params=PARAMS,
        name="rank_products",
        cost_estimate=lasts(10),
    )(cached_len, a_store.reshape(stores * rank, width), first_pages[-1], *[got[j] for j in order])
    partials = [partial] + [swap(partial, "mp", j) for j in range(1, shards)]

    last_pages = stage_pages(last, partial)
    queries = pl.pallas_call(
        functools.partial(query_kernel, dims, shards),
        out_shape=[shape((own_cap * depth, LANES), bf16)] * groups,
        in_specs=[IN_SMEM, IN_VMEM, IN_PLACE] + [IN_VMEM] * (shards + groups),
        out_specs=[IN_VMEM] * groups,
        scratch_shapes=[pltpu.VMEM((number * depth, LANES), f32)],
        compiler_params=PARAMS,
        name="queries",
        cost_estimate=lasts(0.1),
    )(told, b_store.reshape(stores * rank, width), last_pages[-1], *partials, *got)
    queries = [queries[0]] + [swap(queries[j], "req", j) for j in range(1, groups)]
    send_pages(last, last_pages)

    cache, kv = pl.pallas_call(
        functools.partial(place_kernel, dims),
        out_shape=[shape((2, count, context, kv_width), bf16)] * 2,
        in_specs=[IN_SMEM] * 2 + [IN_PLACE] * 2,
        out_specs=[IN_PLACE] * 2,
        scratch_shapes=[pltpu.SemaphoreType.DMA((count,))] * 2,
        compiler_params=PARAMS,
        name="place_pages",
        cost_estimate=lasts(0.1),
    )(told, table, pool, queries[1])
    number_late = len(last) * move_cap
    attended, cache, *for_last = pl.pallas_call(
        functools.partial(early_kernel, dims, first, last),
        out_shape=[
            shape((count, depth, LANES), bf16),
            shape(cache.shape, bf16),
            shape((max(number_late, 1), depth, LANES), bf16),
            shape((max(number_late, 1), depth, context + 2 * count), f32),
            shape((2 * count, kv_width), bf16),
            shape((2 * count, kv_width), bf16),
        ],
        in_specs=[IN_SMEM] * 2 + [IN_VMEM] * 2 + [IN_PLACE] + [IN_VMEM] * (groups + len(first)),
        out_specs=[IN_VMEM, IN_PLACE] + [IN_VMEM] * 4,
        input_output_aliases={4: 1},
        scratch_shapes=[
            pltpu.VMEM((count, depth, LANES), bf16),
            pltpu.VMEM(fresh.shape, f32),
            pltpu.SemaphoreType.DMA((len(first) * move_cap,)),
        ],
        compiler_params=PARAMS,
        name="attend_early",
        cost_estimate=lasts(60),
    )(plan, told, kv, fresh, cache, *queries, *[pages[route] for route in first])

    if last:
        attended, cache = pl.pallas_call(
            functools.partial(late_kernel, dims, last),
            out_shape=[shape(attended.shape, bf16), shape(cache.shape, bf16)],
            in_specs=[IN_PLACE] + [IN_VMEM] * 4 + [IN_PLACE] * 2 + [IN_VMEM] * len(last),
            out_specs=[IN_PLACE, IN_PLACE],
            input_output_aliases={5: 0, 6: 1},
            scratch_shapes=[
                pltpu.SMEM(told.shape, i32),
                pltpu.VMEM((number_late, depth, LANES), bf16),
                pltpu.SemaphoreType.DMA,
                pltpu.SemaphoreType.DMA((number_late,)),
                pltpu.SemaphoreType.DMA((number_late,)),
            ],
            compiler_params=PARAMS,
            name="attend_arrived",
            cost_estimate=lasts(1),
        )(told, *for_last, attended, cache, *[pages[route] for route in last])
    return from_tiles(attended, steps), cache


def solution(mesh):
    placed = (
        P(("rep", "req"), None, "mp"),
        P(("rep", "req"), None, "mp"),
        P(("rep", "req"), None, None, "mp"),
        P(("rep", "req")),
        P("rep"),
        P(("rep", "req"), None, "mp"),
        P(("rep", "req"), None, "mp"),
        P(None, ("rep", "req"), None, "mp"),
        P(("rep", "req"), None),
        P(("rep", "req")),
        P(("rep", "req")),
    )
    return jax.shard_map(
        per_device,
        mesh=mesh,
        in_specs=placed,
        out_specs=(P(("rep", "req"), None, "mp"), P(None, ("rep", "req"), None, "mp")),
        check_vma=False,
    )
```
